32 devices in a mesh: tp: 4 (over y, x), dp: 4 (over z), dq: 2 (over core).
Axes of the slice: x: 2, y: 2, z: 4, core: 2. Of those that a mesh axis runs over, the one named last changes fastest.
Arguments:
- inputs: bfloat16 [16384, 768], P(('dp', 'dq')), may hold values from -6 to 6
- token_ids: int32 [64, 256], P(('dp', 'dq')), may hold values from 0 to 30521, as said below
- crop_counts: int32 [8], P(('dp', 'dq')), may hold values from 1 to 8, as said below
- domain_ids: int32 [64], P(('dp', 'dq')), may hold values from 0 to 1
- positives: bfloat16 [64, 768], P(('dp', 'dq')), may hold values from -0.59765625 to 0.59765625
- distractor_buffer: bfloat16 [16384, 768], P(('dp', 'dq')), may hold values from -0.59765625 to 0.59765625
- w_query: bfloat16 [768, 768], P(None, 'tp'), may hold values from -0.21875 to 0.21875
- b_query: float32 [768], P('tp'), may hold values from -1.75 to 1.75
- w_key: bfloat16 [768, 768], P(None, 'tp'), may hold values from -0.21875 to 0.21875
- w_value: bfloat16 [768, 768], P(None, 'tp'), may hold values from -0.21875 to 0.21875
- b_value: float32 [768], P('tp'), may hold values from -1.75 to 1.75
- w_out: bfloat16 [768, 768], P('tp'), may hold values from -2.5 to 2.5
- b_out: float32 [768], replicated, may hold values from -1.75 to 1.75
- gain_one: float32 [768], replicated, may hold values from 0.5 to 1.5
- shift_one: float32 [768], replicated, may hold values from -1.75 to 1.75
- w_up: bfloat16 [768, 3072], P(None, 'tp'), may hold values from -0.21875 to 0.21875
- b_up: float32 [3072], P('tp'), may hold values from -1.75 to 1.75
- w_down: bfloat16 [3072, 768], P('tp'), may hold values from -0.109375 to 0.109375
- b_down: float32 [768], replicated, may hold values from -1.75 to 1.75
- gain_two: float32 [768], replicated, may hold values from 0.5 to 1.5
- shift_two: float32 [768], replicated, may hold values from -1.75 to 1.75
Outputs:
- grad_inputs: float32 [16384, 768], P(('dp', 'dq'))
- grad_w_query: float32 [768, 768], P(None, 'tp')
- grad_b_query: float32 [768], P('tp')
- grad_w_key: float32 [768, 768], P(None, 'tp')
- grad_w_value: float32 [768, 768], P(None, 'tp')
- grad_b_value: float32 [768], P('tp')
- grad_w_out: float32 [768, 768], P('tp')
- grad_b_out: float32 [768], replicated
- grad_gain_one: float32 [768], replicated
- grad_shift_one: float32 [768], replicated
- grad_w_up: float32 [768, 3072], P(None, 'tp')
- grad_b_up: float32 [3072], P('tp')
- grad_w_down: float32 [3072, 768], P('tp')
- grad_b_down: float32 [768], replicated
- grad_gain_two: float32 [768], replicated
- grad_shift_two: float32 [768], replicated
The draws below stay inside these ranges and needn't reach their ends.
Inputs may be any that keep to these rules, and one draw needn't show every extreme that they name: `token_ids`: each crop holds 64 to 256 nonzero ids as a prefix, then zeros; position 0 holds 101. `crop_counts`: every batch device has at least one live crop; its live crops are its first ones.
All inputs are finite; a program needn't handle non-finite values.
Results may differ from the reference program's by a relative error of at most 0.014.
Values may be sent and summed in bfloat16 or wider, within the bound.
A program may use at most 128 MiB of HBM per device.

```python
import jax
import jax.numpy as jnp
from jax import lax

D = 768
HEADS = 12
HD = 64
FF = 3072
SEQ = 256
CROPS_DEV = 8
BATCH_DEVS = 8
TOK_DEV = 2048
CROPS = 64
TOKENS = 16384
QUEUE = 16384


def draw_token_ids(key, part):
    key = jax.random.fold_in(key, 11)
    key_len, key_ids = jax.random.split(key)
    lengths = jax.random.randint(key_len, (CROPS,), SEQ // 4, SEQ + 1)
    lengths = lengths.at[0].set(SEQ).at[1].set(SEQ // 4)
    token_values = jax.random.randint(key_ids, (CROPS, SEQ), 1000, 30522)
    place = jnp.arange(SEQ)[None, :]
    token_values = jnp.where(place < lengths[:, None], token_values, 0)
    token_values = token_values.at[:, 0].set(101)
    return token_values.at[0, 1].set(30521).astype(jnp.int32)


def draw_crop_counts(key, part):
    key = jax.random.fold_in(key, 23)
    key_counts, key_spot = jax.random.split(key)
    counts = jax.random.randint(key_counts, (BATCH_DEVS,), 1, CROPS_DEV + 1)
    spot = jax.random.randint(key_spot, (), 0, BATCH_DEVS)
    counts = counts.at[spot].set(CROPS_DEV)
    counts = counts.at[(spot + BATCH_DEVS // 2) % BATCH_DEVS].set(1)
    return counts.astype(jnp.int32)


def with_ends(entries, rng, smallest, high):
    shape = entries.shape
    spot = [jax.random.randint(jax.random.fold_in(rng, axis), (), 0, shape[axis]) for axis in range(len(shape))]
    entries = entries.at[tuple(spot)].set(smallest)
    longest = shape.index(max(shape))
    spot[longest] = (spot[longest] + 1) % shape[longest]
    return entries.at[tuple(spot)].set(high)


def steps_of(key, shape, cuts, low, high):
    factor_of, own = 1.0, jax.random.fold_in(key, 6)
    for axis_at, shards_of in cuts:
        draws = jnp.exp(jax.random.uniform(jax.random.fold_in(own, axis_at), (shards_of,), jnp.float32, low / len(cuts), high / len(cuts)))
        factor_of = factor_of * jnp.repeat(draws, shape[axis_at] // shards_of).reshape([-1 if axis == axis_at else 1 for axis in range(len(shape))])
    return factor_of


def bell_draw(rng, dims, scale, limit, cuts=(), kind=jnp.bfloat16):
    result = scale * jax.random.normal(rng, dims, jnp.float32)
    if cuts:
        result = result * steps_of(rng, dims, cuts, -0.22, 0.18)
    return jnp.clip(result, -limit, limit).astype(kind)


def setup_inputs(seed: int = 0) -> dict:
    key_list = jax.random.split(jax.random.key(seed), 22)
    return {
        "inputs": bell_draw(key_list[0], (TOKENS, D), 1.0, 6.0, ((0, 8),)),
        "token_ids": draw_token_ids(jax.random.fold_in(key_list[21], 71), 0),
        "crop_counts": draw_crop_counts(jax.random.fold_in(key_list[21], 71), 0),
        "domain_ids": with_ends(jax.random.randint(key_list[3], (CROPS,), 0, 2), jax.random.fold_in(key_list[3], 1), 0, 1).astype(jnp.int32),
        "positives": bell_draw(key_list[4], (CROPS, D), 0.075, 0.59765625, ((0, 8),)),
        "distractor_buffer": bell_draw(key_list[5], (QUEUE, D), 0.075, 0.59765625, ((0, 8),)),
        "w_query": bell_draw(key_list[6], (D, D), D ** -0.5, 0.21875, ((1, 4),)),
        "b_query": bell_draw(key_list[7], (D,), 0.3, 1.75, ((0, 4),), jnp.float32),
        "w_key": bell_draw(key_list[8], (D, D), D ** -0.5, 0.21875, ((1, 4),)),
        "w_value": bell_draw(key_list[9], (D, D), D ** -0.5, 0.21875, ((1, 4),)),
        "b_value": bell_draw(key_list[10], (D,), 0.3, 1.75, ((0, 4),), jnp.float32),
        "w_out": bell_draw(key_list[11], (D, D), 6 ** -0.5, 2.5, ((0, 4),)),
        "b_out": bell_draw(key_list[12], (D,), 0.3, 1.75, (), jnp.float32),
        "gain_one": jnp.clip(1.0 + 0.1 * jax.random.normal(key_list[13], (D,), jnp.float32), 0.5, 1.5),
        "shift_one": bell_draw(key_list[14], (D,), 0.3, 1.75, (), jnp.float32),
        "w_up": bell_draw(key_list[15], (D, FF), D ** -0.5, 0.21875, ((1, 4),)),
        "b_up": bell_draw(key_list[16], (FF,), 0.3, 1.75, ((0, 4),), jnp.float32),
        "w_down": bell_draw(key_list[17], (FF, D), FF ** -0.5, 0.109375, ((0, 4),)),
        "b_down": bell_draw(key_list[18], (D,), 0.3, 1.75, (), jnp.float32),
        "gain_two": jnp.clip(1.0 + 0.1 * jax.random.normal(key_list[19], (D,), jnp.float32), 0.5, 1.5),
        "shift_two": bell_draw(key_list[20], (D,), 0.3, 1.75, (), jnp.float32),
    }


@jax.custom_vjp
def low(v):
    return lax.optimization_barrier(v.astype(jnp.bfloat16)).astype(jnp.float32)

@jax.custom_vjp
def low_back(v):
    return v

def low_keep(v):
    return (low(v), None)

def low_pass(kept, grad):
    return (grad,)

def back_keep(v):
    return (v, None)

def back_low(kept, grad):
    return (low(grad),)
low.defvjp(low_keep, low_pass)
low_back.defvjp(back_keep, back_low)
ln_eps = 1e-12
logit_divisor = 0.05
loss_scale = 128.0

def mixed_matrix_lines(left, right):
    return jnp.dot(left, right, precision=lax.Precision.HIGHEST, preferred_element_type=jnp.float32)

def layer_norm(value_in, gain, shift):
    center = lax.optimization_barrier(jnp.mean(value_in, axis=-1, keepdims=True))
    centered = value_in - center
    variance = lax.optimization_barrier(jnp.mean(centered * centered, axis=-1, keepdims=True))
    return centered * lax.rsqrt(variance + ln_eps) * gain + shift

def block_loss(params, block_in, keymask, matching_couples, buffered_lookup_vectors, crop_weight):
    w_query, b_query, w_key, w_value, b_value, w_out, b_out, gain_one, shift_one, w_up, b_up, w_down, b_down, gain_two, shift_two = params
    crop_count = keymask.shape[0]
    queries = low(low_back(mixed_matrix_lines(block_in, w_query) + b_query)).reshape(crop_count, SEQ, HEADS, HD)
    key_rows = low(low_back(mixed_matrix_lines(block_in, w_key))).reshape(crop_count, SEQ, HEADS, HD)
    value_rows = low(low_back(mixed_matrix_lines(block_in, w_value) + b_value)).reshape(crop_count, SEQ, HEADS, HD)
    scores = low_back(jnp.einsum('cqhd,ckhd->chqk', queries, key_rows, precision=lax.Precision.HIGHEST) * 0.125)
    scores = jnp.where(keymask[:, None, None, :], scores, -1000000000.0)
    row_max = lax.optimization_barrier(jnp.max(scores, axis=-1, keepdims=True))
    exp_scores = jnp.exp(scores - row_max)
    attn_probs = exp_scores / lax.optimization_barrier(jnp.sum(exp_scores, axis=-1, keepdims=True))
    context = jnp.einsum('chqk,ckhd->cqhd', low(attn_probs), value_rows, precision=lax.Precision.HIGHEST)
    context = low(low_back(context.reshape(crop_count * SEQ, D)))
    attn_out = low_back(mixed_matrix_lines(context, w_out)) + b_out
    hidden = layer_norm(block_in + attn_out, gain_one, shift_one)
    pre_gelu = low_back(mixed_matrix_lines(low(hidden), w_up) + b_up)
    active = low(jax.nn.gelu(pre_gelu, approximate=False))
    ffn_out = low_back(mixed_matrix_lines(active, w_down)) + b_down
    output = layer_norm(hidden + ffn_out, gain_two, shift_two)
    live_tokens = keymask.astype(jnp.float32)
    pooled = lax.optimization_barrier(jnp.sum(output.reshape(crop_count, SEQ, D) * live_tokens[:, :, None], axis=1))
    pooled = pooled / lax.optimization_barrier(jnp.sum(live_tokens, axis=1))[:, None]
    word_vectors = low(pooled * lax.rsqrt(lax.optimization_barrier(jnp.sum(pooled * pooled, axis=-1, keepdims=True)) + 1e-06))
    matching_cosine_scores = lax.optimization_barrier(jnp.sum(word_vectors * matching_couples, axis=-1)) / logit_divisor
    distractor_cosine_scores = mixed_matrix_lines(word_vectors, buffered_lookup_vectors.T) / logit_divisor
    logit_max = jnp.maximum(lax.optimization_barrier(jnp.max(distractor_cosine_scores, axis=-1)), matching_cosine_scores)
    log_total = logit_max + jnp.log(jnp.exp(matching_cosine_scores - logit_max) + lax.optimization_barrier(jnp.sum(jnp.exp(distractor_cosine_scores - logit_max[:, None]), axis=-1)))
    return loss_scale * jnp.sum(crop_weight * (log_total - matching_cosine_scores))

def reference(inputs, token_ids, crop_counts, domain_ids, positives, distractor_buffer, w_query, b_query, w_key, w_value, b_value, w_out, b_out, gain_one, shift_one, w_up, b_up, w_down, b_down, gain_two, shift_two):
    crop_place = jnp.arange(CROPS, dtype=jnp.int32)
    live_crop = (crop_place % CROPS_DEV < crop_counts[crop_place // CROPS_DEV]).astype(jnp.float32)
    member = (domain_ids[:, None] == jnp.arange(2, dtype=jnp.int32)[None, :]).astype(jnp.float32)
    domain_total = lax.optimization_barrier(jnp.sum(member * live_crop[:, None], axis=0))
    own_total = lax.optimization_barrier(jnp.sum(member * domain_total[None, :], axis=1))
    crop_weight = live_crop * CROPS / (2.0 * jnp.maximum(own_total, 1.0))
    params = tuple((item.astype(jnp.float32) for item in (w_query, b_query, w_key, w_value, b_value, w_out, b_out, gain_one, shift_one, w_up, b_up, w_down, b_down, gain_two, shift_two)))
    buffered_lookup_vectors = distractor_buffer.astype(jnp.float32)
    block_ins = inputs.astype(jnp.float32).reshape(BATCH_DEVS, TOK_DEV, D)
    masks = (token_ids != 0).reshape(BATCH_DEVS, CROPS_DEV, SEQ)
    matching_couples = positives.astype(jnp.float32).reshape(BATCH_DEVS, CROPS_DEV, D)
    weight_rows = crop_weight.reshape(BATCH_DEVS, CROPS_DEV)

    def group(running, item):
        block_in, keymask, positive_group, weight_group = item

        def closed(param_set, block_value):
            return block_loss(param_set, block_value, keymask, positive_group, buffered_lookup_vectors, weight_group)
        unused, back = jax.vjp(closed, params, block_in)
        param_grads, input_grad = back(jnp.float32(1.0))
        return (jax.tree.map(jnp.add, running, param_grads), input_grad)
    start = tuple((jnp.zeros_like(item) for item in params))
    gradients, input_grads = lax.scan(group, start, (block_ins, masks, matching_couples, weight_rows))
    return (input_grads.reshape(TOKENS, D), gradients[0], gradients[1], gradients[2], gradients[3], gradients[4], gradients[5], gradients[6], gradients[7], gradients[8], gradients[9], gradients[10], gradients[11], gradients[12], gradients[13], gradients[14])
```

```python
import functools

import jax
import jax.numpy as jnp
from jax import lax
from jax.experimental import pallas as pl
from jax.experimental.pallas import tpu as pltpu
from jax.sharding import PartitionSpec as P

HD = 64
LN_EPS = 1e-12
INV_TEMP = 1.0 / 0.05
LOSS_SCALE = 128.0
MASKED = -1000000000.0
BF = jnp.bfloat16
F32 = jnp.float32
MESH = pl.DeviceIdType.MESH


def dot_nn(left, right):
    return lax.dot_general(left, right, (((1,), (0,)), ((), ())), preferred_element_type=F32)


def dot_nt(left, right):
    return lax.dot_general(left, right, (((1,), (1,)), ((), ())), preferred_element_type=F32)


def dot_tn(left, right):
    return lax.dot_general(left, right, (((0,), (0,)), ((), ())), preferred_element_type=F32)


def loop(count, step):
    def run(i, carry):
        step(i)
        return carry

    lax.fori_loop(0, count, run, 0)


def at(index, size):
    return pl.ds(pl.multiple_of(index * size, size), size)


def remote(src, dst, send_sem, recv_sem, device):
    return pltpu.make_async_remote_copy(
        src_ref=src,
        dst_ref=dst,
        send_sem=send_sem,
        recv_sem=recv_sem,
        device_id=device,
        device_id_type=MESH,
    )


def flip(index, bit):
    return index + bit - 2 * bit * lax.rem(index // bit, 2)


def layer_kernel(sizes, *refs):
    tp_n, dp_n, dq_n, crops_dev, seq, width = sizes
    names = (
        "lens", "dom", "cnt", "x_in", "wqkv_in", "wo_in", "wu_in", "wd_in", "queue_in", "bias_in",
        "vec_in", "pos_in",
        "g_out", "dx_out", "vec_out",
        "wqkv", "wo", "wu", "wd", "xb", "qkv", "prob", "ctx", "xh1", "rstd1", "h1b", "act", "gp",
        "r2", "rstd2",
        "x_s", "ctx_s", "h1_s", "act_s", "df_s", "du_s", "do_s", "dqkv_s",
        "df", "du", "do", "dx", "g0", "r_one", "r_two", "z_one", "z_hi", "res",
        "bb", "emsg", "neg", "shares", "pm_out", "pm_in", "xs", "vbuf", "vrecv",
        "loc", "w_ss", "w_rs", "s_ss", "s_rs", "zd_ss", "zd_rs", "b_ss", "b_rs",
        "a_ss", "a_rs", "e_ss", "e_rs", "p_ss", "p_rs",
        "g1_ss", "g1_rs", "g2_ss", "g2_rs", "gz_ss", "gz_rs", "ga_ss", "ga_rs", "gh_ss", "gh_rs",
        "gf_ss", "gf_rs", "x_ss", "x_rs", "v_ss", "v_rs", "out_sem",
    )
    r = dict(zip(names, refs, strict=True))

    class R:
        pass

    k = R()
    for name, ref in r.items():
        setattr(k, name, ref)

    tokens = crops_dev * seq
    groups = dp_n * dq_n
    dp_bits = dp_n.bit_length() - 1
    hi_bits = (dq_n // 2).bit_length() - 1
    heads_w = width // tp_n
    half = width // 2
    head_half = heads_w // 2
    quarter = half // dp_n
    pairs = width // (2 * HD)

    tp, dp, dq = lax.axis_index("tp"), lax.axis_index("dp"), lax.axis_index("dq")
    core = lax.rem(dq, 2)
    t_x = tp + 1 - 2 * lax.rem(tp, 2)
    t_y = lax.rem(tp + 2, 4)
    t_d = 3 - tp
    t_a = t_x + core * (t_y - t_x)
    t_b = t_x + t_y - t_a
    me = dp * dq_n + dq
    dev_a = (t_a, dp, dq)
    dev_b = (t_b, dp, dq)
    dev_s = (tp, dp, dq + 1 - 2 * core)

    def group_dev(g):
        return (tp, g // dq_n, lax.rem(g, dq_n))

    own_half = at(core, half)
    other_half = at(1 - core, half)

    barrier = pltpu.get_barrier_semaphore()
    for t_peer in (t_x, t_y, t_d):
        pl.semaphore_signal(barrier, inc=1, device_id=(t_peer, dp, dq), device_id_type=MESH)

    def greet(i):
        pl.semaphore_signal(
            barrier, inc=1, device_id=group_dev(lax.rem(me + i + 1, groups)), device_id_type=MESH
        )

    loop(groups - 1, greet)

    locals_ = [
        (k.x_in.at[at(tp, tokens)], k.xb),
        (k.wqkv_in.at[0], k.wqkv.at[0, at(tp, heads_w)]),
        (k.wqkv_in.at[1], k.wqkv.at[1, at(tp, heads_w)]),
        (k.wqkv_in.at[2], k.wqkv.at[2, at(tp, heads_w)]),
        (k.wo_in, k.wo.at[at(tp, heads_w)]),
        (k.wu_in, k.wu.at[tp]),
        (k.wd_in, k.wd.at[tp]),
    ] + [(k.queue_in.at[pl.ds(j * tokens, tokens)], k.du.at[j]) for j in range(tp_n)]
    local = [pltpu.make_async_copy(src, dst, k.loc.at[i]) for i, (src, dst) in enumerate(locals_)]
    for copy in local:
        copy.start()
    pl.semaphore_wait(barrier, 3 + groups - 1)

    def part(c, t, h):
        if c < 3:
            return k.wqkv.at[c, pl.ds(pl.multiple_of(t * heads_w + h * head_half, 32), head_half)]
        if c == 3:
            return k.wo.at[pl.ds(pl.multiple_of(t * heads_w + h * head_half, 32), head_half)]
        if c == 4:
            return k.wu.at[t, at(h, half)]
        return k.wd.at[t, pl.ds(pl.multiple_of(h * half + dp * quarter, 16), quarter)]

    def source(c):
        if c < 3:
            return k.wqkv_in.at[c, at(core, head_half)]
        if c == 3:
            return k.wo_in.at[at(core, head_half)]
        if c == 4:
            return k.wu_in.at[at(core, half)]
        return k.wd_in.at[pl.ds(pl.multiple_of(core * half + dp * quarter, 16), quarter)]

    def w_copy(c, i):
        if i == 0:
            return remote(source(c), part(c, tp, core), k.w_ss.at[c, 0], k.w_rs.at[c, 0], dev_a)
        if i == 1:
            return remote(source(c), part(c, tp, core), k.w_ss.at[c, 1], k.w_rs.at[c, 1], dev_b)
        return remote(
            part(c, t_a, core), part(c, t_a, core), k.w_ss.at[c, 2], k.w_rs.at[c, 2], dev_b
        )

    def w_arrived(c, i):
        t = (t_a, t_b, t_d)[i]
        remote(part(c, t, core), part(c, t, core), k.w_ss.at[c, i], k.w_rs.at[c, i], dev_a).wait_recv()

    def s_part(c, t, h):
        return k.wd.at[t, at(h, half)] if c == 5 else part(c, t, h)

    def s_copy(c, i):
        t = (t_a, t_b, t_d)[i]
        return remote(
            s_part(c, t, core), s_part(c, t, core), k.s_ss.at[c, i], k.s_rs.at[c, t], dev_s
        )

    def s_arrived(c, t):
        remote(
            s_part(c, t, 1 - core), s_part(c, t, 1 - core), k.s_ss.at[c, 0], k.s_rs.at[c, t], dev_s
        ).wait_recv()

    def zd_copy(i, j):
        t = (t_a, t_b, t_d)[i]
        return remote(
            part(5, t, core),
            part(5, t, core),
            k.zd_ss.at[i, j],
            k.zd_rs.at[i, dp],
            (tp, lax.rem(dp + 1 + j, dp_n), dq),
        )

    def zd_arrived(i, j):
        t = (t_a, t_b, t_d)[i]
        z = lax.rem(dp + 1 + j, dp_n)
        there = k.wd.at[t, pl.ds(pl.multiple_of(core * half + z * quarter, 16), quarter)]
        remote(there, there, k.zd_ss.at[i, j], k.zd_rs.at[i, z], dev_s).wait_recv()

    def send_own(c):
        w_copy(c, 0).start()
        w_copy(c, 1).start()

    def pass_on(c, sibling=True):
        w_arrived(c, 0)
        w_copy(c, 2).start()
        if sibling:
            s_copy(c, 0).start()
        w_arrived(c, 1)
        if sibling:
            s_copy(c, 1).start()

    def last_on(c):
        w_arrived(c, 2)
        s_copy(c, 2).start()

    bias_peers = (t_x, t_y, t_d)

    def bias_copy(i):
        return remote(
            k.bias_in, k.bb.at[tp], k.b_ss.at[i], k.b_rs.at[i], (bias_peers[i], dp, dq)
        )

    for i in range(3):
        bias_copy(i).start()
    send_own(5)
    send_own(0)
    send_own(1)
    k.bb[tp] = k.bias_in[...]

    pass_on(5, sibling=False)
    for i in range(2):
        for j in range(dp_n - 1):
            zd_copy(i, j).start()
    send_own(2)
    pass_on(0)
    send_own(3)
    pass_on(1)
    send_own(4)
    w_arrived(5, 2)
    for j in range(dp_n - 1):
        zd_copy(2, j).start()
    last_on(0)

    local[0].wait()
    a_copies = [
        remote(k.xb.at[:, other_half], k.x_s, k.a_ss.at[0], k.a_rs.at[0], dev_s),
        remote(k.ctx, k.ctx_s, k.a_ss.at[1], k.a_rs.at[1], dev_s),
        remote(k.h1b, k.h1_s, k.a_ss.at[2], k.a_rs.at[2], dev_s),
    ]
    a_copies[0].start()
    for i in range(3):
        bias_copy(i).wait_recv()

    def project(c):
        local[1 + c].wait()
        for i in range(3):
            s_arrived(c, (t_a, t_b, t_d)[i])

        def tile(i):
            out = dot_nt(k.xb[...], k.wqkv[c, at(i, 256), :])
            if c != 1:
                row = 1 if c == 0 else 2
                bias = k.bb[0, row : row + 1, at(i, 256)]
                for t in range(1, tp_n):
                    bias = bias + k.bb[t, row : row + 1, at(i, 256)]
                out = out + bias
            out = out.astype(BF)
            k.qkv[c, :, at(i, 256)] = out * BF(0.125) if c == 0 else out

        loop(width // 256, tile)

    pass_on(2)
    last_on(1)
    project(0)
    pass_on(3)
    last_on(2)
    project(1)
    project(2)

    lane = lax.broadcasted_iota(jnp.int32, (seq, 2 * HD), 1)
    first_head = lane < HD
    key_lane = lax.broadcasted_iota(jnp.int32, (seq, seq), 1)

    def attend(i):
        crop, pair = i // pairs, lax.rem(i, pairs)
        rows, cols = at(crop, seq), at(pair, 2 * HD)
        live = key_lane < k.lens[crops_dev * tp + crop]
        q, key, val = k.qkv[0, rows, cols], k.qkv[1, rows, cols], k.qkv[2, rows, cols]
        outs = []
        for h in range(2):
            mine = first_head if h == 0 else ~first_head
            s = dot_nt(jnp.where(mine, q, jnp.zeros_like(q)), key)
            s = jnp.where(live, s, MASKED)
            e = jnp.exp(s - jnp.max(s, axis=-1, keepdims=True))
            p = (e / jnp.sum(e, axis=-1, keepdims=True)).astype(BF)
            k.prob[2 * i + h] = p
            outs.append(dot_nn(p, val))
        k.ctx[rows, cols] = jnp.where(first_head, outs[0], outs[1]).astype(BF)

    loop(crops_dev * pairs // 2, attend)
    last_on(3)
    loop(crops_dev * pairs // 2, lambda i: attend(i + crops_dev * pairs // 2))
    a_copies[1].start()

    local[4].wait()
    for i in range(3):
        s_arrived(3, (t_a, t_b, t_d)[i])

    def attn_out(i):
        rows = at(i, 256)
        k.r2[rows, :] = (
            dot_nn(k.ctx[rows, :], k.wo[...]) + k.vec_in[0:1, :] + k.xb[rows, :].astype(F32)
        )

    loop(tokens // 256, attn_out)

    def norm(v):
        centered = v - jnp.mean(v, axis=-1, keepdims=True)
        rstd = lax.rsqrt(jnp.mean(centered * centered, axis=-1, keepdims=True) + LN_EPS)
        return centered * rstd, rstd

    def norm_one(i):
        rows = at(i, 64)
        xh, rstd = norm(k.r2[rows, :])
        k.xh1[rows, :] = xh
        k.rstd1[rows, :] = rstd
        h1 = xh * k.vec_in[1:2, :] + k.vec_in[2:3, :]
        k.h1b[rows, :] = h1.astype(BF)
        k.r2[rows, :] = h1 + k.vec_in[3:4, :]

    loop(tokens // 64, norm_one)
    a_copies[2].start()

    def act_copy(i):
        t = (tp, t_a, t_b, t_d)[i]
        return remote(
            k.act.at[t, :, other_half], k.act_s.at[t], k.a_ss.at[3 + i], k.a_rs.at[3 + t], dev_s
        )

    def up(t):
        def tile(i):
            cols = at(i, 256)
            u = dot_nn(k.h1b[...], k.wu[t, :, cols]) + k.bb[t, 0:1, cols]
            cdf = 0.5 * lax.erf(u * 0.7071067811865476) + 0.5
            k.act[t, :, cols] = (u * cdf).astype(BF)
            k.gp[t, :, cols] = (cdf + u * (jnp.exp(u * u * -0.5) * 0.3989422804014327)).astype(BF)

        loop(width // 256, tile)

    def down(t):
        def tile(i):
            cols = at(i, 256)
            k.r2[:, cols] += dot_nn(k.act[t], k.wd[t, :, cols])

        loop(width // 256, tile)

    local[5].wait()
    local[6].wait()
    up(tp)
    act_copy(0).start()
    pass_on(4)
    for i in range(3):
        for j in range(dp_n - 1):
            zd_arrived(i, j)
        s_copy(5, i).start()
    down(tp)
    s_arrived(4, t_a)
    up(t_a)
    act_copy(1).start()
    s_arrived(4, t_b)
    up(t_b)
    act_copy(2).start()
    s_arrived(5, t_a)
    down(t_a)
    s_arrived(5, t_b)
    down(t_b)
    last_on(4)
    s_arrived(5, t_d)
    s_arrived(4, t_d)
    up(t_d)
    act_copy(3).start()
    down(t_d)

    sub64 = lax.broadcasted_iota(jnp.int32, (64, 1), 0)
    zero_row = jnp.zeros((1, width), F32)
    lens_f = [k.lens[crops_dev * tp + c].astype(F32) for c in range(crops_dev)]
    k.xs[...] = jnp.zeros_like(k.xs)
    for c in range(crops_dev):

        def norm_two(i, total, c=c):
            rows = pl.ds(pl.multiple_of(c * seq + i * 64, 64), 64)
            xh, rstd = norm(k.r2[rows, :])
            k.r2[rows, :] = xh
            k.rstd2[rows, :] = rstd
            live = sub64 + i * 64 < k.lens[crops_dev * tp + c]
            return total + jnp.sum(jnp.where(live, xh, 0.0), axis=0, keepdims=True)

        k.xs[c : c + 1, :] = lax.fori_loop(0, seq // 64, norm_two, zero_row)

    row8 = lax.broadcasted_iota(jnp.int32, (8, 1), 0)
    row8w = lax.broadcasted_iota(jnp.int32, (8, width), 0)
    lane8w = lax.broadcasted_iota(jnp.int32, (8, width), 1)

    def per_crop(values, other=0.0):
        out = jnp.full((8, 1), other, F32)
        for c in range(crops_dev):
            out = jnp.where(row8 == c, values[c], out)
        return out

    crop_len = per_crop(lens_f, 1.0)
    gain_two, shift_two = k.vec_in[4:5, :], k.vec_in[5:6, :]
    xs = k.xs[...]
    is_crop = row8 < crops_dev
    pooled = jnp.where(is_crop, xs / crop_len * gain_two + shift_two, 0.0)
    inv_norm = lax.rsqrt(jnp.sum(pooled * pooled, axis=-1, keepdims=True) + 1e-06)
    e_own = (pooled * inv_norm).astype(BF).astype(F32)
    live_n = k.cnt[0]
    crops_group = crops_dev * tp_n
    dom_total = [jnp.float32(0.0), jnp.float32(0.0)]
    for c in range(crops_group):
        is_live = jnp.where(c < live_n, 1.0, 0.0)
        is_one = k.dom[c].astype(F32)
        dom_total[0] = dom_total[0] + is_live * (1.0 - is_one)
        dom_total[1] = dom_total[1] + is_live * is_one
    meta = jnp.where(lane8w == 0, dom_total[0], jnp.where(lane8w == 1, dom_total[1], 0.0))
    k.emsg[me] = jnp.where(row8w == crops_dev, meta, e_own)

    def e_copy(i):
        return remote(
            k.emsg.at[me],
            k.emsg.at[me],
            k.e_ss.at[i],
            k.e_rs.at[me],
            group_dev(lax.rem(me + 1 + i, groups)),
        )

    def e_wait(i):
        g = lax.rem(me + 1 + i, groups)
        remote(k.emsg.at[g], k.emsg.at[g], k.e_ss.at[i], k.e_rs.at[g], dev_s).wait_recv()

    loop(groups - 1, lambda i: e_copy(i).start())
    for copy in local[7:]:
        copy.wait()
    loop(groups - 1, e_wait)

    row64 = lax.rem(lax.broadcasted_iota(jnp.int32, (64, 1), 0), 8)
    n_block = 8

    def queue_block(b):
        es = k.emsg[pl.ds(b * n_block, n_block)].reshape(64, width)
        es = jnp.where(row64 < crops_dev, es, 0.0).astype(BF)
        for j in range(tp_n):
            k.neg[:, j * tokens : (j + 1) * tokens] = dot_nt(es, k.du[j]) * INV_TEMP
        neg = k.neg[...]
        top = jnp.max(neg, axis=-1, keepdims=True)
        share = jnp.exp(neg - top)
        total = jnp.sum(share, axis=-1, keepdims=True)
        high = share.astype(BF)
        k.shares[0:64, :] = high
        k.shares[64:128, :] = (share - high.astype(F32)).astype(BF)

        def pull(i):
            cols = at(i, 256)
            both = dot_nn(k.shares[:, 0:tokens], k.du[0, :, cols])
            for j in range(1, tp_n):
                both = both + dot_nn(k.shares[:, j * tokens : (j + 1) * tokens], k.du[j, :, cols])
            k.pm_out[pl.ds(b * n_block, n_block), :, cols] = (both[0:64] + both[64:128]).reshape(
                n_block, 8, 256
            )

        loop(width // 256, pull)
        first = lax.broadcasted_iota(jnp.int32, (64, 128), 1) == 0
        k.pm_out[pl.ds(b * n_block, n_block), :, width:] = jnp.where(first, top, total).reshape(
            n_block, 8, 128
        )

    loop(groups // n_block, queue_block)

    def p_copy(i):
        g = lax.rem(me + 1 + i, groups)
        return remote(k.pm_out.at[g], k.pm_in.at[me], k.p_ss.at[i], k.p_rs.at[me], group_dev(g))

    def p_wait(i):
        g = lax.rem(me + 1 + i, groups)
        remote(k.pm_in.at[g], k.pm_in.at[g], k.p_ss.at[i], k.p_rs.at[g], dev_s).wait_recv()

    loop(groups - 1, lambda i: p_copy(i).start())
    k.pm_in[me] = k.pm_out[me]
    loop(groups - 1, p_wait)

    tops = k.pm_in[:, :, width:]
    top_all = jnp.max(tops, axis=0)[:, 0:1]
    dom_lanes = jnp.sum(k.emsg[:, crops_dev : crops_dev + 1, 0:128], axis=0)

    def merge(g, carry):
        total, pulled = carry
        stats = k.pm_in[g, :, width:]
        scale = jnp.exp(stats[:, 0:1] - top_all)
        return (total + scale * stats[:, 1:2], pulled + scale * k.pm_in[g, :, 0:width])

    total_all, pulled = lax.fori_loop(
        0, groups, merge, (jnp.zeros((8, 1), F32), jnp.zeros((8, width), F32))
    )
    lse_q = top_all + jnp.log(total_all)
    positives = k.pos_in[...]
    pos = jnp.sum(e_own * positives, axis=-1, keepdims=True) * INV_TEMP
    top_both = jnp.maximum(pos, lse_q)
    lse = top_both + jnp.log(jnp.exp(pos - top_both) + jnp.exp(lse_q - top_both))
    weights = []
    for c in range(crops_dev):
        at_c = crops_dev * tp + c
        is_one = k.dom[at_c].astype(F32)
        own_total = dom_lanes[:, 0:1] * (1.0 - is_one) + dom_lanes[:, 1:2] * is_one
        is_live = jnp.where(at_c < live_n, 1.0, 0.0)
        weights.append(
            is_live * (LOSS_SCALE * crops_group * groups) / (2.0 * jnp.maximum(own_total, 1.0))
        )
    crop_weight = per_crop(weights)
    de = crop_weight * (
        (jnp.exp(lse_q - lse) / total_all * INV_TEMP) * pulled
        + ((jnp.exp(pos - lse) - 1.0) * INV_TEMP) * positives
    )
    dpool = inv_norm * (de - pooled * (jnp.sum(pooled * de, axis=-1, keepdims=True) * inv_norm * inv_norm))
    dpool = jnp.where(is_crop, dpool / crop_len, 0.0)
    vec = k.vbuf.at[0]
    vec[...] = jnp.zeros_like(vec)
    vec[6:7, :] = jnp.sum(dpool * xs, axis=0, keepdims=True)
    vec[7:8, :] = jnp.sum(dpool * crop_len, axis=0, keepdims=True)

    dgain = dpool * gain_two
    dgain_mean = jnp.mean(dgain, axis=-1, keepdims=True)
    b_down_sum = zero_row
    for c in range(crops_dev):
        dg, dg_mean = dgain[c : c + 1, :], dgain_mean[c : c + 1, :]

        def norm_two_back(i, total, c=c, dg=dg, dg_mean=dg_mean):
            rows = pl.ds(pl.multiple_of(c * seq + i * 64, 64), 64)
            xh = k.r2[rows, :]
            live = sub64 + i * 64 < k.lens[crops_dev * tp + c]
            scale = jnp.where(live, k.rstd2[rows, :], 0.0)
            dr = scale * (dg - dg_mean - xh * jnp.mean(dg * xh, axis=-1, keepdims=True))
            k.r2[rows, :] = dr
            k.df[rows, :] = dr.astype(BF)
            return total + jnp.sum(dr, axis=0, keepdims=True)

        b_down_sum = lax.fori_loop(0, seq // 64, norm_two_back, b_down_sum)
    vec[3:4, :] = b_down_sum
    df_copy = remote(k.df, k.df_s, k.a_ss.at[7], k.a_rs.at[7], dev_s)
    df_copy.start()

    for c in range(6):
        for i in range(3):
            w_copy(c, i).wait_send()
            s_copy(c, i).wait_send()
    for i in range(3):
        for j in range(dp_n - 1):
            zd_copy(i, j).wait_send()
        bias_copy(i).wait_send()
    for i in range(4):
        act_copy(i).wait_send()
    for copy in a_copies:
        copy.wait_send()
    loop(groups - 1, lambda i: e_copy(i).wait_send())
    loop(groups - 1, lambda i: p_copy(i).wait_send())

    g_ref = (lambda t: k.g0.at[t], lambda t: k.act.at[t, 0:half], lambda t: k.gp.at[t, 0:half])

    def g1_copy(n, i):
        t_from, t_to = ((t_a, 0), (t_d, 1))[i]
        return remote(g_ref[n](t_from), k.r_one.at[n, t_to], k.g1_ss.at[n, i], k.g1_rs.at[n, i], dev_a)

    def g2_copy(n):
        return remote(g_ref[n](t_b), k.r_two.at[n], k.g2_ss.at[n], k.g2_rs.at[n], dev_b)

    def z_span(bits):
        start, size = 0, half
        for bit in range(bits):
            size //= 2
            start = start + lax.rem(dp // (1 << bit), 2) * size
        return start, size

    def z_dev(bit):
        return (tp, flip(dp, 1 << bit), dq)

    def z_rows(start, size):
        return pl.ds(pl.multiple_of(start, 16), size)

    def gz_copy(n, bit):
        start, size = z_span(bit)
        size //= 2
        away = start + (1 - lax.rem(dp // (1 << bit), 2)) * size
        offset = half - 2 * size
        return remote(
            g_ref[n](tp).at[z_rows(away, size)],
            k.z_one.at[n, pl.ds(offset, size)],
            k.gz_ss.at[n, bit],
            k.gz_rs.at[n, bit],
            z_dev(bit),
        )

    def gz_add(n, bit):
        start, size = z_span(bit + 1)
        offset = half - 2 * size
        mine = g_ref[n](tp).at[z_rows(start, size)]
        total = mine[...].astype(F32) + k.z_one[n, pl.ds(offset, size)].astype(F32)
        if bit == dp_bits - 1 and hi_bits == 0:
            k.res[n, z_rows(start, size)] = total.astype(BF)
        else:
            mine[...] = total.astype(BF)

    def gh_copy(n, bit):
        start, size = z_span(dp_bits)
        return remote(
            g_ref[n](tp).at[z_rows(start, size)],
            k.z_hi.at[n, bit],
            k.gh_ss.at[n, bit],
            k.gh_rs.at[n, bit],
            (tp, dp, flip(dq, 2 << bit)),
        )

    def ga_copy(n, bit):
        start, size = z_span(bit + 1)
        rows = k.res.at[n, z_rows(start, size)]
        return remote(rows, rows, k.ga_ss.at[n, bit], k.ga_rs.at[n, bit], z_dev(bit))

    def ga_wait(n, bit):
        start, size = z_span(bit)
        away = start + (1 - lax.rem(dp // (1 << bit), 2)) * (size // 2)
        rows = k.res.at[n, z_rows(away, size // 2)]
        remote(rows, rows, k.ga_ss.at[n, bit], k.ga_rs.at[n, bit], dev_s).wait_recv()

    def gf_copy(n):
        dst = k.g_out.at[n, own_half]
        return remote(k.res.at[n], dst, k.gf_ss.at[n], k.gf_rs.at[n], dev_s)

    def gf_local(n):
        return pltpu.make_async_copy(k.res.at[n], k.g_out.at[n, own_half], k.out_sem.at[n])

    def add_rows(dst, src):
        def step(i):
            rows = at(i, 64)
            dst[rows, :] = (dst[rows, :].astype(F32) + src[rows, :].astype(F32)).astype(BF)

        loop(half // 64, step)

    def plane_first(n):
        g1_copy(n, 0).start()
        g1_copy(n, 1).start()

    def plane_second(n):
        g1_copy(n, 1).wait_recv()
        add_rows(g_ref[n](t_b), k.r_one.at[n, 1])
        g2_copy(n).start()
        g1_copy(n, 0).wait_recv()
        add_rows(g_ref[n](tp), k.r_one.at[n, 0])

    def plane_done(n):
        g2_copy(n).wait_recv()
        add_rows(g_ref[n](tp), k.r_two.at[n])
        gz_copy(n, 0).start()

    def z_step(n, bit):
        gz_copy(n, bit).wait_recv()
        gz_copy(n, bit).wait_send()
        gz_add(n, bit)
        if bit + 1 < dp_bits:
            gz_copy(n, bit + 1).start()

    def z_finish_reduce(n):
        for bit in range(hi_bits):
            gh_copy(n, bit).start()
            gh_copy(n, bit).wait()
            start, size = z_span(dp_bits)
            mine = g_ref[n](tp).at[z_rows(start, size)]
            total = (mine[...].astype(F32) + k.z_hi[n, bit].astype(F32)).astype(BF)
            if bit == hi_bits - 1:
                k.res[n, z_rows(start, size)] = total
            else:
                mine[...] = total
        ga_copy(n, dp_bits - 1).start()

    def z_back(n, bit):
        ga_wait(n, bit)
        if bit > 0:
            ga_copy(n, bit - 1).start()
        else:
            gf_copy(n).start()
            gf_local(n).start()

    def du_copy(i):
        t = (tp, t_a, t_b, t_d)[i]
        return remote(
            k.du.at[t, :, other_half], k.du_s.at[t], k.a_ss.at[8 + i], k.a_rs.at[8 + t], dev_s
        )

    def hidden_back(t):
        def tile(i, _):
            cols = at(i, 256)
            da = dot_nt(k.df[...], k.wd[t, cols, :])
            d = (da * k.gp[t, :, cols].astype(F32)).astype(BF)
            k.du[t, :, cols] = d
            vec[pl.ds(8 + t, 1), cols] = jnp.sum(d.astype(F32), axis=0, keepdims=True)
            return _

        lax.fori_loop(0, width // 256, tile, 0)

    def down_piece(t):
        k.g0[t] = (
            dot_tn(k.act[t, :, own_half], k.df[...]) + dot_tn(k.act_s[t], k.df_s[...])
        ).astype(BF)

    def up_piece(t):
        for h in range(2):
            rows = slice(h * half, (h + 1) * half)
            k.act[t, 0:half, rows] = (
                dot_tn(k.h1b[:, rows], k.du[t, :, own_half]) + dot_tn(k.h1_s[:, rows], k.du_s[t])
            ).astype(BF)

    hidden_back(t_a)
    du_copy(1).start()
    df_copy.wait()
    for t in range(tp_n):
        remote(k.act_s.at[t], k.act_s.at[t], k.a_ss.at[3], k.a_rs.at[3 + t], dev_s).wait_recv()
    down_piece(t_a)
    down_piece(t_d)
    plane_first(0)
    down_piece(t_b)
    down_piece(tp)
    hidden_back(t_d)
    du_copy(3).start()
    hidden_back(t_b)
    du_copy(2).start()
    hidden_back(tp)
    du_copy(0).start()
    a_copies[2].wait_recv()

    def du_arrived(t):
        remote(k.du_s.at[t], k.du_s.at[t], k.a_ss.at[8], k.a_rs.at[8 + t], dev_s).wait_recv()

    du_arrived(t_a)
    up_piece(t_a)
    du_arrived(t_d)
    up_piece(t_d)
    plane_first(1)
    plane_second(0)
    du_arrived(t_b)
    up_piece(t_b)
    du_arrived(tp)
    up_piece(tp)

    def hidden_grad(i):
        cols = at(i, 256)
        total = k.r2[:, cols]
        for t in range(tp_n):
            total = total + dot_nt(k.du[t], k.wu[t, cols, :])
        k.r2[:, cols] = total

    loop(width // 256, hidden_grad)

    gain_one = k.vec_in[1:2, :]

    def norm_one_back(i, sums):
        rows = at(i, 64)
        dh, xh = k.r2[rows, :], k.xh1[rows, :]
        dxh = dh * gain_one
        dr = k.rstd1[rows, :] * (
            dxh
            - jnp.mean(dxh, axis=-1, keepdims=True)
            - xh * jnp.mean(dxh * xh, axis=-1, keepdims=True)
        )
        k.r2[rows, :] = dr
        k.do[rows, :] = dr.astype(BF)
        return (
            sums[0] + jnp.sum(dr, axis=0, keepdims=True),
            sums[1] + jnp.sum(dh * xh, axis=0, keepdims=True),
            sums[2] + jnp.sum(dh, axis=0, keepdims=True),
        )

    out_sum, gain_sum, shift_sum = lax.fori_loop(
        0, tokens // 64, norm_one_back, (zero_row, zero_row, zero_row)
    )
    vec[2:3, :] = out_sum
    vec[4:5, :] = gain_sum
    vec[5:6, :] = shift_sum
    do_copy = remote(k.do.at[:, other_half], k.do_s, k.a_ss.at[12], k.a_rs.at[12], dev_s)
    do_copy.start()

    def context_grad(i):
        k.df[:, at(i, 256)] = dot_nt(k.do[...], k.wo[at(i, 256), :]).astype(BF)

    loop(width // 256, context_grad)
    plane_done(0)

    dqkv = [k.wd.at[c, 0:tokens] for c in range(3)]

    def attend_back(i):
        crop, pair = i // pairs, lax.rem(i, pairs)
        rows, cols = at(crop, seq), at(pair, 2 * HD)
        q, key, val = k.qkv[0, rows, cols], k.qkv[1, rows, cols], k.qkv[2, rows, cols]
        dctx = k.df[rows, cols]
        dqs, dks, dvs = [], [], []
        for h in range(2):
            mine = first_head if h == 0 else ~first_head
            p = k.prob[2 * i + h]
            pf = p.astype(F32)
            dprob = dot_nt(jnp.where(mine, dctx, jnp.zeros_like(dctx)), val)
            ds = (pf * (dprob - jnp.sum(dprob * pf, axis=-1, keepdims=True))).astype(BF)
            dvs.append(dot_tn(p, dctx))
            dqs.append(dot_nn(ds, key))
            dks.append(dot_tn(ds, q))
        dqkv[0][rows, cols] = (jnp.where(first_head, dqs[0], dqs[1]) * 0.125).astype(BF)
        dqkv[1][rows, cols] = jnp.where(first_head, dks[0], dks[1]).astype(BF)
        dqkv[2][rows, cols] = jnp.where(first_head, dvs[0], dvs[1]).astype(BF)

    n_att = crops_dev * pairs
    loop(n_att // 2, attend_back)
    z_step(0, 0)
    plane_second(1)
    loop(n_att // 2, lambda i: attend_back(i + n_att // 2))

    dqkv_copies = [
        remote(dqkv[c], k.dqkv_s.at[c], k.a_ss.at[13 + c], k.a_rs.at[13 + c], dev_s)
        for c in range(3)
    ]
    for copy in dqkv_copies:
        copy.start()
    for bit in range(1, dp_bits):
        z_step(0, bit)
    z_finish_reduce(0)

    def input_grad(i):
        cols = at(i, 256)
        total = k.r2[:, cols]
        for c in range(3):
            total = total + dot_nn(dqkv[c][...], k.wqkv[c, :, cols])
        k.dx[:, cols] = total.astype(BF)

    spots = ((0, 0), (0, 1), (1, 0), (1, 1))

    def head_pieces(c):
        row, col = spots[c]

        def step(i):
            cols = at(i, half)
            if c < 3:
                g = dot_tn(dqkv[c][:, cols], k.xb[:, own_half]) + dot_tn(
                    k.dqkv_s[c, :, cols], k.x_s[...]
                )
            else:
                g = dot_tn(k.ctx[:, cols], k.do[:, own_half]) + dot_tn(k.ctx_s[:, cols], k.do_s[...])
            g = g.astype(BF)
            span = slice(row * heads_w, (row + 1) * heads_w)
            lanes = slice(col * half, (col + 1) * half)
            k.gp[2 * i, span, lanes] = g[0:heads_w]
            k.gp[2 * i + 1, span, lanes] = g[heads_w:]

        loop(tp_n // 2, step)

    a_copies[0].wait_recv()
    a_copies[1].wait_recv()
    do_copy.wait()
    head_pieces(3)
    for c in range(3):
        dqkv_copies[c].wait()
        head_pieces(c)
    plane_first(2)
    vec[0:1, :] = jnp.sum(dqkv[0][...].astype(F32), axis=0, keepdims=True)
    vec[1:2, :] = jnp.sum(dqkv[2][...].astype(F32), axis=0, keepdims=True)
    plane_done(1)
    loop(width // 256, input_grad)

    def dx_rows(t):
        return k.dx_out.at[at(t, tokens)]

    def dx_copy(i):
        if i == 0:
            return remote(k.dx, dx_rows(tp), k.x_ss.at[0], k.x_rs.at[0], dev_a)
        if i == 1:
            return remote(k.dx, dx_rows(tp), k.x_ss.at[1], k.x_rs.at[1], dev_b)
        return remote(dx_rows(t_a), dx_rows(t_a), k.x_ss.at[2], k.x_rs.at[2], dev_b)

    def dx_arrived(i):
        there = dx_rows((t_a, t_b, t_d)[i])
        remote(there, there, k.x_ss.at[i], k.x_rs.at[i], dev_a).wait_recv()

    dx_copy(0).start()
    dx_copy(1).start()
    dx_local = pltpu.make_async_copy(k.dx, dx_rows(tp), k.out_sem.at[3])
    dx_local.start()

    rounds = (
        [dev_s, (t_x, dp, dq), (t_y, dp, dq)]
        + [z_dev(bit) for bit in range(dp_bits)]
        + [(tp, dp, flip(dq, 2 << bit)) for bit in range(hi_bits)]
    )

    def v_copy(i):
        return remote(k.vbuf.at[i], k.vrecv.at[i], k.v_ss.at[i], k.v_rs.at[i], rounds[i])

    def v_step(i):
        v_copy(i).wait_recv()
        k.vbuf[i + 1] = k.vbuf[i] + k.vrecv[i]
        if i + 1 < len(rounds):
            v_copy(i + 1).start()

    v_copy(0).start()
    for bit in range(dp_bits - 1, 0, -1):
        z_back(0, bit)
    z_step(1, 0)
    v_step(0)
    plane_second(2)
    z_back(0, 0)
    for bit in range(1, dp_bits):
        z_step(1, bit)
    z_finish_reduce(1)
    v_step(1)
    for bit in range(dp_bits - 1, -1, -1):
        z_back(1, bit)
    v_step(2)
    plane_done(2)
    dx_arrived(0)
    dx_copy(2).start()
    for bit in range(dp_bits):
        z_step(2, bit)
    z_finish_reduce(2)
    for bit in range(dp_bits - 1, -1, -1):
        z_back(2, bit)
    for i in range(3, len(rounds)):
        v_step(i)
    k.vec_out[...] = k.vbuf[len(rounds)]

    dx_arrived(1)
    dx_arrived(2)
    for i in range(3):
        dx_copy(i).wait_send()
        du_copy(i).wait_send()
    du_copy(3).wait_send()
    dx_local.wait()
    for n in range(3):
        other = k.g_out.at[n, other_half]
        remote(other, other, k.gf_ss.at[n], k.gf_rs.at[n], dev_s).wait_recv()
        gf_copy(n).wait_send()
        gf_local(n).wait()
        for i in range(2):
            g1_copy(n, i).wait_send()
        g2_copy(n).wait_send()
        for bit in range(dp_bits):
            ga_copy(n, bit).wait_send()
    for i in range(len(rounds)):
        v_copy(i).wait_send()


def run_layer(mesh_sizes, args):
    tp_n, dp_n, dq_n = mesh_sizes
    lens, dom, cnt, x_in, wqkv_in, wo_in, wu_in, wd_in, queue_in, bias_in, vec_in, pos_in = args
    width = x_in.shape[1]
    crops_dev = lens.shape[0] // tp_n
    tokens = x_in.shape[0] // tp_n
    seq = tokens // crops_dev
    groups = dp_n * dq_n
    half = width // 2
    dp_bits = dp_n.bit_length() - 1
    hi_bits = (dq_n // 2).bit_length() - 1
    n_rounds = 1 + 2 + dp_bits + hi_bits
    heads = width // HD
    smem = pl.BlockSpec(memory_space=pltpu.SMEM)
    vmem = pl.BlockSpec(memory_space=pltpu.VMEM)
    hbm = pl.BlockSpec(memory_space=pl.ANY)
    dma = pltpu.SemaphoreType.DMA

    def b16(*shape):
        return pltpu.VMEM(shape, BF)

    def f32(*shape):
        return pltpu.VMEM(shape, F32)

    scratch = [
        b16(3, width, width),
        b16(width, width),
        b16(tp_n, width, width),
        b16(tp_n, width, width),
        b16(tokens, width),
        b16(3, tokens, width),
        b16(crops_dev * heads, seq, seq),
        b16(tokens, width),
        f32(tokens, width),
        f32(tokens, 1),
        b16(tokens, width),
        b16(tp_n, tokens, width),
        b16(tp_n, tokens, width),
        f32(tokens, width),
        f32(tokens, 1),
        b16(tokens, half),
        b16(tokens, width),
        b16(tokens, width),
        b16(tp_n, tokens, half),
        b16(tokens, width),
        b16(tp_n, tokens, half),
        b16(tokens, half),
        b16(3, tokens, width),
        b16(tokens, width),
        b16(tp_n, tokens, width),
        b16(tokens, width),
        b16(tokens, width),
        b16(tp_n, half, width),
        b16(3, 2, half, width),
        b16(3, half, width),
        b16(3, half, width),
        b16(3, max(hi_bits, 1), half // dp_n, width),
        b16(3, half, width),
        f32(tp_n, 8, width),
        f32(groups, 8, width),
        f32(64, tp_n * tokens),
        b16(128, tp_n * tokens),
        f32(groups, 8, width + 128),
        f32(groups, 8, width + 128),
        f32(8, width),
        f32(n_rounds + 1, 16, width),
        f32(n_rounds, 16, width),
        dma((7 + tp_n,)),
        dma((6, 3)),
        dma((6, 3)),
        dma((6, 3)),
        dma((6, tp_n)),
        dma((3, dp_n)),
        dma((3, dp_n)),
        dma((3,)),
        dma((3,)),
        dma((16,)),
        dma((16,)),
        dma((groups,)),
        dma((groups,)),
        dma((groups,)),
        dma((groups,)),
        dma((3, 2)),
        dma((3, 2)),
        dma((3,)),
        dma((3,)),
        dma((3, dp_bits)),
        dma((3, dp_bits)),
        dma((3, dp_bits)),
        dma((3, dp_bits)),
        dma((3, max(hi_bits, 1))),
        dma((3, max(hi_bits, 1))),
        dma((3,)),
        dma((3,)),
        dma((3,)),
        dma((3,)),
        dma((n_rounds,)),
        dma((n_rounds,)),
        dma((4,)),
    ]
    return pl.pallas_call(
        functools.partial(layer_kernel, (tp_n, dp_n, dq_n, crops_dev, seq, width)),
        out_shape=(
            jax.ShapeDtypeStruct((3, width, width), BF),
            jax.ShapeDtypeStruct((tp_n * tokens, width), BF),
            jax.ShapeDtypeStruct((16, width), F32),
        ),
        in_specs=[smem, smem, smem] + [hbm] * 6 + [vmem] * 3,
        out_specs=(hbm, hbm, vmem),
        scratch_shapes=scratch,
        compiler_params=pltpu.CompilerParams(
            collective_id=0, has_side_effects=True, vmem_limit_bytes=63 * 2**20
        ),
    )(*args)


def body(
    mesh_sizes,
    inputs,
    token_ids,
    crop_counts,
    domain_ids,
    positives,
    distractor_buffer,
    w_query,
    b_query,
    w_key,
    w_value,
    b_value,
    w_out,
    b_out,
    gain_one,
    shift_one,
    w_up,
    b_up,
    w_down,
    b_down,
    gain_two,
    shift_two,
):
    tp_n = mesh_sizes[0]
    tp = lax.axis_index("tp")
    width = inputs.shape[1]
    heads_w = w_query.shape[1]
    half = width // 2
    crops_dev = token_ids.shape[0] // tp_n
    lens = jnp.sum((token_ids != 0).astype(jnp.int32), axis=1)
    wqkv = jnp.stack([w_query.T, w_key.T, w_value.T])

    def placed(shard):
        return lax.dynamic_update_slice(jnp.zeros((width,), F32), shard, (tp * heads_w,))

    zero = jnp.zeros((width,), F32)
    bias_rows = jnp.stack([b_up, placed(b_query), placed(b_value)] + [zero] * 5)
    vec_rows = jnp.stack([b_out, gain_one, shift_one, b_down, gain_two, shift_two, zero, zero])
    own_positives = lax.dynamic_slice_in_dim(positives, tp * crops_dev, crops_dev).astype(F32)
    own_positives = jnp.pad(own_positives, ((0, 8 - crops_dev), (0, 0)))
    grads, dx, vec = run_layer(
        mesh_sizes,
        (
            lens,
            domain_ids,
            crop_counts,
            inputs,
            wqkv,
            w_out,
            w_up,
            w_down,
            distractor_buffer,
            bias_rows,
            vec_rows,
            own_positives,
        ),
    )
    grads = grads.astype(F32)
    grad_w_down = grads[0]
    grad_w_up = grads[1].reshape(2, half, 2, half).transpose(2, 1, 0, 3).reshape(width, width)
    heads = grads[2].reshape(2, 2, heads_w, 2, half)

    def untransposed(piece):
        return piece.transpose(0, 2, 1).reshape(width, heads_w)

    grad_w_query = untransposed(heads[:, 0, :, 0, :])
    grad_w_key = untransposed(heads[:, 0, :, 1, :])
    grad_w_value = untransposed(heads[:, 1, :, 0, :])
    grad_w_out = heads[:, 1, :, 1, :].transpose(1, 0, 2).reshape(heads_w, width)

    def own(row):
        return lax.dynamic_slice_in_dim(row, tp * heads_w, heads_w)

    return (
        dx.astype(F32),
        grad_w_query,
        own(vec[0]),
        grad_w_key,
        grad_w_value,
        own(vec[1]),
        grad_w_out,
        vec[2],
        vec[4],
        vec[5],
        grad_w_up,
        lax.dynamic_slice_in_dim(vec, 8 + tp, 1)[0],
        grad_w_down,
        vec[3],
        vec[6],
        vec[7],
    )


def solution(mesh):
    mesh_sizes = (mesh.shape["tp"], mesh.shape["dp"], mesh.shape["dq"])
    rows = P(("dp", "dq"), None)
    groups = P(("dp", "dq"))
    return jax.shard_map(
        functools.partial(body, mesh_sizes),
        mesh=mesh,
        in_specs=(
            rows,
            rows,
            groups,
            groups,
            rows,
            rows,
            P(None, "tp"),
            P("tp"),
            P(None, "tp"),
            P(None, "tp"),
            P("tp"),
            P("tp", None),
            P(),
            P(),
            P(),
            P(None, "tp"),
            P("tp"),
            P("tp", None),
            P(),
            P(),
            P(),
        ),
        out_specs=(
            rows,
            P(None, "tp"),
            P("tp"),
            P(None, "tp"),
            P(None, "tp"),
            P("tp"),
            P("tp", None),
            P(),
            P(),
            P(),
            P(None, "tp"),
            P("tp"),
            P("tp", None),
            P(),
            P(),
            P(),
        ),
        check_vma=False,
    )
```

```python
import functools

import jax
import jax.numpy as jnp
from jax import lax
from jax.experimental import pallas as pl
from jax.experimental.pallas import tpu as pltpu
from jax.sharding import PartitionSpec as P

HD = 64
LN_EPS = 1e-12
INV_TEMP = 1.0 / 0.05
LOSS_SCALE = 128.0
MASKED = -1000000000.0
BF = jnp.bfloat16
F32 = jnp.float32
MESH = pl.DeviceIdType.MESH


def dot_nn(left, right):
    return lax.dot_general(left, right, (((1,), (0,)), ((), ())), preferred_element_type=F32)


def dot_nt(left, right):
    return lax.dot_general(left, right, (((1,), (1,)), ((), ())), preferred_element_type=F32)


def dot_tn(left, right):
    return lax.dot_general(left, right, (((0,), (0,)), ((), ())), preferred_element_type=F32)


def loop(count, step):
    def run(i, carry):
        step(i)
        return carry

    lax.fori_loop(0, count, run, 0)


def each(count, step):
    def run(i, carry):
        step(i)
        return carry

    lax.fori_loop(0, count, run, 0)


def at(index, size):
    return pl.ds(pl.multiple_of(index * size, size), size)


def remote(src, dst, send_sem, recv_sem, device):
    return pltpu.make_async_remote_copy(
        src_ref=src,
        dst_ref=dst,
        send_sem=send_sem,
        recv_sem=recv_sem,
        device_id=device,
        device_id_type=MESH,
    )


def flip(index, bit):
    return index + bit - 2 * bit * lax.rem(index // bit, 2)


def layer_kernel(sizes, *refs):
    tp_n, dp_n, dq_n, crops_dev, seq, width = sizes
    names = (
        "ids", "dom", "cnt", "pos_in", "b_q", "b_v", "b_up", "b_out", "gain1", "shift1", "b_down",
        "gain2", "shift2", "x_in", "wq_in", "wk_in", "wv_in", "wo_in", "wu_in", "wd_in", "queue_in",
        "gd_out", "gu_out", "gh_out", "dx_out", "vec_out",
        "wqkv", "wo", "wu", "wd", "xb", "qkv", "prob", "ctx", "xh1", "rstd1", "h1b", "act", "gp",
        "r2", "rstd2",
        "x_s", "ctx_s", "h1_s", "act_s", "df_s", "du_s", "do_s", "dqkv_s",
        "df", "du", "do", "g0", "r_one", "r_two", "z_one", "z_hi", "res",
        "bb", "emsg", "es", "neg", "shares", "pm_out", "pm_in", "xs", "posf", "pulled",
        "vec", "v_plane", "v_z", "v_hi",
        "loc", "w_ss", "w_rs", "s_ss", "s_rs", "zd_ss", "zd_rs", "b_ss", "b_rs",
        "a_ss", "a_rs", "e_ss", "e_rs", "p_ss", "p_rs",
        "g1_ss", "g1_rs", "g2_ss", "g2_rs", "gz_ss", "gz_rs", "ga_ss", "ga_rs", "gh_ss", "gh_rs",
        "gf_ss", "gf_rs", "x_ss", "x_rs", "v_ss", "v_rs", "out_sem",
    )

    class Refs:
        pass

    k = Refs()
    for name, ref in zip(names, refs, strict=True):
        setattr(k, name, ref)

    tokens = crops_dev * seq
    groups = dp_n * dq_n
    dp_bits = dp_n.bit_length() - 1
    hi_bits = (dq_n // 2).bit_length() - 1
    heads_w = width // tp_n
    heads_t = heads_w // HD
    slot = (heads_w + 127) // 128 * 128
    half = width // 2
    head_half = heads_w // 2
    quarter = half // dp_n
    lane_blocks = width // 256

    tp, dp, dq = lax.axis_index("tp"), lax.axis_index("dp"), lax.axis_index("dq")
    core = lax.rem(dq, 2)
    t_x = tp + 1 - 2 * lax.rem(tp, 2)
    t_y = lax.rem(tp + 2, 4)
    t_d = 3 - tp
    t_a = t_x + core * (t_y - t_x)
    t_b = t_x + t_y - t_a
    me = dp * dq_n + dq
    dev_a = (t_a, dp, dq)
    dev_b = (t_b, dp, dq)
    dev_s = (tp, dp, dq + 1 - 2 * core)
    others = (t_a, t_b, t_d)

    def group_dev(g):
        return (tp, g // dq_n, lax.rem(g, dq_n))

    own_half = at(core, half)
    other_half = at(1 - core, half)

    barrier = pltpu.get_barrier_semaphore()
    for t_peer in (t_x, t_y, t_d):
        pl.semaphore_signal(barrier, inc=1, device_id=(t_peer, dp, dq), device_id_type=MESH)

    def greet(i):
        pl.semaphore_signal(
            barrier, inc=1, device_id=group_dev(lax.rem(me + i + 1, groups)), device_id_type=MESH
        )

    each(groups - 1, greet)

    def t_rows(t):
        return at(t, heads_w)

    locals_ = [(k.x_in.at[at(tp, tokens)], k.xb)]
    for c, ref in enumerate((k.wq_in, k.wk_in, k.wv_in)):
        locals_.append((ref.at[0:tokens], k.qkv.at[c, 0]))
        locals_.append((ref.at[tokens:width], k.qkv.at[c, 1, 0 : width - tokens]))
    locals_ += [(k.wo_in, k.wo.at[t_rows(tp)]), (k.wu_in, k.wu.at[tp]), (k.wd_in, k.wd.at[tp])]
    locals_ += [(k.queue_in.at[pl.ds(j * tokens, tokens)], k.du.at[j]) for j in range(tp_n)]
    local = [pltpu.make_async_copy(src, dst, k.loc.at[i]) for i, (src, dst) in enumerate(locals_)]
    for copy in local:
        copy.start()
    k.bb[tp] = jnp.zeros((8, width), F32)
    k.bb[tp, 0:1, :] = k.b_up[...][None, :]
    k.bb[tp, 1:2, 0:heads_w] = k.b_q[...][None, :]
    k.bb[tp, 2:3, 0:heads_w] = k.b_v[...][None, :]
    k.es[...] = jnp.zeros_like(k.es)
    k.pulled[...] = jnp.zeros_like(k.pulled)
    k.xs[...] = jnp.zeros_like(k.xs)
    k.vec[...] = jnp.zeros_like(k.vec)
    pl.semaphore_wait(barrier, 3 + groups - 1)

    def part(c, t, h):
        if c < 3:
            return k.wqkv.at[c, pl.ds(pl.multiple_of(t * heads_w + h * head_half, 32), head_half)]
        if c == 3:
            return k.wo.at[pl.ds(pl.multiple_of(t * heads_w + h * head_half, 32), head_half)]
        if c == 4:
            return k.wu.at[t, at(h, half)]
        return k.wd.at[t, pl.ds(pl.multiple_of(h * half + dp * quarter, 16), quarter)]

    def source(c):
        if c < 3:
            return part(c, tp, core)
        if c == 3:
            return k.wo_in.at[at(core, head_half)]
        if c == 4:
            return k.wu_in.at[at(core, half)]
        return k.wd_in.at[pl.ds(pl.multiple_of(core * half + dp * quarter, 16), quarter)]

    def w_copy(c, i):
        if i < 2:
            return remote(
                source(c), part(c, tp, core), k.w_ss.at[c, i], k.w_rs.at[c, i], (dev_a, dev_b)[i]
            )
        there = part(c, t_a, core)
        return remote(there, there, k.w_ss.at[c, 2], k.w_rs.at[c, 2], dev_b)

    def w_arrived(c, i):
        there = part(c, others[i], core)
        remote(there, there, k.w_ss.at[c, i], k.w_rs.at[c, i], dev_a).wait_recv()

    def s_part(c, t, h):
        return k.wd.at[t, at(h, half)] if c == 5 else part(c, t, h)

    def s_copy(c, i):
        there = s_part(c, others[i], core)
        return remote(there, there, k.s_ss.at[c, i], k.s_rs.at[c, i], dev_s)

    def s_arrived(c, t, i):
        there = s_part(c, t, 1 - core)
        remote(there, there, k.s_ss.at[c, i], k.s_rs.at[c, i], dev_s).wait_recv()

    def from_a(c):
        s_arrived(c, t_a, 1)

    def from_b(c):
        s_arrived(c, t_b, 0)

    def from_d(c):
        s_arrived(c, t_d, 2)

    def zd_copy(i, j):
        there = part(5, others[i], core)
        return remote(
            there,
            there,
            k.zd_ss.at[i, j],
            k.zd_rs.at[i, dp],
            (tp, lax.rem(dp + 1 + j, dp_n), dq),
        )

    def zd_arrived(i, j):
        z = lax.rem(dp + 1 + j, dp_n)
        there = k.wd.at[others[i], pl.ds(pl.multiple_of(core * half + z * quarter, 16), quarter)]
        remote(there, there, k.zd_ss.at[i, j], k.zd_rs.at[i, z], dev_s).wait_recv()

    def send_own(c):
        w_copy(c, 0).start()
        w_copy(c, 1).start()

    def pass_on(c):
        w_arrived(c, 0)
        w_copy(c, 2).start()
        if c < 5:
            s_copy(c, 0).start()
        w_arrived(c, 1)
        if c < 5:
            s_copy(c, 1).start()

    def last_on(c):
        w_arrived(c, 2)
        s_copy(c, 2).start()

    def send_planes(i):
        for j in range(dp_n - 1):
            zd_copy(i, j).start()

    def bias_copy(i):
        mine = k.bb.at[tp]
        return remote(mine, mine, k.b_ss.at[i], k.b_rs.at[i], ((t_x, t_y, t_d)[i], dp, dq))

    def bias_arrived(i):
        there = k.bb.at[(t_x, t_y, t_d)[i]]
        remote(there, there, k.b_ss.at[i], k.b_rs.at[i], dev_s).wait_recv()

    first_head = lax.broadcasted_iota(jnp.int32, (seq, 2 * HD), 1) < HD

    def project(t):
        for c in range(3):
            out = dot_nt(k.xb[...], k.wqkv[c, t_rows(t), :])
            if c != 1:
                row = 1 if c == 0 else 2
                out = out + k.bb[t, row : row + 1, 0:heads_w]
            out = out.astype(BF)
            k.qkv[c, t] = out * BF(0.125) if c == 0 else out

    def head_views(block):
        views = []
        for h in range(heads_t):
            base = h // 2 * 2 * HD
            if h == heads_t - 1 and heads_t % 2:
                views.append((slice(base, base + HD), None))
            else:
                views.append((slice(base, base + 2 * HD), h % 2))
        return views

    views = head_views(heads_w)

    def masked(value, side):
        if side is None:
            return value
        keep = first_head if side == 0 else ~first_head
        return jnp.where(keep, value, jnp.zeros_like(value))

    def merged(outs, store):
        for h, (lanes, side) in enumerate(views):
            if side is None:
                store(lanes, outs[h])
            elif side == 1:
                store(lanes, jnp.where(first_head, outs[h - 1], outs[h]))

    def attend(t, crop):
        rows = slice(crop * seq, (crop + 1) * seq)
        ids = jnp.broadcast_to(k.ids[pl.ds(crops_dev * tp + crop, 1), :], (seq, seq))
        outs = []
        for h, (lanes, side) in enumerate(views):
            s = dot_nt(masked(k.qkv[0, t, rows, lanes], side), k.qkv[1, t, rows, lanes])
            s = jnp.where(ids != 0, s, MASKED)
            e = jnp.exp(s - jnp.max(s, axis=-1, keepdims=True))
            p = (e * (1.0 / jnp.sum(e, axis=-1, keepdims=True))).astype(BF)
            k.prob[(crop * tp_n + t) * heads_t + h] = p
            outs.append(dot_nn(p, k.qkv[2, t, rows, lanes]))

        def store(lanes, value):
            k.ctx[t, rows, lanes] = value.astype(BF)

        merged(outs, store)

    def attention(t):
        project(t)
        for crop in range(crops_dev):
            attend(t, crop)

    send_own(5)
    for c in range(3):
        local[1 + 2 * c].wait()
        local[2 + 2 * c].wait()
        k.wqkv[c, t_rows(tp), 0:tokens] = k.qkv[c, 0].T
        k.wqkv[c, t_rows(tp), tokens:width] = k.qkv[c, 1, 0 : width - tokens].T
        if c < 2:
            send_own(c)
    for i in range(3):
        bias_copy(i).start()
    local[0].wait()
    a_copies = [
        remote(k.xb.at[:, other_half], k.x_s, k.a_ss.at[0], k.a_rs.at[0], dev_s),
        remote(k.ctx, k.ctx_s, k.a_ss.at[1], k.a_rs.at[1], dev_s),
        remote(k.h1b, k.h1_s, k.a_ss.at[2], k.a_rs.at[2], dev_s),
    ]
    a_copies[0].start()
    project(tp)
    pass_on(5)
    send_planes(0)
    send_planes(1)
    send_own(2)
    send_own(3)
    attend(tp, 0)
    pass_on(0)
    for crop in range(1, crops_dev):
        attend(tp, crop)
    pass_on(1)
    w_arrived(5, 2)
    send_planes(2)
    pass_on(2)
    pass_on(3)
    send_own(4)
    for i in range(3):
        bias_arrived(i)
    for c in range(3):
        from_a(c)
    attention(t_a)
    last_on(0)
    for c in range(3):
        from_b(c)
    attention(t_b)
    last_on(1)
    last_on(2)
    last_on(3)
    for c in range(3):
        from_d(c)
    attention(t_d)
    a_copies[1].start()

    local[7].wait()
    from_a(3)
    from_b(3)
    from_d(3)

    def attn_out(i):
        rows = at(i, 256)
        total = k.xb[rows, :].astype(F32) + k.b_out[...][None, :]
        for t in range(tp_n):
            total = total + dot_nn(k.ctx[t, rows, :], k.wo[t * heads_w : (t + 1) * heads_w, :])
        k.r2[rows, :] = total

    loop(tokens // 256, attn_out)

    def norm(v):
        centered = v - jnp.mean(v, axis=-1, keepdims=True)
        rstd = lax.rsqrt(jnp.mean(centered * centered, axis=-1, keepdims=True) + LN_EPS)
        return centered * rstd, rstd

    gain_one = k.gain1[...][None, :]
    shift_one = k.shift1[...][None, :]
    b_down = k.b_down[...][None, :]

    def norm_one(i):
        rows = at(i, 64)
        xh, rstd = norm(k.r2[rows, :])
        k.xh1[rows, :] = xh
        k.rstd1[rows, :] = rstd
        h1 = xh * gain_one + shift_one
        k.h1b[rows, :] = h1.astype(BF)
        k.r2[rows, :] = h1 + b_down

    loop(tokens // 64, norm_one)
    a_copies[2].start()

    def act_copy(i):
        t = (tp, t_a, t_b, t_d)[i]
        return remote(
            k.act.at[t, :, other_half], k.act_s.at[t], k.a_ss.at[3 + i], k.a_rs.at[3 + t], dev_s
        )

    def up(t):
        def tile(i):
            cols = at(i, 256)
            u = dot_nn(k.h1b[...], k.wu[t, :, cols]) + k.bb[t, 0:1, cols]
            cdf = 0.5 * lax.erf(u * 0.7071067811865476) + 0.5
            k.act[t, :, cols] = (u * cdf).astype(BF)
            k.gp[t, :, cols] = (cdf + u * (jnp.exp(u * u * -0.5) * 0.3989422804014327)).astype(BF)

        loop(lane_blocks, tile)

    def down(t):
        def tile(i):
            cols = at(i, 256)
            k.r2[:, cols] += dot_nn(k.act[t], k.wd[t, :, cols])

        loop(lane_blocks, tile)

    local[8].wait()
    local[9].wait()
    pass_on(4)
    up(tp)
    act_copy(0).start()
    from_a(4)
    up(t_a)
    act_copy(1).start()
    from_b(4)
    up(t_b)
    act_copy(2).start()
    down(tp)
    for i in range(3):
        for j in range(dp_n - 1):
            zd_arrived(i, j)
        s_copy(5, i).start()
    last_on(4)
    from_a(5)
    down(t_a)
    from_b(5)
    down(t_b)
    from_d(4)
    up(t_d)
    act_copy(3).start()
    from_d(5)
    down(t_d)

    sub64 = lax.broadcasted_iota(jnp.int32, (64, 1), 0).astype(F32)
    zero_row = jnp.zeros((1, width), F32)

    def crop_ids(c):
        return k.ids[pl.ds(crops_dev * tp + c, 1), :]

    lens = [
        jnp.sum(jnp.where(crop_ids(c) != 0, 1.0, 0.0), axis=-1, keepdims=True)
        for c in range(crops_dev)
    ]
    for c in range(crops_dev):

        def norm_two(i, total, c=c):
            rows = pl.ds(pl.multiple_of(c * seq + i * 64, 64), 64)
            xh, rstd = norm(k.r2[rows, :])
            k.r2[rows, :] = xh
            k.rstd2[rows, :] = rstd
            live = sub64 + (i * 64).astype(F32) < lens[c]
            return total + jnp.sum(jnp.where(live, xh, 0.0), axis=0, keepdims=True)

        k.xs[c : c + 1, :] = lax.fori_loop(0, seq // 64, norm_two, zero_row)

    row8 = lax.broadcasted_iota(jnp.int32, (8, 1), 0)

    def per_crop(values, other=0.0):
        out = jnp.full((8, 1), other, F32)
        for c in range(crops_dev):
            out = jnp.where(row8 == c, values[c], out)
        return out

    crop_len = per_crop(lens, 1.0)
    gain_two, shift_two = k.gain2[...][None, :], k.shift2[...][None, :]
    xs = k.xs[...]
    is_crop = row8 < crops_dev
    pooled = jnp.where(is_crop, xs / crop_len * gain_two + shift_two, 0.0)
    inv_norm = lax.rsqrt(jnp.sum(pooled * pooled, axis=-1, keepdims=True) + 1e-06)
    e_own = (pooled * inv_norm).astype(BF).astype(F32)
    live_n = k.cnt[0]
    crops_group = crops_dev * tp_n
    dom_total = [jnp.float32(0.0), jnp.float32(0.0)]
    for c in range(crops_group):
        is_live = jnp.where(c < live_n, 1.0, 0.0)
        is_one = k.dom[c].astype(F32)
        dom_total[0] = dom_total[0] + is_live * (1.0 - is_one)
        dom_total[1] = dom_total[1] + is_live * is_one
    lane_row = lax.broadcasted_iota(jnp.int32, (1, 256), 1)
    meta_row = crops_dev * lane_blocks

    def crop_block(c, j):
        return slice(c * lane_blocks + j, c * lane_blocks + j + 1)

    def lanes_of(j):
        return slice(j * 256, (j + 1) * 256)

    for c in range(crops_dev):
        for j in range(lane_blocks):
            k.emsg[me, crop_block(c, j), :] = e_own[c : c + 1, lanes_of(j)]
    k.emsg[me, meta_row : meta_row + 1, :] = jnp.where(
        lane_row == 0, dom_total[0], jnp.where(lane_row == 1, dom_total[1], 0.0)
    )

    def e_copy(i):
        mine = k.emsg.at[me]
        return remote(
            mine, mine, k.e_ss.at[i], k.e_rs.at[me], group_dev(lax.rem(me + 1 + i, groups))
        )

    def e_wait(i):
        g = lax.rem(me + 1 + i, groups)
        remote(k.emsg.at[g], k.emsg.at[g], k.e_ss.at[i], k.e_rs.at[g], dev_s).wait_recv()

    each(groups - 1, lambda i: e_copy(i).start())
    k.posf[...] = k.pos_in[...].astype(F32)
    positives = jnp.concatenate(
        [k.posf[pl.ds(crops_dev * tp + c, 1), :] for c in range(crops_dev)]
        + [jnp.zeros((8 - crops_dev, width), F32)],
        axis=0,
    )
    pos = jnp.sum(e_own * positives, axis=-1, keepdims=True) * INV_TEMP
    for copy in local[10:]:
        copy.wait()
    each(groups - 1, e_wait)
    for c in range(crops_dev):
        for j in range(lane_blocks):
            k.es[:, c : c + 1, lanes_of(j)] = k.emsg[:, crop_block(c, j), :]

    n_block = 8
    lane_msg = lax.broadcasted_iota(jnp.int32, (n_block, 1, 256), 2)

    def queue_block(b):
        span = pl.ds(b * n_block, n_block)
        es = k.es[span].reshape(8 * n_block, width).astype(BF)
        for j in range(tp_n):
            k.neg[:, j * tokens : (j + 1) * tokens] = dot_nt(es, k.du[j]) * INV_TEMP
        neg = k.neg[...]
        top = jnp.max(neg, axis=-1, keepdims=True)
        share = jnp.exp(neg - top)
        total = jnp.sum(share, axis=-1, keepdims=True)
        high = share.astype(BF)
        k.shares[0 : 8 * n_block, :] = high
        k.shares[8 * n_block :, :] = (share - high.astype(F32)).astype(BF)
        for j in range(lane_blocks):
            both = dot_nn(k.shares[:, 0:tokens], k.du[0, :, lanes_of(j)])
            for i in range(1, tp_n):
                both = both + dot_nn(
                    k.shares[:, i * tokens : (i + 1) * tokens], k.du[i, :, lanes_of(j)]
                )
            pull = (both[0 : 8 * n_block] + both[8 * n_block :]).reshape(n_block, 8, 256)
            for c in range(crops_dev):
                k.pm_out[span, crop_block(c, j), :] = pull[:, c : c + 1, :]
        top = top.reshape(n_block, 8, 1)
        total = total.reshape(n_block, 8, 1)
        stats = jnp.zeros((n_block, 1, 256), F32)
        for c in range(crops_dev):
            stats = jnp.where(lane_msg == 2 * c, top[:, c : c + 1, :], stats)
            stats = jnp.where(lane_msg == 2 * c + 1, total[:, c : c + 1, :], stats)
        k.pm_out[span, meta_row : meta_row + 1, :] = stats

    loop(groups // n_block, queue_block)

    def p_copy(i):
        g = lax.rem(me + 1 + i, groups)
        return remote(k.pm_out.at[g], k.pm_in.at[me], k.p_ss.at[i], k.p_rs.at[me], group_dev(g))

    def p_wait(i):
        g = lax.rem(me + 1 + i, groups)
        remote(k.pm_in.at[g], k.pm_in.at[g], k.p_ss.at[i], k.p_rs.at[g], dev_s).wait_recv()

    each(groups - 1, lambda i: p_copy(i).start())
    k.pm_in[me] = k.pm_out[me]
    dom_lanes = jnp.sum(k.emsg[:, meta_row : meta_row + 1, :], axis=0)
    weights = []
    for c in range(crops_dev):
        at_c = crops_dev * tp + c
        is_one = k.dom[at_c].astype(F32)
        own_total = dom_lanes[:, 0:1] * (1.0 - is_one) + dom_lanes[:, 1:2] * is_one
        is_live = jnp.where(at_c < live_n, 1.0, 0.0)
        weights.append(
            is_live * (LOSS_SCALE * crops_group * groups) / (2.0 * jnp.maximum(own_total, 1.0))
        )
    crop_weight = per_crop(weights)
    each(groups - 1, p_wait)

    tops_all, totals_all = [], []
    for c in range(crops_dev):
        tops = k.pm_in[:, meta_row : meta_row + 1, 2 * c : 2 * c + 1]
        totals = k.pm_in[:, meta_row : meta_row + 1, 2 * c + 1 : 2 * c + 2]
        top_c = jnp.max(tops, axis=0, keepdims=True)
        scale = jnp.exp(tops - top_c)
        tops_all.append(top_c[0])
        totals_all.append(jnp.sum(scale * totals, axis=0))
        for j in range(lane_blocks):
            k.pulled[c : c + 1, lanes_of(j)] = jnp.sum(
                scale * k.pm_in[:, crop_block(c, j), :], axis=0
            )
    total_all = per_crop(totals_all, 1.0)
    lse_q = per_crop(tops_all) + jnp.log(total_all)
    top_both = jnp.maximum(pos, lse_q)
    lse = top_both + jnp.log(jnp.exp(pos - top_both) + jnp.exp(lse_q - top_both))
    de = crop_weight * (
        (jnp.exp(lse_q - lse) / total_all * INV_TEMP) * k.pulled[...]
        + ((jnp.exp(pos - lse) - 1.0) * INV_TEMP) * positives
    )
    dpool = inv_norm * (
        de - pooled * (jnp.sum(pooled * de, axis=-1, keepdims=True) * inv_norm * inv_norm)
    )
    dpool = jnp.where(is_crop, dpool / crop_len, 0.0)
    k.vec[6:7, :] = jnp.sum(dpool * xs, axis=0, keepdims=True)
    k.vec[7:8, :] = jnp.sum(dpool * crop_len, axis=0, keepdims=True)

    dgain = dpool * gain_two
    dgain_mean = jnp.mean(dgain, axis=-1, keepdims=True)
    b_down_sum = zero_row
    for c in range(crops_dev):
        dg, dg_mean = dgain[c : c + 1, :], dgain_mean[c : c + 1, :]

        def norm_two_back(i, total, c=c, dg=dg, dg_mean=dg_mean):
            rows = pl.ds(pl.multiple_of(c * seq + i * 64, 64), 64)
            xh = k.r2[rows, :]
            live = sub64 + (i * 64).astype(F32) < lens[c]
            scale = jnp.where(live, k.rstd2[rows, :], 0.0)
            dr = scale * (dg - dg_mean - xh * jnp.mean(dg * xh, axis=-1, keepdims=True))
            k.r2[rows, :] = dr
            k.df[rows, :] = dr.astype(BF)
            return total + jnp.sum(dr, axis=0, keepdims=True)

        b_down_sum = lax.fori_loop(0, seq // 64, norm_two_back, b_down_sum)
    k.vec[3:4, :] = b_down_sum
    df_copy = remote(k.df, k.df_s, k.a_ss.at[7], k.a_rs.at[7], dev_s)
    df_copy.start()

    for c in range(6):
        for i in range(3):
            w_copy(c, i).wait_send()
            s_copy(c, i).wait_send()
    for i in range(3):
        for j in range(dp_n - 1):
            zd_copy(i, j).wait_send()
        bias_copy(i).wait_send()
    for i in range(4):
        act_copy(i).wait_send()
    for copy in a_copies:
        copy.wait_send()
    each(groups - 1, lambda i: e_copy(i).wait_send())
    each(groups - 1, lambda i: p_copy(i).wait_send())

    g_ref = (lambda t: k.g0.at[t], lambda t: k.act.at[t, 0:half], lambda t: k.gp.at[t, 0:half])

    def g1_copy(n, i):
        t_from = (t_a, t_d)[i]
        return remote(g_ref[n](t_from), k.r_one.at[n, i], k.g1_ss.at[n, i], k.g1_rs.at[n, i], dev_a)

    def g2_copy(n):
        return remote(g_ref[n](t_b), k.r_two.at[n], k.g2_ss.at[n], k.g2_rs.at[n], dev_b)

    def z_span(bits):
        start, size = 0, half
        for bit in range(bits):
            size //= 2
            start = start + lax.rem(dp // (1 << bit), 2) * size
        return start, size

    def z_dev(bit):
        return (tp, flip(dp, 1 << bit), dq)

    def z_rows(start, size):
        return pl.ds(pl.multiple_of(start, 16), size)

    def gz_copy(n, bit):
        start, size = z_span(bit)
        size //= 2
        away = start + (1 - lax.rem(dp // (1 << bit), 2)) * size
        offset = half - 2 * size
        return remote(
            g_ref[n](tp).at[z_rows(away, size)],
            k.z_one.at[n, pl.ds(offset, size)],
            k.gz_ss.at[n, bit],
            k.gz_rs.at[n, bit],
            z_dev(bit),
        )

    def gz_add(n, bit):
        start, size = z_span(bit + 1)
        offset = half - 2 * size
        mine = g_ref[n](tp).at[z_rows(start, size)]
        total = mine[...].astype(F32) + k.z_one[n, pl.ds(offset, size)].astype(F32)
        if bit == dp_bits - 1 and hi_bits == 0:
            k.res[n, z_rows(start, size)] = total.astype(BF)
        else:
            mine[...] = total.astype(BF)

    def gh_copy(n, bit):
        start, size = z_span(dp_bits)
        return remote(
            g_ref[n](tp).at[z_rows(start, size)],
            k.z_hi.at[n, bit],
            k.gh_ss.at[n, bit],
            k.gh_rs.at[n, bit],
            (tp, dp, flip(dq, 2 << bit)),
        )

    def ga_copy(n, bit):
        start, size = z_span(bit + 1)
        rows = k.res.at[n, z_rows(start, size)]
        return remote(rows, rows, k.ga_ss.at[n, bit], k.ga_rs.at[n, bit], z_dev(bit))

    def ga_wait(n, bit):
        start, size = z_span(bit)
        away = start + (1 - lax.rem(dp // (1 << bit), 2)) * (size // 2)
        rows = k.res.at[n, z_rows(away, size // 2)]
        remote(rows, rows, k.ga_ss.at[n, bit], k.ga_rs.at[n, bit], dev_s).wait_recv()

    spots = ((0, 0), (0, 1), (1, 0), (1, 1))

    def head_spot(j):
        row, col = spots[j]
        return slice(row * heads_w, (row + 1) * heads_w), slice(col * half, (col + 1) * half)

    def final_parts(n, cols):
        if n == 0:
            return [(k.res.at[0], k.gd_out.at[cols])]
        if n == 1:
            return [
                (k.res.at[1, :, h * half : (h + 1) * half], k.gu_out.at[h * half : (h + 1) * half, cols])
                for h in range(2)
            ]
        return [(k.res.at[2, head_spot(j)[0], head_spot(j)[1]], k.gh_out.at[j, :, cols]) for j in range(4)]

    def final_copies(n):
        first = (0, 1, 3)[n]
        away, here = [], []
        for i, (src, dst) in enumerate(final_parts(n, own_half)):
            away.append(remote(src, dst, k.gf_ss.at[first + i], k.gf_rs.at[first + i], dev_s))
            here.append(pltpu.make_async_copy(src, dst, k.out_sem.at[first + i]))
        return away, here

    def final_arrived(n):
        first = (0, 1, 3)[n]
        for i, (_, dst) in enumerate(final_parts(n, other_half)):
            remote(dst, dst, k.gf_ss.at[first + i], k.gf_rs.at[first + i], dev_s).wait_recv()

    def add_rows(dst, srcs):
        def step(i):
            rows = at(i, 64)
            total = dst[rows, :].astype(F32)
            for src in srcs:
                total = total + src[rows, :].astype(F32)
            dst[rows, :] = total.astype(BF)

        loop(half // 64, step)

    def plane_second(n):
        g1_copy(n, 1).wait_recv()
        add_rows(g_ref[n](t_b), [k.r_one.at[n, 1]])
        g2_copy(n).start()

    def plane_done(n):
        g1_copy(n, 0).wait_recv()
        g2_copy(n).wait_recv()
        add_rows(g_ref[n](tp), [k.r_one.at[n, 0], k.r_two.at[n]])
        gz_copy(n, 0).start()

    def z_step(n, bit):
        gz_copy(n, bit).wait()
        gz_add(n, bit)
        if bit + 1 < dp_bits:
            gz_copy(n, bit + 1).start()
            return
        for b in range(hi_bits):
            gh_copy(n, b).start()
            gh_copy(n, b).wait()
            start, size = z_span(dp_bits)
            mine = g_ref[n](tp).at[z_rows(start, size)]
            total = (mine[...].astype(F32) + k.z_hi[n, b].astype(F32)).astype(BF)
            if b == hi_bits - 1:
                k.res[n, z_rows(start, size)] = total
            else:
                mine[...] = total
        ga_copy(n, dp_bits - 1).start()

    def z_back(n, bit):
        ga_wait(n, bit)
        if bit > 0:
            ga_copy(n, bit - 1).start()
        else:
            for copies in final_copies(n):
                for copy in copies:
                    copy.start()

    def du_copy(t, i):
        return remote(
            k.du.at[t, :, other_half], k.du_s.at[t], k.a_ss.at[8 + i], k.a_rs.at[8 + t], dev_s
        )

    def du_arrived(t):
        remote(k.du_s.at[t], k.du_s.at[t], k.a_ss.at[8], k.a_rs.at[8 + t], dev_s).wait_recv()

    def hidden_back(t, i):
        def tile(j):
            cols = at(j, 256)
            da = dot_nt(k.df[...], k.wd[t, cols, :])
            d = (da * k.gp[t, :, cols].astype(F32)).astype(BF)
            k.du[t, :, cols] = d
            k.vec[pl.ds(8 + t, 1), cols] = jnp.sum(d.astype(F32), axis=0, keepdims=True)

        loop(lane_blocks, tile)
        du_copy(t, i).start()

    def down_piece(t):
        k.g0[t] = (
            dot_tn(k.act[t, :, own_half], k.df[...]) + dot_tn(k.act_s[t], k.df_s[...])
        ).astype(BF)

    def up_piece(t):
        du_arrived(t)
        for h in range(2):
            rows = slice(h * half, (h + 1) * half)
            k.act[t, 0:half, rows] = (
                dot_tn(k.h1b[:, rows], k.du[t, :, own_half]) + dot_tn(k.h1_s[:, rows], k.du_s[t])
            ).astype(BF)

    hidden_back(t_d, 0)
    df_copy.wait()
    for t in range(tp_n):
        remote(k.act_s.at[t], k.act_s.at[t], k.a_ss.at[3], k.a_rs.at[3 + t], dev_s).wait_recv()
    down_piece(t_d)
    g1_copy(0, 1).start()
    down_piece(t_a)
    g1_copy(0, 0).start()
    hidden_back(t_a, 1)
    down_piece(t_b)
    hidden_back(t_b, 2)
    down_piece(tp)
    hidden_back(tp, 3)
    a_copies[2].wait_recv()
    up_piece(t_d)
    g1_copy(1, 1).start()
    plane_second(0)
    up_piece(t_a)
    g1_copy(1, 0).start()
    up_piece(t_b)
    up_piece(tp)

    def hidden_grad(i):
        cols = at(i, 256)
        total = k.r2[:, cols]
        for t in range(tp_n):
            total = total + dot_nt(k.du[t], k.wu[t, cols, :])
        k.r2[:, cols] = total

    loop(lane_blocks, hidden_grad)

    def norm_one_back(i, sums):
        rows = at(i, 64)
        dh, xh = k.r2[rows, :], k.xh1[rows, :]
        dxh = dh * gain_one
        dr = k.rstd1[rows, :] * (
            dxh
            - jnp.mean(dxh, axis=-1, keepdims=True)
            - xh * jnp.mean(dxh * xh, axis=-1, keepdims=True)
        )
        k.r2[rows, :] = dr
        k.do[rows, :] = dr.astype(BF)
        return (
            sums[0] + jnp.sum(dr, axis=0, keepdims=True),
            sums[1] + jnp.sum(dh * xh, axis=0, keepdims=True),
            sums[2] + jnp.sum(dh, axis=0, keepdims=True),
        )

    out_sum, gain_sum, shift_sum = lax.fori_loop(
        0, tokens // 64, norm_one_back, (zero_row, zero_row, zero_row)
    )
    k.vec[2:3, :] = out_sum
    k.vec[4:5, :] = gain_sum
    k.vec[5:6, :] = shift_sum
    do_copy = remote(k.do.at[:, other_half], k.do_s, k.a_ss.at[12], k.a_rs.at[12], dev_s)
    do_copy.start()

    def grad_lanes(c, lanes):
        return slice(c * slot + lanes.start, c * slot + lanes.stop)

    def attend_back(t, crop):
        rows = slice(crop * seq, (crop + 1) * seq)
        dctx_all = dot_nt(k.do[rows, :], k.wo[t_rows(t), :]).astype(BF)
        dqs, dks, dvs = [], [], []
        for h, (lanes, side) in enumerate(views):
            q, key, val = (k.qkv[c, t, rows, lanes] for c in range(3))
            dctx = dctx_all[:, lanes]
            p = k.prob[(crop * tp_n + t) * heads_t + h]
            pf = p.astype(F32)
            dprob = dot_nt(masked(dctx, side), val)
            ds = (pf * (dprob - jnp.sum(dprob * pf, axis=-1, keepdims=True))).astype(BF)
            dvs.append(dot_tn(p, dctx))
            dqs.append(dot_nn(ds, key) * 0.125)
            dks.append(dot_tn(ds, q))
        for c, outs in enumerate((dqs, dks, dvs)):

            def store(lanes, value, c=c):
                k.wd[t, rows, grad_lanes(c, lanes)] = value.astype(BF)

            merged(outs, store)

    def dqkv_copy(t, i):
        return remote(
            k.wd.at[t, 0:tokens], k.dqkv_s.at[t], k.a_ss.at[13 + i], k.a_rs.at[13 + t], dev_s
        )

    def dqkv_arrived(t):
        there = k.dqkv_s.at[t]
        remote(there, there, k.a_ss.at[13], k.a_rs.at[13 + t], dev_s).wait_recv()

    def attention_back(t, i):
        for crop in range(crops_dev):
            attend_back(t, crop)
        dqkv_copy(t, i).start()

    heads_lanes = slice(0, heads_w)

    def out_piece(t):
        rows, lanes = head_spot(3)
        k.gp[t, rows, lanes] = (
            dot_tn(k.ctx[t], k.do[:, own_half]) + dot_tn(k.ctx_s[t], k.do_s[...])
        ).astype(BF)

    def head_piece(t):
        dqkv_arrived(t)
        for c in range(3):
            rows, lanes = head_spot(c)
            cols = grad_lanes(c, heads_lanes)
            k.gp[t, rows, lanes] = (
                dot_tn(k.wd[t, 0:tokens, cols], k.xb[:, own_half])
                + dot_tn(k.dqkv_s[t, :, cols], k.x_s[...])
            ).astype(BF)

    def input_grad(i):
        cols = at(i, 256)
        total = k.r2[:, cols]
        for t in range(tp_n):
            for c in range(3):
                total = total + dot_nn(
                    k.wd[t, 0:tokens, grad_lanes(c, heads_lanes)],
                    k.wqkv[c, t * heads_w : (t + 1) * heads_w, cols],
                )
        k.do[:, cols] = total.astype(BF)

    def dx_rows(t):
        return k.dx_out.at[at(t, tokens)]

    def dx_copy(i):
        if i < 2:
            return remote(k.do, dx_rows(tp), k.x_ss.at[i], k.x_rs.at[i], (dev_a, dev_b)[i])
        return remote(dx_rows(t_a), dx_rows(t_a), k.x_ss.at[2], k.x_rs.at[2], dev_b)

    def dx_arrived(i):
        there = dx_rows(others[i])
        remote(there, there, k.x_ss.at[i], k.x_rs.at[i], dev_a).wait_recv()

    def v_sibling():
        return remote(k.vec, k.v_hi.at[0], k.v_ss.at[0], k.v_rs.at[0], dev_s)

    def v_plane(i):
        mine = k.v_plane.at[tp]
        return remote(
            mine, mine, k.v_ss.at[1 + i], k.v_rs.at[1 + i], ((t_x, t_y, t_d)[i], dp, dq)
        )

    def v_plane_arrived(i):
        there = k.v_plane.at[(t_x, t_y, t_d)[i]]
        remote(there, there, k.v_ss.at[1 + i], k.v_rs.at[1 + i], dev_s).wait_recv()

    def v_planes(j):
        mine = k.v_z.at[dp]
        return remote(
            mine, mine, k.v_ss.at[4 + j], k.v_rs.at[4 + dp], (tp, lax.rem(dp + 1 + j, dp_n), dq)
        )

    def v_planes_arrived(j):
        z = lax.rem(dp + 1 + j, dp_n)
        there = k.v_z.at[z]
        remote(there, there, k.v_ss.at[4 + j], k.v_rs.at[4 + z], dev_s).wait_recv()

    def v_group(bit):
        at_ = 4 + dp_n + bit
        return remote(
            k.v_hi.at[1 + 2 * bit],
            k.v_hi.at[2 + 2 * bit],
            k.v_ss.at[at_],
            k.v_rs.at[at_],
            (tp, dp, flip(dq, 2 << bit)),
        )

    attention_back(t_d, 0)
    do_copy.wait()
    a_copies[0].wait_recv()
    a_copies[1].wait_recv()
    out_piece(t_d)
    out_piece(t_a)
    attention_back(t_a, 1)
    plane_done(0)
    head_piece(t_d)
    g1_copy(2, 1).start()
    attention_back(t_b, 2)
    head_piece(t_a)
    g1_copy(2, 0).start()
    plane_second(1)
    attention_back(tp, 3)
    z_step(0, 0)
    out_piece(t_b)
    out_piece(tp)
    head_piece(t_b)
    head_piece(tp)
    for t in range(tp_n):
        for c, lanes in ((0, slice(0, heads_w)), (2, slice(slot, slot + heads_w))):
            grads = k.wd[t, 0:tokens, grad_lanes(c, heads_lanes)].astype(F32)
            k.vec[12 + t : 13 + t, lanes] = jnp.sum(grads, axis=0, keepdims=True)
    v_sibling().start()
    loop(lane_blocks, input_grad)
    dx_local = pltpu.make_async_copy(k.do, dx_rows(tp), k.out_sem.at[7])
    dx_local.start()
    v_sibling().wait()
    k.v_plane[tp] = k.vec[...] + k.v_hi[0]
    for i in range(3):
        v_plane(i).start()
    for bit in range(1, dp_bits):
        z_step(0, bit)
    plane_done(1)
    z_back(0, dp_bits - 1)
    plane_second(2)
    dx_copy(0).start()
    dx_copy(1).start()
    z_step(1, 0)
    for bit in range(dp_bits - 2, -1, -1):
        z_back(0, bit)
    for bit in range(1, dp_bits):
        z_step(1, bit)
    for i in range(3):
        v_plane_arrived(i)
    v_sum = k.v_plane[0]
    for t in range(1, tp_n):
        v_sum = v_sum + k.v_plane[t]
    k.v_z[dp] = v_sum
    plane_done(2)
    for j in range(dp_n - 1):
        v_planes(j).start()
    z_back(1, dp_bits - 1)
    z_step(2, 0)
    dx_arrived(0)
    dx_copy(2).start()
    for bit in range(dp_bits - 2, -1, -1):
        z_back(1, bit)
    for bit in range(1, dp_bits):
        z_step(2, bit)
    for j in range(dp_n - 1):
        v_planes_arrived(j)
    v_all = k.v_z[0]
    for z in range(1, dp_n):
        v_all = v_all + k.v_z[z]
    for bit in range(hi_bits):
        k.v_hi[1 + 2 * bit] = v_all
        v_group(bit).start()
        v_group(bit).wait_recv()
        v_all = v_all + k.v_hi[2 + 2 * bit]
    k.vec_out[...] = v_all
    for bit in range(dp_bits - 1, -1, -1):
        z_back(2, bit)

    dx_arrived(1)
    dx_arrived(2)
    for i in range(3):
        dx_copy(i).wait_send()
        v_plane(i).wait_send()
    for j in range(dp_n - 1):
        v_planes(j).wait_send()
    for bit in range(hi_bits):
        v_group(bit).wait_send()
    for i, t in enumerate((t_d, t_a, t_b, tp)):
        du_copy(t, i).wait_send()
        dqkv_copy(t, i).wait_send()
    dx_local.wait()
    for n in range(3):
        final_arrived(n)
        away, here = final_copies(n)
        for copy in away:
            copy.wait_send()
        for copy in here:
            copy.wait()
        for i in range(2):
            g1_copy(n, i).wait_send()
        g2_copy(n).wait_send()
        for bit in range(dp_bits):
            ga_copy(n, bit).wait_send()


def run_layer(mesh_sizes, args):
    tp_n, dp_n, dq_n = mesh_sizes
    ids, x_in = args[0], args[13]
    width = x_in.shape[1]
    crops_dev = ids.shape[0] // tp_n
    tokens = x_in.shape[0] // tp_n
    seq = tokens // crops_dev
    groups = dp_n * dq_n
    half = width // 2
    heads_w = width // tp_n
    dp_bits = dp_n.bit_length() - 1
    hi_bits = (dq_n // 2).bit_length() - 1
    heads = width // HD
    smem = pl.BlockSpec(memory_space=pltpu.SMEM)
    vmem = pl.BlockSpec(memory_space=pltpu.VMEM)
    hbm = pl.BlockSpec(memory_space=pl.ANY)
    dma = pltpu.SemaphoreType.DMA

    def b16(*shape):
        return pltpu.VMEM(shape, BF)

    def f32(*shape):
        return pltpu.VMEM(shape, F32)

    scratch = [
        b16(3, width, width),
        b16(width, width),
        b16(tp_n, width, width),
        b16(tp_n, width, width),
        b16(tokens, width),
        b16(3, tp_n, tokens, heads_w),
        b16(crops_dev * heads, seq, seq),
        b16(tp_n, tokens, heads_w),
        f32(tokens, width),
        f32(tokens, 1),
        b16(tokens, width),
        b16(tp_n, tokens, width),
        b16(tp_n, tokens, width),
        f32(tokens, width),
        f32(tokens, 1),
        b16(tokens, half),
        b16(tp_n, tokens, heads_w),
        b16(tokens, width),
        b16(tp_n, tokens, half),
        b16(tokens, width),
        b16(tp_n, tokens, half),
        b16(tokens, half),
        b16(tp_n, tokens, width),
        b16(tokens, width),
        b16(tp_n, tokens, width),
        b16(tokens, width),
        b16(tp_n, half, width),
        b16(3, 2, half, width),
        b16(3, half, width),
        b16(3, half - half // dp_n, width),
        b16(3, max(hi_bits, 1), half // dp_n, width),
        b16(3, half, width),
        f32(tp_n, 8, width),
        f32(groups, 8, 256),
        f32(groups, 8, width),
        f32(64, tp_n * tokens),
        b16(128, tp_n * tokens),
        f32(groups, 8, 256),
        f32(groups, 8, 256),
        f32(8, width),
        f32(ids.shape[0], width),
        f32(8, width),
        f32(16, width),
        f32(tp_n, 16, width),
        f32(dp_n, 16, width),
        f32(1 + 2 * hi_bits, 16, width),
        dma((10 + tp_n,)),
        dma((6, 3)),
        dma((6, 3)),
        dma((6, 3)),
        dma((6, 3)),
        dma((3, dp_n)),
        dma((3, dp_n)),
        dma((3,)),
        dma((3,)),
        dma((17,)),
        dma((17,)),
        dma((groups,)),
        dma((groups,)),
        dma((groups,)),
        dma((groups,)),
        dma((3, 2)),
        dma((3, 2)),
        dma((3,)),
        dma((3,)),
        dma((3, dp_bits)),
        dma((3, dp_bits)),
        dma((3, dp_bits)),
        dma((3, dp_bits)),
        dma((3, max(hi_bits, 1))),
        dma((3, max(hi_bits, 1))),
        dma((7,)),
        dma((7,)),
        dma((3,)),
        dma((3,)),
        dma((4 + dp_n + hi_bits,)),
        dma((4 + dp_n + hi_bits,)),
        dma((8,)),
    ]
    return pl.pallas_call(
        functools.partial(layer_kernel, (tp_n, dp_n, dq_n, crops_dev, seq, width)),
        out_shape=(
            jax.ShapeDtypeStruct((width, width), BF),
            jax.ShapeDtypeStruct((width, width), BF),
            jax.ShapeDtypeStruct((4, heads_w, width), BF),
            jax.ShapeDtypeStruct((tp_n * tokens, width), BF),
            jax.ShapeDtypeStruct((16, width), F32),
        ),
        in_specs=[vmem, smem, smem] + [vmem] * 10 + [hbm] * 8,
        out_specs=(hbm, hbm, hbm, hbm, vmem),
        scratch_shapes=scratch,
        compiler_params=pltpu.CompilerParams(
            collective_id=0, has_side_effects=True, vmem_limit_bytes=63 * 2**20
        ),
    )(*args)


def widen_kernel(gd, gu, gh, go, dx, gd_o, gu_o, gq_o, gk_o, gv_o, go_o, dx_o):
    gd_o[...] = gd[...].astype(F32)
    gu_o[...] = gu[...].astype(F32)
    go_o[...] = go[0].astype(F32)
    dx_o[...] = dx[...].astype(F32)
    for c, out in enumerate((gq_o, gk_o, gv_o)):
        out[...] = gh[c].astype(F32).T


def widen(gd, gu, gh, dx):
    width, tokens, heads_w = gd.shape[0], dx.shape[0], gh.shape[1]
    steps = 8
    lane_steps = width // 128
    row_steps = heads_w // 48
    rows = pl.BlockSpec((width // steps, width), lambda i: (i, 0))
    tall = pl.BlockSpec((128, heads_w), lambda i: (jnp.minimum(i, lane_steps - 1), 0))
    out = pl.BlockSpec((48, width), lambda i: (jnp.minimum(i, row_steps - 1), 0))
    tokens_spec = pl.BlockSpec((tokens // steps, width), lambda i: (i, 0))
    return pl.pallas_call(
        widen_kernel,
        grid=(steps,),
        out_shape=(
            jax.ShapeDtypeStruct((width, width), F32),
            jax.ShapeDtypeStruct((width, width), F32),
            jax.ShapeDtypeStruct((width, heads_w), F32),
            jax.ShapeDtypeStruct((width, heads_w), F32),
            jax.ShapeDtypeStruct((width, heads_w), F32),
            jax.ShapeDtypeStruct((heads_w, width), F32),
            jax.ShapeDtypeStruct((tokens, width), F32),
        ),
        in_specs=[
            rows,
            rows,
            pl.BlockSpec((3, heads_w, 128), lambda i: (0, 0, jnp.minimum(i, lane_steps - 1))),
            pl.BlockSpec((1, 48, width), lambda i: (3, jnp.minimum(i, row_steps - 1), 0)),
            tokens_spec,
        ],
        out_specs=(rows, rows, tall, tall, tall, out, tokens_spec),
    )(gd, gu, gh, gh, dx)


def body(
    mesh_sizes,
    inputs,
    token_ids,
    crop_counts,
    domain_ids,
    positives,
    distractor_buffer,
    w_query,
    b_query,
    w_key,
    w_value,
    b_value,
    w_out,
    b_out,
    gain_one,
    shift_one,
    w_up,
    b_up,
    w_down,
    b_down,
    gain_two,
    shift_two,
):
    tp = lax.axis_index("tp")
    heads_w = w_query.shape[1]
    slot = (heads_w + 127) // 128 * 128
    gd, gu, gh, dx, vec = run_layer(
        mesh_sizes,
        (
            token_ids,
            domain_ids,
            crop_counts,
            positives,
            b_query,
            b_value,
            b_up,
            b_out,
            gain_one,
            shift_one,
            b_down,
            gain_two,
            shift_two,
            inputs,
            w_query,
            w_key,
            w_value,
            w_out,
            w_up,
            w_down,
            distractor_buffer,
        ),
    )
    grad_w_down, grad_w_up, grad_w_query, grad_w_key, grad_w_value, grad_w_out, grad_inputs = widen(
        gd, gu, gh, dx
    )
    own_up = lax.dynamic_slice_in_dim(vec, 8 + tp, 1)[0]
    own_heads = lax.dynamic_slice_in_dim(vec, 12 + tp, 1)[0]
    return (
        grad_inputs,
        grad_w_query,
        own_heads[0:heads_w],
        grad_w_key,
        grad_w_value,
        own_heads[slot : slot + heads_w],
        grad_w_out,
        vec[2],
        vec[4],
        vec[5],
        grad_w_up,
        own_up,
        grad_w_down,
        vec[3],
        vec[6],
        vec[7],
    )


def solution(mesh):
    mesh_sizes = (mesh.shape["tp"], mesh.shape["dp"], mesh.shape["dq"])
    rows = P(("dp", "dq"), None)
    groups = P(("dp", "dq"))
    return jax.shard_map(
        functools.partial(body, mesh_sizes),
        mesh=mesh,
        in_specs=(
            rows,
            rows,
            groups,
            groups,
            rows,
            rows,
            P(None, "tp"),
            P("tp"),
            P(None, "tp"),
            P(None, "tp"),
            P("tp"),
            P("tp", None),
            P(),
            P(),
            P(),
            P(None, "tp"),
            P("tp"),
            P("tp", None),
            P(),
            P(),
            P(),
        ),
        out_specs=(
            rows,
            P(None, "tp"),
            P("tp"),
            P(None, "tp"),
            P(None, "tp"),
            P("tp"),
            P("tp", None),
            P(),
            P(),
            P(),
            P(None, "tp"),
            P("tp"),
            P("tp", None),
            P(),
            P(),
            P(),
        ),
        check_vma=False,
    )
```

```python
import functools

import jax
import jax.numpy as jnp
from jax import lax
from jax.experimental import pallas as pl
from jax.experimental.pallas import tpu as pltpu
from jax.sharding import PartitionSpec as P

HD = 64
LN_EPS = 1e-12
INV_TEMP = 1.0 / 0.05
LOSS_SCALE = 128.0
MASKED = -1000000000.0
BF = jnp.bfloat16
F32 = jnp.float32
MESH = pl.DeviceIdType.MESH


def dot_nn(left, right):
    return lax.dot_general(left, right, (((1,), (0,)), ((), ())), preferred_element_type=F32)


def dot_nt(left, right):
    return lax.dot_general(left, right, (((1,), (1,)), ((), ())), preferred_element_type=F32)


def dot_tn(left, right):
    return lax.dot_general(left, right, (((0,), (0,)), ((), ())), preferred_element_type=F32)


def loop(count, step):
    def run(i, carry):
        step(i)
        return carry

    lax.fori_loop(0, count, run, 0)


def each(count, step):
    def run(i, carry):
        step(i)
        return carry

    lax.fori_loop(0, count, run, 0)


def at(index, size):
    return pl.ds(pl.multiple_of(index * size, size), size)


def remote(src, dst, send_sem, recv_sem, device):
    return pltpu.make_async_remote_copy(
        src_ref=src,
        dst_ref=dst,
        send_sem=send_sem,
        recv_sem=recv_sem,
        device_id=device,
        device_id_type=MESH,
    )


def flip(index, bit):
    return index + bit - 2 * bit * lax.rem(index // bit, 2)


def layer_kernel(sizes, *refs):
    tp_n, dp_n, dq_n, crops_dev, seq, width = sizes
    names = (
        "ids", "dom", "cnt", "pos_in", "b_q", "b_v", "b_up", "b_out", "gain1", "shift1", "b_down",
        "gain2", "shift2", "x_in", "wq_in", "wk_in", "wv_in", "wo_in", "wu_in", "wd_in", "queue_in",
        "gd_out", "gu_out", "gh_out", "dx_out", "vec_out",
        "wqkv", "wo", "wu", "wd", "xb", "qkv", "prob", "ctx", "xh1", "rstd1", "h1b", "act", "gp",
        "r2", "rstd2",
        "x_s", "ctx_s", "h1_s", "act_s", "df_s", "du_s", "do_s", "dqkv_s",
        "df", "du", "do", "g0", "r_one", "r_two", "z_one", "z_hi", "res",
        "bb", "emsg", "es", "neg", "shares", "pm_out", "pm_in", "xs", "posf", "pulled",
        "vec", "v_plane", "v_z", "v_hi",
        "loc", "w_ss", "w_rs", "s_ss", "s_rs", "zd_ss", "zd_rs", "b_ss", "b_rs",
        "a_ss", "a_rs", "e_ss", "e_rs", "p_ss", "p_rs",
        "g1_ss", "g1_rs", "g2_ss", "g2_rs", "gz_ss", "gz_rs", "ga_ss", "ga_rs", "gh_ss", "gh_rs",
        "gf_ss", "gf_rs", "x_ss", "x_rs", "v_ss", "v_rs", "out_sem",
    )

    class Refs:
        pass

    k = Refs()
    for name, ref in zip(names, refs, strict=True):
        setattr(k, name, ref)

    tokens = crops_dev * seq
    groups = dp_n * dq_n
    dp_bits = dp_n.bit_length() - 1
    hi_bits = (dq_n // 2).bit_length() - 1
    heads_w = width // tp_n
    heads_t = heads_w // HD
    slot = (heads_w + 127) // 128 * 128
    half = width // 2
    head_half = heads_w // 2
    quarter = half // dp_n
    lane_blocks = width // 256

    tp, dp, dq = lax.axis_index("tp"), lax.axis_index("dp"), lax.axis_index("dq")
    core = lax.rem(dq, 2)
    t_x = tp + 1 - 2 * lax.rem(tp, 2)
    t_y = lax.rem(tp + 2, 4)
    t_d = 3 - tp
    t_a = t_x + core * (t_y - t_x)
    t_b = t_x + t_y - t_a
    me = dp * dq_n + dq
    dev_a = (t_a, dp, dq)
    dev_b = (t_b, dp, dq)
    dev_s = (tp, dp, dq + 1 - 2 * core)
    others = (t_a, t_b, t_d)

    def group_dev(g):
        return (tp, g // dq_n, lax.rem(g, dq_n))

    own_half = at(core, half)
    other_half = at(1 - core, half)

    barrier = pltpu.get_barrier_semaphore()
    for t_peer in (t_x, t_y, t_d):
        pl.semaphore_signal(barrier, inc=1, device_id=(t_peer, dp, dq), device_id_type=MESH)

    def greet(i):
        pl.semaphore_signal(
            barrier, inc=1, device_id=group_dev(lax.rem(me + i + 1, groups)), device_id_type=MESH
        )

    each(groups - 1, greet)

    def t_rows(t):
        return at(t, heads_w)

    locals_ = [(k.x_in.at[at(tp, tokens)], k.xb)]
    heads_in = (k.wq_in, k.wk_in, k.wv_in)
    locals_ += [(heads_in[c], k.wqkv.at[c, t_rows(tp)]) for c in range(3)]
    locals_ += [(k.wo_in, k.wo.at[t_rows(tp)]), (k.wu_in, k.wu.at[tp]), (k.wd_in, k.wd.at[tp])]
    locals_ += [(k.queue_in.at[pl.ds(j * tokens, tokens)], k.du.at[j]) for j in range(tp_n)]
    local = [pltpu.make_async_copy(src, dst, k.loc.at[i]) for i, (src, dst) in enumerate(locals_)]
    for copy in local:
        copy.start()
    k.bb[tp] = jnp.zeros((8, width), F32)
    k.bb[tp, 0:1, :] = k.b_up[...][None, :]
    k.bb[tp, 1:2, 0:heads_w] = k.b_q[...][None, :]
    k.bb[tp, 2:3, 0:heads_w] = k.b_v[...][None, :]
    k.es[...] = jnp.zeros_like(k.es)
    k.pulled[...] = jnp.zeros_like(k.pulled)
    k.xs[...] = jnp.zeros_like(k.xs)
    k.vec[...] = jnp.zeros_like(k.vec)
    pl.semaphore_wait(barrier, 3 + groups - 1)

    def part(c, t, h):
        if c < 3:
            return k.wqkv.at[c, pl.ds(pl.multiple_of(t * heads_w + h * head_half, 32), head_half)]
        if c == 3:
            return k.wo.at[pl.ds(pl.multiple_of(t * heads_w + h * head_half, 32), head_half)]
        if c == 4:
            return k.wu.at[t, at(h, half)]
        return k.wd.at[t, pl.ds(pl.multiple_of(h * half + dp * quarter, 16), quarter)]

    def source(c):
        if c < 3:
            return heads_in[c].at[at(core, head_half)]
        if c == 3:
            return k.wo_in.at[at(core, head_half)]
        if c == 4:
            return k.wu_in.at[at(core, half)]
        return k.wd_in.at[pl.ds(pl.multiple_of(core * half + dp * quarter, 16), quarter)]

    def w_copy(c, i):
        if i < 2:
            return remote(
                source(c), part(c, tp, core), k.w_ss.at[c, i], k.w_rs.at[c, i], (dev_a, dev_b)[i]
            )
        there = part(c, t_a, core)
        return remote(there, there, k.w_ss.at[c, 2], k.w_rs.at[c, 2], dev_b)

    def w_arrived(c, i):
        there = part(c, others[i], core)
        remote(there, there, k.w_ss.at[c, i], k.w_rs.at[c, i], dev_a).wait_recv()

    def s_part(c, t, h):
        return k.wd.at[t, at(h, half)] if c == 5 else part(c, t, h)

    def s_copy(c, i):
        there = s_part(c, others[i], core)
        return remote(there, there, k.s_ss.at[c, i], k.s_rs.at[c, i], dev_s)

    def s_arrived(c, t, i):
        there = s_part(c, t, 1 - core)
        remote(there, there, k.s_ss.at[c, i], k.s_rs.at[c, i], dev_s).wait_recv()

    def from_a(c):
        s_arrived(c, t_a, 1)

    def from_b(c):
        s_arrived(c, t_b, 0)

    def from_d(c):
        s_arrived(c, t_d, 2)

    def zd_copy(i, j):
        there = part(5, others[i], core)
        return remote(
            there,
            there,
            k.zd_ss.at[i, j],
            k.zd_rs.at[i, dp],
            (tp, lax.rem(dp + 1 + j, dp_n), dq),
        )

    def zd_arrived(i, j):
        z = lax.rem(dp + 1 + j, dp_n)
        there = k.wd.at[others[i], pl.ds(pl.multiple_of(core * half + z * quarter, 16), quarter)]
        remote(there, there, k.zd_ss.at[i, j], k.zd_rs.at[i, z], dev_s).wait_recv()

    def send_own(c):
        w_copy(c, 0).start()
        w_copy(c, 1).start()

    def pass_on(c):
        w_arrived(c, 0)
        w_copy(c, 2).start()
        if c < 5:
            s_copy(c, 0).start()
        w_arrived(c, 1)
        if c < 5:
            s_copy(c, 1).start()

    def last_on(c):
        w_arrived(c, 2)
        s_copy(c, 2).start()

    def send_planes(i):
        for j in range(dp_n - 1):
            zd_copy(i, j).start()

    def bias_copy(i):
        mine = k.bb.at[tp]
        return remote(mine, mine, k.b_ss.at[i], k.b_rs.at[i], ((t_x, t_y, t_d)[i], dp, dq))

    def bias_arrived(i):
        there = k.bb.at[(t_x, t_y, t_d)[i]]
        remote(there, there, k.b_ss.at[i], k.b_rs.at[i], dev_s).wait_recv()

    first_head = lax.broadcasted_iota(jnp.int32, (seq, 2 * HD), 1) < HD

    def project(t):
        for c in range(3):
            out = dot_nt(k.xb[...], k.wqkv[c, t_rows(t), :])
            if c != 1:
                row = 1 if c == 0 else 2
                out = out + k.bb[t, row : row + 1, 0:heads_w]
            out = out.astype(BF)
            k.qkv[c, t] = out * BF(0.125) if c == 0 else out

    def head_views(block):
        views = []
        for h in range(heads_t):
            base = h // 2 * 2 * HD
            if h == heads_t - 1 and heads_t % 2:
                views.append((slice(base, base + HD), None))
            else:
                views.append((slice(base, base + 2 * HD), h % 2))
        return views

    views = head_views(heads_w)

    def masked(value, side):
        if side is None:
            return value
        keep = first_head if side == 0 else ~first_head
        return jnp.where(keep, value, jnp.zeros_like(value))

    def merged(outs, store):
        for h, (lanes, side) in enumerate(views):
            if side is None:
                store(lanes, outs[h])
            elif side == 1:
                store(lanes, jnp.where(first_head, outs[h - 1], outs[h]))

    def attend(t, crop):
        rows = slice(crop * seq, (crop + 1) * seq)
        ids = jnp.broadcast_to(k.ids[pl.ds(crops_dev * tp + crop, 1), :], (seq, seq))
        outs = []
        for h, (lanes, side) in enumerate(views):
            s = dot_nt(masked(k.qkv[0, t, rows, lanes], side), k.qkv[1, t, rows, lanes])
            s = jnp.where(ids != 0, s, MASKED)
            e = jnp.exp(s - jnp.max(s, axis=-1, keepdims=True))
            p = (e * (1.0 / jnp.sum(e, axis=-1, keepdims=True))).astype(BF)
            k.prob[(crop * tp_n + t) * heads_t + h] = p
            outs.append(dot_nn(p, k.qkv[2, t, rows, lanes]))

        def store(lanes, value):
            k.ctx[t, rows, lanes] = value.astype(BF)

        merged(outs, store)

    def attention(t):
        project(t)
        for crop in range(crops_dev):
            attend(t, crop)

    send_own(5)
    send_own(0)
    send_own(1)
    for i in range(3):
        bias_copy(i).start()
    for copy in local[0:4]:
        copy.wait()
    a_copies = [
        remote(k.xb.at[:, other_half], k.x_s, k.a_ss.at[0], k.a_rs.at[0], dev_s),
        remote(k.ctx, k.ctx_s, k.a_ss.at[1], k.a_rs.at[1], dev_s),
        remote(k.h1b, k.h1_s, k.a_ss.at[2], k.a_rs.at[2], dev_s),
    ]
    a_copies[0].start()
    project(tp)
    pass_on(5)
    send_planes(0)
    send_planes(1)
    send_own(2)
    send_own(3)
    attend(tp, 0)
    pass_on(0)
    for crop in range(1, crops_dev):
        attend(tp, crop)
    pass_on(1)
    w_arrived(5, 2)
    send_planes(2)
    pass_on(2)
    pass_on(3)
    send_own(4)
    for i in range(3):
        bias_arrived(i)
    for c in range(3):
        from_a(c)
    attention(t_a)
    last_on(0)
    for c in range(3):
        from_b(c)
    attention(t_b)
    last_on(1)
    last_on(2)
    last_on(3)
    for c in range(3):
        from_d(c)
    attention(t_d)
    a_copies[1].start()

    local[4].wait()
    from_a(3)
    from_b(3)
    from_d(3)

    def attn_out(i):
        rows = at(i, 256)
        total = k.xb[rows, :].astype(F32) + k.b_out[...][None, :]
        for t in range(tp_n):
            total = total + dot_nn(k.ctx[t, rows, :], k.wo[t * heads_w : (t + 1) * heads_w, :])
        k.r2[rows, :] = total

    loop(tokens // 256, attn_out)

    def norm(v):
        centered = v - jnp.mean(v, axis=-1, keepdims=True)
        rstd = lax.rsqrt(jnp.mean(centered * centered, axis=-1, keepdims=True) + LN_EPS)
        return centered * rstd, rstd

    gain_one = k.gain1[...][None, :]
    shift_one = k.shift1[...][None, :]
    b_down = k.b_down[...][None, :]

    def norm_one(i):
        rows = at(i, 64)
        xh, rstd = norm(k.r2[rows, :])
        k.xh1[rows, :] = xh
        k.rstd1[rows, :] = rstd
        h1 = xh * gain_one + shift_one
        k.h1b[rows, :] = h1.astype(BF)
        k.r2[rows, :] = h1 + b_down

    loop(tokens // 64, norm_one)
    a_copies[2].start()

    def act_copy(i):
        t = (tp, t_a, t_b, t_d)[i]
        return remote(
            k.act.at[t, :, other_half], k.act_s.at[t], k.a_ss.at[3 + i], k.a_rs.at[3 + t], dev_s
        )

    def up(t):
        def tile(i):
            cols = at(i, 256)
            u = dot_nn(k.h1b[...], k.wu[t, :, cols]) + k.bb[t, 0:1, cols]
            cdf = 0.5 * lax.erf(u * 0.7071067811865476) + 0.5
            k.act[t, :, cols] = (u * cdf).astype(BF)
            k.gp[t, :, cols] = (cdf + u * (jnp.exp(u * u * -0.5) * 0.3989422804014327)).astype(BF)

        loop(lane_blocks, tile)

    def down(t):
        def tile(i):
            cols = at(i, 256)
            k.r2[:, cols] += dot_nn(k.act[t], k.wd[t, :, cols])

        loop(lane_blocks, tile)

    local[5].wait()
    local[6].wait()
    pass_on(4)
    up(tp)
    act_copy(0).start()
    from_a(4)
    up(t_a)
    act_copy(1).start()
    from_b(4)
    up(t_b)
    act_copy(2).start()
    down(tp)
    for i in range(3):
        for j in range(dp_n - 1):
            zd_arrived(i, j)
        s_copy(5, i).start()
    last_on(4)
    from_a(5)
    down(t_a)
    from_b(5)
    down(t_b)
    from_d(4)
    up(t_d)
    act_copy(3).start()
    from_d(5)
    down(t_d)

    sub64 = lax.broadcasted_iota(jnp.int32, (64, 1), 0).astype(F32)
    zero_row = jnp.zeros((1, width), F32)

    def crop_ids(c):
        return k.ids[pl.ds(crops_dev * tp + c, 1), :]

    lens = [
        jnp.sum(jnp.where(crop_ids(c) != 0, 1.0, 0.0), axis=-1, keepdims=True)
        for c in range(crops_dev)
    ]
    for c in range(crops_dev):

        def norm_two(i, total, c=c):
            rows = pl.ds(pl.multiple_of(c * seq + i * 64, 64), 64)
            xh, rstd = norm(k.r2[rows, :])
            k.r2[rows, :] = xh
            k.rstd2[rows, :] = rstd
            live = sub64 + (i * 64).astype(F32) < lens[c]
            return total + jnp.sum(jnp.where(live, xh, 0.0), axis=0, keepdims=True)

        k.xs[c : c + 1, :] = lax.fori_loop(0, seq // 64, norm_two, zero_row)

    row8 = lax.broadcasted_iota(jnp.int32, (8, 1), 0)

    def per_crop(values, other=0.0):
        out = jnp.full((8, 1), other, F32)
        for c in range(crops_dev):
            out = jnp.where(row8 == c, values[c], out)
        return out

    crop_len = per_crop(lens, 1.0)
    gain_two, shift_two = k.gain2[...][None, :], k.shift2[...][None, :]
    xs = k.xs[...]
    is_crop = row8 < crops_dev
    pooled = jnp.where(is_crop, xs / crop_len * gain_two + shift_two, 0.0)
    inv_norm = lax.rsqrt(jnp.sum(pooled * pooled, axis=-1, keepdims=True) + 1e-06)
    e_own = (pooled * inv_norm).astype(BF).astype(F32)
    live_n = k.cnt[0]
    crops_group = crops_dev * tp_n
    dom_total = [jnp.float32(0.0), jnp.float32(0.0)]
    for c in range(crops_group):
        is_live = jnp.where(c < live_n, 1.0, 0.0)
        is_one = k.dom[c].astype(F32)
        dom_total[0] = dom_total[0] + is_live * (1.0 - is_one)
        dom_total[1] = dom_total[1] + is_live * is_one
    lane_row = lax.broadcasted_iota(jnp.int32, (1, 256), 1)
    meta_row = crops_dev * lane_blocks

    def crop_block(c, j):
        return slice(c * lane_blocks + j, c * lane_blocks + j + 1)

    def lanes_of(j):
        return slice(j * 256, (j + 1) * 256)

    for c in range(crops_dev):
        for j in range(lane_blocks):
            k.emsg[me, crop_block(c, j), :] = e_own[c : c + 1, lanes_of(j)]
    k.emsg[me, meta_row : meta_row + 1, :] = jnp.where(
        lane_row == 0, dom_total[0], jnp.where(lane_row == 1, dom_total[1], 0.0)
    )

    def e_copy(i):
        mine = k.emsg.at[me]
        return remote(
            mine, mine, k.e_ss.at[i], k.e_rs.at[me], group_dev(lax.rem(me + 1 + i, groups))
        )

    def e_wait(i):
        g = lax.rem(me + 1 + i, groups)
        remote(k.emsg.at[g], k.emsg.at[g], k.e_ss.at[i], k.e_rs.at[g], dev_s).wait_recv()

    each(groups - 1, lambda i: e_copy(i).start())
    k.posf[...] = k.pos_in[...].astype(F32)
    positives = jnp.concatenate(
        [k.posf[pl.ds(crops_dev * tp + c, 1), :] for c in range(crops_dev)]
        + [jnp.zeros((8 - crops_dev, width), F32)],
        axis=0,
    )
    pos = jnp.sum(e_own * positives, axis=-1, keepdims=True) * INV_TEMP
    for copy in local[7:]:
        copy.wait()
    each(groups - 1, e_wait)
    for c in range(crops_dev):
        for j in range(lane_blocks):
            k.es[:, c : c + 1, lanes_of(j)] = k.emsg[:, crop_block(c, j), :]

    n_block = 8
    lane_msg = lax.broadcasted_iota(jnp.int32, (n_block, 1, 256), 2)

    def queue_block(b):
        span = pl.ds(b * n_block, n_block)
        es = k.es[span].reshape(8 * n_block, width).astype(BF)
        for j in range(tp_n):
            k.neg[:, j * tokens : (j + 1) * tokens] = dot_nt(es, k.du[j]) * INV_TEMP
        neg = k.neg[...]
        top = jnp.max(neg, axis=-1, keepdims=True)
        share = jnp.exp(neg - top)
        total = jnp.sum(share, axis=-1, keepdims=True)
        high = share.astype(BF)
        k.shares[0 : 8 * n_block, :] = high
        k.shares[8 * n_block :, :] = (share - high.astype(F32)).astype(BF)
        for j in range(lane_blocks):
            both = dot_nn(k.shares[:, 0:tokens], k.du[0, :, lanes_of(j)])
            for i in range(1, tp_n):
                both = both + dot_nn(
                    k.shares[:, i * tokens : (i + 1) * tokens], k.du[i, :, lanes_of(j)]
                )
            pull = (both[0 : 8 * n_block] + both[8 * n_block :]).reshape(n_block, 8, 256)
            for c in range(crops_dev):
                k.pm_out[span, crop_block(c, j), :] = pull[:, c : c + 1, :]
        top = top.reshape(n_block, 8, 1)
        total = total.reshape(n_block, 8, 1)
        stats = jnp.zeros((n_block, 1, 256), F32)
        for c in range(crops_dev):
            stats = jnp.where(lane_msg == 2 * c, top[:, c : c + 1, :], stats)
            stats = jnp.where(lane_msg == 2 * c + 1, total[:, c : c + 1, :], stats)
        k.pm_out[span, meta_row : meta_row + 1, :] = stats

    loop(groups // n_block, queue_block)

    def p_copy(i):
        g = lax.rem(me + 1 + i, groups)
        return remote(k.pm_out.at[g], k.pm_in.at[me], k.p_ss.at[i], k.p_rs.at[me], group_dev(g))

    def p_wait(i):
        g = lax.rem(me + 1 + i, groups)
        remote(k.pm_in.at[g], k.pm_in.at[g], k.p_ss.at[i], k.p_rs.at[g], dev_s).wait_recv()

    each(groups - 1, lambda i: p_copy(i).start())
    k.pm_in[me] = k.pm_out[me]
    dom_lanes = jnp.sum(k.emsg[:, meta_row : meta_row + 1, :], axis=0)
    weights = []
    for c in range(crops_dev):
        at_c = crops_dev * tp + c
        is_one = k.dom[at_c].astype(F32)
        own_total = dom_lanes[:, 0:1] * (1.0 - is_one) + dom_lanes[:, 1:2] * is_one
        is_live = jnp.where(at_c < live_n, 1.0, 0.0)
        weights.append(
            is_live * (LOSS_SCALE * crops_group * groups) / (2.0 * jnp.maximum(own_total, 1.0))
        )
    crop_weight = per_crop(weights)
    each(groups - 1, p_wait)

    tops_all, totals_all = [], []
    for c in range(crops_dev):
        tops = k.pm_in[:, meta_row : meta_row + 1, 2 * c : 2 * c + 1]
        totals = k.pm_in[:, meta_row : meta_row + 1, 2 * c + 1 : 2 * c + 2]
        top_c = jnp.max(tops, axis=0, keepdims=True)
        scale = jnp.exp(tops - top_c)
        tops_all.append(top_c[0])
        totals_all.append(jnp.sum(scale * totals, axis=0))
        for j in range(lane_blocks):
            k.pulled[c : c + 1, lanes_of(j)] = jnp.sum(
                scale * k.pm_in[:, crop_block(c, j), :], axis=0
            )
    total_all = per_crop(totals_all, 1.0)
    lse_q = per_crop(tops_all) + jnp.log(total_all)
    top_both = jnp.maximum(pos, lse_q)
    lse = top_both + jnp.log(jnp.exp(pos - top_both) + jnp.exp(lse_q - top_both))
    de = crop_weight * (
        (jnp.exp(lse_q - lse) / total_all * INV_TEMP) * k.pulled[...]
        + ((jnp.exp(pos - lse) - 1.0) * INV_TEMP) * positives
    )
    dpool = inv_norm * (
        de - pooled * (jnp.sum(pooled * de, axis=-1, keepdims=True) * inv_norm * inv_norm)
    )
    dpool = jnp.where(is_crop, dpool / crop_len, 0.0)
    k.vec[6:7, :] = jnp.sum(dpool * xs, axis=0, keepdims=True)
    k.vec[7:8, :] = jnp.sum(dpool * crop_len, axis=0, keepdims=True)

    dgain = dpool * gain_two
    dgain_mean = jnp.mean(dgain, axis=-1, keepdims=True)
    b_down_sum = zero_row
    for c in range(crops_dev):
        dg, dg_mean = dgain[c : c + 1, :], dgain_mean[c : c + 1, :]

        def norm_two_back(i, total, c=c, dg=dg, dg_mean=dg_mean):
            rows = pl.ds(pl.multiple_of(c * seq + i * 64, 64), 64)
            xh = k.r2[rows, :]
            live = sub64 + (i * 64).astype(F32) < lens[c]
            scale = jnp.where(live, k.rstd2[rows, :], 0.0)
            dr = scale * (dg - dg_mean - xh * jnp.mean(dg * xh, axis=-1, keepdims=True))
            k.r2[rows, :] = dr
            k.df[rows, :] = dr.astype(BF)
            return total + jnp.sum(dr, axis=0, keepdims=True)

        b_down_sum = lax.fori_loop(0, seq // 64, norm_two_back, b_down_sum)
    k.vec[3:4, :] = b_down_sum
    df_copy = remote(k.df, k.df_s, k.a_ss.at[7], k.a_rs.at[7], dev_s)
    df_copy.start()

    for c in range(6):
        for i in range(3):
            w_copy(c, i).wait_send()
            s_copy(c, i).wait_send()
    for i in range(3):
        for j in range(dp_n - 1):
            zd_copy(i, j).wait_send()
        bias_copy(i).wait_send()
    for i in range(4):
        act_copy(i).wait_send()
    for copy in a_copies:
        copy.wait_send()
    each(groups - 1, lambda i: e_copy(i).wait_send())
    each(groups - 1, lambda i: p_copy(i).wait_send())

    g_ref = (lambda t: k.g0.at[t], lambda t: k.act.at[t, 0:half], lambda t: k.gp.at[t, 0:half])

    def g1_copy(n, i):
        t_from = (t_a, t_d)[i]
        return remote(g_ref[n](t_from), k.r_one.at[n, i], k.g1_ss.at[n, i], k.g1_rs.at[n, i], dev_a)

    def g2_copy(n):
        return remote(g_ref[n](t_b), k.r_two.at[n], k.g2_ss.at[n], k.g2_rs.at[n], dev_b)

    def z_span(bits):
        start, size = 0, half
        for bit in range(bits):
            size //= 2
            start = start + lax.rem(dp // (1 << bit), 2) * size
        return start, size

    def z_dev(bit):
        return (tp, flip(dp, 1 << bit), dq)

    def z_rows(start, size):
        return pl.ds(pl.multiple_of(start, 16), size)

    def gz_copy(n, bit):
        start, size = z_span(bit)
        size //= 2
        away = start + (1 - lax.rem(dp // (1 << bit), 2)) * size
        offset = half - 2 * size
        return remote(
            g_ref[n](tp).at[z_rows(away, size)],
            k.z_one.at[n, pl.ds(offset, size)],
            k.gz_ss.at[n, bit],
            k.gz_rs.at[n, bit],
            z_dev(bit),
        )

    def gz_add(n, bit):
        start, size = z_span(bit + 1)
        offset = half - 2 * size
        mine = g_ref[n](tp).at[z_rows(start, size)]
        total = mine[...].astype(F32) + k.z_one[n, pl.ds(offset, size)].astype(F32)
        if bit == dp_bits - 1 and hi_bits == 0:
            k.res[n, z_rows(start, size)] = total.astype(BF)
        else:
            mine[...] = total.astype(BF)

    def gh_copy(n, bit):
        start, size = z_span(dp_bits)
        return remote(
            g_ref[n](tp).at[z_rows(start, size)],
            k.z_hi.at[n, bit],
            k.gh_ss.at[n, bit],
            k.gh_rs.at[n, bit],
            (tp, dp, flip(dq, 2 << bit)),
        )

    def ga_copy(n, bit):
        start, size = z_span(bit + 1)
        rows = k.res.at[n, z_rows(start, size)]
        return remote(rows, rows, k.ga_ss.at[n, bit], k.ga_rs.at[n, bit], z_dev(bit))

    def ga_wait(n, bit):
        start, size = z_span(bit)
        away = start + (1 - lax.rem(dp // (1 << bit), 2)) * (size // 2)
        rows = k.res.at[n, z_rows(away, size // 2)]
        remote(rows, rows, k.ga_ss.at[n, bit], k.ga_rs.at[n, bit], dev_s).wait_recv()

    spots = ((0, 0), (0, 1), (1, 0), (1, 1))

    def head_spot(j):
        row, col = spots[j]
        return slice(row * heads_w, (row + 1) * heads_w), slice(col * half, (col + 1) * half)

    def final_parts(n, cols):
        if n == 0:
            return [(k.res.at[0], k.gd_out.at[cols])]
        if n == 1:
            return [
                (k.res.at[1, :, h * half : (h + 1) * half], k.gu_out.at[h * half : (h + 1) * half, cols])
                for h in range(2)
            ]
        return [(k.res.at[2, head_spot(j)[0], head_spot(j)[1]], k.gh_out.at[j, :, cols]) for j in range(4)]

    def final_copies(n):
        first = (0, 1, 3)[n]
        away, here = [], []
        for i, (src, dst) in enumerate(final_parts(n, own_half)):
            away.append(remote(src, dst, k.gf_ss.at[first + i], k.gf_rs.at[first + i], dev_s))
            here.append(pltpu.make_async_copy(src, dst, k.out_sem.at[first + i]))
        return away, here

    def final_arrived(n):
        first = (0, 1, 3)[n]
        for i, (_, dst) in enumerate(final_parts(n, other_half)):
            remote(dst, dst, k.gf_ss.at[first + i], k.gf_rs.at[first + i], dev_s).wait_recv()

    def add_rows(dst, srcs):
        def step(i):
            rows = at(i, 64)
            total = dst[rows, :].astype(F32)
            for src in srcs:
                total = total + src[rows, :].astype(F32)
            dst[rows, :] = total.astype(BF)

        loop(half // 64, step)

    def plane_second(n):
        g1_copy(n, 1).wait_recv()
        add_rows(g_ref[n](t_b), [k.r_one.at[n, 1]])
        g2_copy(n).start()

    def plane_done(n):
        g1_copy(n, 0).wait_recv()
        g2_copy(n).wait_recv()
        add_rows(g_ref[n](tp), [k.r_one.at[n, 0], k.r_two.at[n]])
        gz_copy(n, 0).start()

    def z_step(n, bit):
        gz_copy(n, bit).wait()
        gz_add(n, bit)
        if bit + 1 < dp_bits:
            gz_copy(n, bit + 1).start()
            return
        for b in range(hi_bits):
            gh_copy(n, b).start()
            gh_copy(n, b).wait()
            start, size = z_span(dp_bits)
            mine = g_ref[n](tp).at[z_rows(start, size)]
            total = (mine[...].astype(F32) + k.z_hi[n, b].astype(F32)).astype(BF)
            if b == hi_bits - 1:
                k.res[n, z_rows(start, size)] = total
            else:
                mine[...] = total
        ga_copy(n, dp_bits - 1).start()

    def z_back(n, bit):
        ga_wait(n, bit)
        if bit > 0:
            ga_copy(n, bit - 1).start()
        else:
            for copies in final_copies(n):
                for copy in copies:
                    copy.start()

    def du_copy(t, i):
        return remote(
            k.du.at[t, :, other_half], k.du_s.at[t], k.a_ss.at[8 + i], k.a_rs.at[8 + t], dev_s
        )

    def du_arrived(t):
        remote(k.du_s.at[t], k.du_s.at[t], k.a_ss.at[8], k.a_rs.at[8 + t], dev_s).wait_recv()

    def hidden_back(t, i):
        def tile(j):
            cols = at(j, 256)
            da = dot_nt(k.df[...], k.wd[t, cols, :])
            d = (da * k.gp[t, :, cols].astype(F32)).astype(BF)
            k.du[t, :, cols] = d
            k.vec[pl.ds(8 + t, 1), cols] = jnp.sum(d.astype(F32), axis=0, keepdims=True)

        loop(lane_blocks, tile)
        du_copy(t, i).start()

    def down_piece(t):
        k.g0[t] = (
            dot_tn(k.act[t, :, own_half], k.df[...]) + dot_tn(k.act_s[t], k.df_s[...])
        ).astype(BF)

    def up_piece(t):
        du_arrived(t)
        for h in range(2):
            rows = slice(h * half, (h + 1) * half)
            k.act[t, 0:half, rows] = (
                dot_tn(k.h1b[:, rows], k.du[t, :, own_half]) + dot_tn(k.h1_s[:, rows], k.du_s[t])
            ).astype(BF)

    hidden_back(t_d, 0)
    df_copy.wait()
    for t in range(tp_n):
        remote(k.act_s.at[t], k.act_s.at[t], k.a_ss.at[3], k.a_rs.at[3 + t], dev_s).wait_recv()
    down_piece(t_d)
    g1_copy(0, 1).start()
    down_piece(t_a)
    g1_copy(0, 0).start()
    hidden_back(t_a, 1)
    down_piece(t_b)
    hidden_back(t_b, 2)
    down_piece(tp)
    hidden_back(tp, 3)
    a_copies[2].wait_recv()
    up_piece(t_d)
    g1_copy(1, 1).start()
    plane_second(0)
    up_piece(t_a)
    g1_copy(1, 0).start()
    up_piece(t_b)
    up_piece(tp)

    def hidden_grad(i):
        cols = at(i, 256)
        total = k.r2[:, cols]
        for t in range(tp_n):
            total = total + dot_nt(k.du[t], k.wu[t, cols, :])
        k.r2[:, cols] = total

    loop(lane_blocks, hidden_grad)

    def norm_one_back(i, sums):
        rows = at(i, 64)
        dh, xh = k.r2[rows, :], k.xh1[rows, :]
        dxh = dh * gain_one
        dr = k.rstd1[rows, :] * (
            dxh
            - jnp.mean(dxh, axis=-1, keepdims=True)
            - xh * jnp.mean(dxh * xh, axis=-1, keepdims=True)
        )
        k.r2[rows, :] = dr
        k.do[rows, :] = dr.astype(BF)
        return (
            sums[0] + jnp.sum(dr, axis=0, keepdims=True),
            sums[1] + jnp.sum(dh * xh, axis=0, keepdims=True),
            sums[2] + jnp.sum(dh, axis=0, keepdims=True),
        )

    out_sum, gain_sum, shift_sum = lax.fori_loop(
        0, tokens // 64, norm_one_back, (zero_row, zero_row, zero_row)
    )
    k.vec[2:3, :] = out_sum
    k.vec[4:5, :] = gain_sum
    k.vec[5:6, :] = shift_sum
    do_copy = remote(k.do.at[:, other_half], k.do_s, k.a_ss.at[12], k.a_rs.at[12], dev_s)
    do_copy.start()

    def grad_lanes(c, lanes):
        return slice(c * slot + lanes.start, c * slot + lanes.stop)

    def attend_back(t, crop):
        rows = slice(crop * seq, (crop + 1) * seq)
        dctx_all = dot_nt(k.do[rows, :], k.wo[t_rows(t), :]).astype(BF)
        dqs, dks, dvs = [], [], []
        for h, (lanes, side) in enumerate(views):
            q, key, val = (k.qkv[c, t, rows, lanes] for c in range(3))
            dctx = dctx_all[:, lanes]
            p = k.prob[(crop * tp_n + t) * heads_t + h]
            pf = p.astype(F32)
            dprob = dot_nt(masked(dctx, side), val)
            ds = (pf * (dprob - jnp.sum(dprob * pf, axis=-1, keepdims=True))).astype(BF)
            dvs.append(dot_tn(p, dctx))
            dqs.append(dot_nn(ds, key) * 0.125)
            dks.append(dot_tn(ds, q))
        for c, outs in enumerate((dqs, dks, dvs)):

            def store(lanes, value, c=c):
                k.wd[t, rows, grad_lanes(c, lanes)] = value.astype(BF)

            merged(outs, store)

    def dqkv_copy(t, i):
        return remote(
            k.wd.at[t, 0:tokens], k.dqkv_s.at[t], k.a_ss.at[13 + i], k.a_rs.at[13 + t], dev_s
        )

    def dqkv_arrived(t):
        there = k.dqkv_s.at[t]
        remote(there, there, k.a_ss.at[13], k.a_rs.at[13 + t], dev_s).wait_recv()

    def attention_back(t, i):
        for crop in range(crops_dev):
            attend_back(t, crop)
        dqkv_copy(t, i).start()

    heads_lanes = slice(0, heads_w)

    def out_piece(t):
        rows, lanes = head_spot(3)
        k.gp[t, rows, lanes] = (
            dot_tn(k.ctx[t], k.do[:, own_half]) + dot_tn(k.ctx_s[t], k.do_s[...])
        ).astype(BF)

    def head_piece(t):
        dqkv_arrived(t)
        for c in range(3):
            rows, lanes = head_spot(c)
            cols = grad_lanes(c, heads_lanes)
            k.gp[t, rows, lanes] = (
                dot_tn(k.wd[t, 0:tokens, cols], k.xb[:, own_half])
                + dot_tn(k.dqkv_s[t, :, cols], k.x_s[...])
            ).astype(BF)

    def input_grad(i):
        cols = at(i, 256)
        total = k.r2[:, cols]
        for t in range(tp_n):
            for c in range(3):
                total = total + dot_nn(
                    k.wd[t, 0:tokens, grad_lanes(c, heads_lanes)],
                    k.wqkv[c, t * heads_w : (t + 1) * heads_w, cols],
                )
        k.do[:, cols] = total.astype(BF)

    def dx_rows(t):
        return k.dx_out.at[at(t, tokens)]

    def dx_copy(i):
        if i < 2:
            return remote(k.do, dx_rows(tp), k.x_ss.at[i], k.x_rs.at[i], (dev_a, dev_b)[i])
        return remote(dx_rows(t_a), dx_rows(t_a), k.x_ss.at[2], k.x_rs.at[2], dev_b)

    def dx_arrived(i):
        there = dx_rows(others[i])
        remote(there, there, k.x_ss.at[i], k.x_rs.at[i], dev_a).wait_recv()

    def v_sibling():
        return remote(k.vec, k.v_hi.at[0], k.v_ss.at[0], k.v_rs.at[0], dev_s)

    def v_plane(i):
        mine = k.v_plane.at[tp]
        return remote(
            mine, mine, k.v_ss.at[1 + i], k.v_rs.at[1 + i], ((t_x, t_y, t_d)[i], dp, dq)
        )

    def v_plane_arrived(i):
        there = k.v_plane.at[(t_x, t_y, t_d)[i]]
        remote(there, there, k.v_ss.at[1 + i], k.v_rs.at[1 + i], dev_s).wait_recv()

    def v_planes(j):
        mine = k.v_z.at[dp]
        return remote(
            mine, mine, k.v_ss.at[4 + j], k.v_rs.at[4 + dp], (tp, lax.rem(dp + 1 + j, dp_n), dq)
        )

    def v_planes_arrived(j):
        z = lax.rem(dp + 1 + j, dp_n)
        there = k.v_z.at[z]
        remote(there, there, k.v_ss.at[4 + j], k.v_rs.at[4 + z], dev_s).wait_recv()

    def v_group(bit):
        at_ = 4 + dp_n + bit
        return remote(
            k.v_hi.at[1 + 2 * bit],
            k.v_hi.at[2 + 2 * bit],
            k.v_ss.at[at_],
            k.v_rs.at[at_],
            (tp, dp, flip(dq, 2 << bit)),
        )

    attention_back(t_d, 0)
    do_copy.wait()
    a_copies[0].wait_recv()
    a_copies[1].wait_recv()
    out_piece(t_d)
    out_piece(t_a)
    attention_back(t_a, 1)
    plane_done(0)
    head_piece(t_d)
    g1_copy(2, 1).start()
    attention_back(t_b, 2)
    head_piece(t_a)
    g1_copy(2, 0).start()
    plane_second(1)
    attention_back(tp, 3)
    z_step(0, 0)
    out_piece(t_b)
    out_piece(tp)
    head_piece(t_b)
    head_piece(tp)
    for t in range(tp_n):
        for c, lanes in ((0, slice(0, heads_w)), (2, slice(slot, slot + heads_w))):
            grads = k.wd[t, 0:tokens, grad_lanes(c, heads_lanes)].astype(F32)
            k.vec[12 + t : 13 + t, lanes] = jnp.sum(grads, axis=0, keepdims=True)
    v_sibling().start()
    loop(lane_blocks, input_grad)
    dx_local = pltpu.make_async_copy(k.do, dx_rows(tp), k.out_sem.at[7])
    dx_local.start()
    v_sibling().wait()
    k.v_plane[tp] = k.vec[...] + k.v_hi[0]
    for i in range(3):
        v_plane(i).start()
    for bit in range(1, dp_bits):
        z_step(0, bit)
    plane_done(1)
    z_back(0, dp_bits - 1)
    plane_second(2)
    dx_copy(0).start()
    dx_copy(1).start()
    z_step(1, 0)
    for bit in range(dp_bits - 2, -1, -1):
        z_back(0, bit)
    for bit in range(1, dp_bits):
        z_step(1, bit)
    for i in range(3):
        v_plane_arrived(i)
    v_sum = k.v_plane[0]
    for t in range(1, tp_n):
        v_sum = v_sum + k.v_plane[t]
    k.v_z[dp] = v_sum
    plane_done(2)
    for j in range(dp_n - 1):
        v_planes(j).start()
    z_back(1, dp_bits - 1)
    z_step(2, 0)
    dx_arrived(0)
    dx_copy(2).start()
    for bit in range(dp_bits - 2, -1, -1):
        z_back(1, bit)
    for bit in range(1, dp_bits):
        z_step(2, bit)
    for j in range(dp_n - 1):
        v_planes_arrived(j)
    v_all = k.v_z[0]
    for z in range(1, dp_n):
        v_all = v_all + k.v_z[z]
    for bit in range(hi_bits):
        k.v_hi[1 + 2 * bit] = v_all
        v_group(bit).start()
        v_group(bit).wait_recv()
        v_all = v_all + k.v_hi[2 + 2 * bit]
    k.vec_out[...] = v_all
    for bit in range(dp_bits - 1, -1, -1):
        z_back(2, bit)

    dx_arrived(1)
    dx_arrived(2)
    for i in range(3):
        dx_copy(i).wait_send()
        v_plane(i).wait_send()
    for j in range(dp_n - 1):
        v_planes(j).wait_send()
    for bit in range(hi_bits):
        v_group(bit).wait_send()
    for i, t in enumerate((t_d, t_a, t_b, tp)):
        du_copy(t, i).wait_send()
        dqkv_copy(t, i).wait_send()
    dx_local.wait()
    for n in range(3):
        final_arrived(n)
        away, here = final_copies(n)
        for copy in away:
            copy.wait_send()
        for copy in here:
            copy.wait()
        for i in range(2):
            g1_copy(n, i).wait_send()
        g2_copy(n).wait_send()
        for bit in range(dp_bits):
            ga_copy(n, bit).wait_send()


def run_layer(mesh_sizes, args):
    tp_n, dp_n, dq_n = mesh_sizes
    ids, x_in = args[0], args[13]
    width = x_in.shape[1]
    crops_dev = ids.shape[0] // tp_n
    tokens = x_in.shape[0] // tp_n
    seq = tokens // crops_dev
    groups = dp_n * dq_n
    half = width // 2
    heads_w = width // tp_n
    dp_bits = dp_n.bit_length() - 1
    hi_bits = (dq_n // 2).bit_length() - 1
    heads = width // HD
    smem = pl.BlockSpec(memory_space=pltpu.SMEM)
    vmem = pl.BlockSpec(memory_space=pltpu.VMEM)
    hbm = pl.BlockSpec(memory_space=pl.ANY)
    dma = pltpu.SemaphoreType.DMA

    def b16(*shape):
        return pltpu.VMEM(shape, BF)

    def f32(*shape):
        return pltpu.VMEM(shape, F32)

    scratch = [
        b16(3, width, width),
        b16(width, width),
        b16(tp_n, width, width),
        b16(tp_n, width, width),
        b16(tokens, width),
        b16(3, tp_n, tokens, heads_w),
        b16(crops_dev * heads, seq, seq),
        b16(tp_n, tokens, heads_w),
        f32(tokens, width),
        f32(tokens, 1),
        b16(tokens, width),
        b16(tp_n, tokens, width),
        b16(tp_n, tokens, width),
        f32(tokens, width),
        f32(tokens, 1),
        b16(tokens, half),
        b16(tp_n, tokens, heads_w),
        b16(tokens, width),
        b16(tp_n, tokens, half),
        b16(tokens, width),
        b16(tp_n, tokens, half),
        b16(tokens, half),
        b16(tp_n, tokens, width),
        b16(tokens, width),
        b16(tp_n, tokens, width),
        b16(tokens, width),
        b16(tp_n, half, width),
        b16(3, 2, half, width),
        b16(3, half, width),
        b16(3, half - half // dp_n, width),
        b16(3, max(hi_bits, 1), half // dp_n, width),
        b16(3, half, width),
        f32(tp_n, 8, width),
        f32(groups, 8, 256),
        f32(groups, 8, width),
        f32(64, tp_n * tokens),
        b16(128, tp_n * tokens),
        f32(groups, 8, 256),
        f32(groups, 8, 256),
        f32(8, width),
        f32(ids.shape[0], width),
        f32(8, width),
        f32(16, width),
        f32(tp_n, 16, width),
        f32(dp_n, 16, width),
        f32(1 + 2 * hi_bits, 16, width),
        dma((7 + tp_n,)),
        dma((6, 3)),
        dma((6, 3)),
        dma((6, 3)),
        dma((6, 3)),
        dma((3, dp_n)),
        dma((3, dp_n)),
        dma((3,)),
        dma((3,)),
        dma((17,)),
        dma((17,)),
        dma((groups,)),
        dma((groups,)),
        dma((groups,)),
        dma((groups,)),
        dma((3, 2)),
        dma((3, 2)),
        dma((3,)),
        dma((3,)),
        dma((3, dp_bits)),
        dma((3, dp_bits)),
        dma((3, dp_bits)),
        dma((3, dp_bits)),
        dma((3, max(hi_bits, 1))),
        dma((3, max(hi_bits, 1))),
        dma((7,)),
        dma((7,)),
        dma((3,)),
        dma((3,)),
        dma((4 + dp_n + hi_bits,)),
        dma((4 + dp_n + hi_bits,)),
        dma((8,)),
    ]
    return pl.pallas_call(
        functools.partial(layer_kernel, (tp_n, dp_n, dq_n, crops_dev, seq, width)),
        out_shape=(
            jax.ShapeDtypeStruct((width, width), BF),
            jax.ShapeDtypeStruct((width, width), BF),
            jax.ShapeDtypeStruct((4, heads_w, width), BF),
            jax.ShapeDtypeStruct((tp_n * tokens, width), BF),
            jax.ShapeDtypeStruct((16, width), F32),
        ),
        in_specs=[vmem, smem, smem] + [vmem] * 10 + [hbm] * 8,
        out_specs=(hbm, hbm, hbm, hbm, vmem),
        scratch_shapes=scratch,
        compiler_params=pltpu.CompilerParams(
            collective_id=0, has_side_effects=True, vmem_limit_bytes=63 * 2**20
        ),
    )(*args)


def widen_kernel(gd, gu, gh, dx, gd_o, gu_o, gq_o, gk_o, gv_o, go_o, dx_o):
    gd_o[...] = gd[...].astype(F32)
    gu_o[...] = gu[...].astype(F32)
    dx_o[...] = dx[...].astype(F32)
    for c, out in enumerate((gq_o, gk_o, gv_o, go_o)):
        out[...] = gh[c].astype(F32)


def widen(gd, gu, gh, dx):
    width, tokens, heads_w = gd.shape[0], dx.shape[0], gh.shape[1]
    steps = 8
    row_steps = heads_w // 48
    rows = pl.BlockSpec((width // steps, width), lambda i: (i, 0))
    out = pl.BlockSpec((48, width), lambda i: (jnp.minimum(i, row_steps - 1), 0))
    tokens_spec = pl.BlockSpec((tokens // steps, width), lambda i: (i, 0))
    return pl.pallas_call(
        widen_kernel,
        grid=(steps,),
        out_shape=(
            jax.ShapeDtypeStruct((width, width), F32),
            jax.ShapeDtypeStruct((width, width), F32),
            jax.ShapeDtypeStruct((heads_w, width), F32),
            jax.ShapeDtypeStruct((heads_w, width), F32),
            jax.ShapeDtypeStruct((heads_w, width), F32),
            jax.ShapeDtypeStruct((heads_w, width), F32),
            jax.ShapeDtypeStruct((tokens, width), F32),
        ),
        in_specs=[
            rows,
            rows,
            pl.BlockSpec((4, 48, width), lambda i: (0, jnp.minimum(i, row_steps - 1), 0)),
            tokens_spec,
        ],
        out_specs=(rows, rows, out, out, out, out, tokens_spec),
    )(gd, gu, gh, dx)


def body(
    mesh_sizes,
    inputs,
    token_ids,
    crop_counts,
    domain_ids,
    positives,
    distractor_buffer,
    w_query,
    b_query,
    w_key,
    w_value,
    b_value,
    w_out,
    b_out,
    gain_one,
    shift_one,
    w_up,
    b_up,
    w_down,
    b_down,
    gain_two,
    shift_two,
):
    tp = lax.axis_index("tp")
    heads_w = w_query.shape[1]
    slot = (heads_w + 127) // 128 * 128
    gd, gu, gh, dx, vec = run_layer(
        mesh_sizes,
        (
            token_ids,
            domain_ids,
            crop_counts,
            positives,
            b_query,
            b_value,
            b_up,
            b_out,
            gain_one,
            shift_one,
            b_down,
            gain_two,
            shift_two,
            inputs,
            w_query.T,
            w_key.T,
            w_value.T,
            w_out,
            w_up,
            w_down,
            distractor_buffer,
        ),
    )
    grad_w_down, grad_w_up, grad_w_query, grad_w_key, grad_w_value, grad_w_out, grad_inputs = widen(
        gd, gu, gh, dx
    )
    own_up = lax.dynamic_slice_in_dim(vec, 8 + tp, 1)[0]
    own_heads = lax.dynamic_slice_in_dim(vec, 12 + tp, 1)[0]
    return (
        grad_inputs,
        grad_w_query.T,
        own_heads[0:heads_w],
        grad_w_key.T,
        grad_w_value.T,
        own_heads[slot : slot + heads_w],
        grad_w_out,
        vec[2],
        vec[4],
        vec[5],
        grad_w_up,
        own_up,
        grad_w_down,
        vec[3],
        vec[6],
        vec[7],
    )


def solution(mesh):
    mesh_sizes = (mesh.shape["tp"], mesh.shape["dp"], mesh.shape["dq"])
    rows = P(("dp", "dq"), None)
    groups = P(("dp", "dq"))
    return jax.shard_map(
        functools.partial(body, mesh_sizes),
        mesh=mesh,
        in_specs=(
            rows,
            rows,
            groups,
            groups,
            rows,
            rows,
            P(None, "tp"),
            P("tp"),
            P(None, "tp"),
            P(None, "tp"),
            P("tp"),
            P("tp", None),
            P(),
            P(),
            P(),
            P(None, "tp"),
            P("tp"),
            P("tp", None),
            P(),
            P(),
            P(),
        ),
        out_specs=(
            rows,
            P(None, "tp"),
            P("tp"),
            P(None, "tp"),
            P(None, "tp"),
            P("tp"),
            P("tp", None),
            P(),
            P(),
            P(),
            P(None, "tp"),
            P("tp"),
            P("tp", None),
            P(),
            P(),
            P(),
        ),
        check_vma=False,
    )
```

```python
import functools

import jax
import jax.numpy as jnp
from jax import lax
from jax.experimental import pallas as pl
from jax.experimental.pallas import tpu as pltpu
from jax.sharding import PartitionSpec as P

HD = 64
LN_EPS = 1e-12
INV_TEMP = 1.0 / 0.05
LOSS_SCALE = 128.0
MASKED = -1000000000.0
BF = jnp.bfloat16
F32 = jnp.float32
MESH = pl.DeviceIdType.MESH


BACKWARD_ORDER = (
    "HBb", "DPd0", "DPd1", "HBp", "HBa", "DPb1", "DPa0", "DPb0", "P1_D0", "HBd", "HG", "P1_D1",
    "UPd1", "DPa1", "L1B", "DPp0", "P2_D0", "ABp0", "DPp1", "UPa1", "ABd0", "UPb0", "Z0_D0",
    "UPb1", "ABd1", "P1_U1", "P2_D1", "ABa0", "UPd0", "Z1_D0", "ABp1", "UPp1", "UPa0", "P2_U1",
    "Z0_D1", "HQd", "P1_U0", "ABb0", "A1_D0", "OPd", "ABa1", "Z0_U1", "OPp", "UPp0", "HVd",
    "Z1_D1", "ABb1", "P2_U0", "HQp", "OPb", "HQa", "OPa", "A0_D0", "Z1_U1", "HQb", "A1_D1",
    "P1_H0", "HVb", "P1_H1", "IG", "Z0_U0", "HVp", "VS", "P2_H0", "HVa", "F_D0", "Z1_U0",
    "P2_H1", "DX", "Z0_H0", "A1_U0", "Z0_H1", "Z1_H0", "A1_U1", "Z1_H1", "V1", "A1_H0", "A0_U1",
    "DXF", "A1_H1", "A0_U0", "F_U1", "V2", "A0_D1", "A0_H0", "F_U0", "A0_H1", "DXL", "F_H0",
    "F_D1", "F_H1", "V3",
)


def dot_nn(left, right):
    return lax.dot_general(left, right, (((1,), (0,)), ((), ())), preferred_element_type=F32)


def dot_nt(left, right):
    return lax.dot_general(left, right, (((1,), (1,)), ((), ())), preferred_element_type=F32)


def dot_tn(left, right):
    return lax.dot_general(left, right, (((0,), (0,)), ((), ())), preferred_element_type=F32)


def loop(count, step):
    def run(i, carry):
        step(i)
        return carry

    lax.fori_loop(0, count, run, 0)


def each(count, step):
    def run(i, carry):
        step(i)
        return carry

    lax.fori_loop(0, count, run, 0)


def at(index, size):
    return pl.ds(pl.multiple_of(index * size, size), size)


def remote(src, dst, send_sem, recv_sem, device):
    return pltpu.make_async_remote_copy(
        src_ref=src,
        dst_ref=dst,
        send_sem=send_sem,
        recv_sem=recv_sem,
        device_id=device,
        device_id_type=MESH,
    )


def flip(index, bit):
    return index + bit - 2 * bit * lax.rem(index // bit, 2)


def halvings_of(width, dp_n):
    count, rows = 0, width // 4
    while 2 << count <= dp_n and rows // 2 % 16 == 0:
        count, rows = count + 1, rows // 2
    return count


def layer_kernel(sizes, *refs):
    tp_n, dp_n, dq_n, crops_dev, seq, width = sizes
    names = (
        "ids", "dom", "cnt", "pos_in", "b_q", "b_v", "b_up", "b_out", "gain1", "shift1", "b_down",
        "gain2", "shift2", "x_in", "wq_in", "wk_in", "wv_in", "wo_in", "wu_in", "wd_in", "queue_in",
        "gd_out", "gu_out", "gh_out", "dx_out", "vec_out",
        "wqkv", "wo", "wu", "wd", "xb", "qkv", "prob", "ctx", "xh1", "rstd1", "h1b", "act", "gp",
        "r2", "rstd2",
        "x_s", "ctx_s", "h1_s", "act_s", "df_s", "du_s", "do_s", "dqkv_s",
        "df", "du", "do", "g0", "r_one", "r_two", "z_one", "z_hi", "res",
        "bb", "emsg", "es", "neg", "shares", "pm_out", "pm_in", "xs", "posf", "pulled",
        "vec", "v_plane", "v_z", "v_hi",
        "loc", "w_ss", "w_rs", "s_ss", "s_rs", "zd_ss", "zd_rs", "b_ss", "b_rs",
        "a_ss", "a_rs", "e_ss", "e_rs", "p_ss", "p_rs",
        "g1_ss", "g1_rs", "g2_ss", "g2_rs", "gz_ss", "gz_rs", "ga_ss", "ga_rs", "gh_ss", "gh_rs",
        "gf_ss", "gf_rs", "x_ss", "x_rs", "v_ss", "v_rs", "out_sem",
    )

    class Refs:
        pass

    k = Refs()
    for name, ref in zip(names, refs, strict=True):
        setattr(k, name, ref)

    tokens = crops_dev * seq
    groups = dp_n * dq_n
    dp_bits = dp_n.bit_length() - 1
    hi_bits = (dq_n // 2).bit_length() - 1
    heads_w = width // tp_n
    heads_t = heads_w // HD
    slot = (heads_w + 127) // 128 * 128
    half = width // 2
    head_half = heads_w // 2
    quarter = half // dp_n
    lane_blocks = width // 256
    halvings = halvings_of(width, dp_n)

    tp, dp, dq = lax.axis_index("tp"), lax.axis_index("dp"), lax.axis_index("dq")
    core = lax.rem(dq, 2)
    t_x = tp + 1 - 2 * lax.rem(tp, 2)
    t_y = lax.rem(tp + 2, 4)
    t_d = 3 - tp
    t_a = t_x + core * (t_y - t_x)
    t_b = t_x + t_y - t_a
    me = dp * dq_n + dq
    dev_a = (t_a, dp, dq)
    dev_b = (t_b, dp, dq)
    dev_s = (tp, dp, dq + 1 - 2 * core)
    others = (t_a, t_b, t_d)

    def group_dev(g):
        return (tp, g // dq_n, lax.rem(g, dq_n))

    own_half = at(core, half)
    other_half = at(1 - core, half)

    barrier = pltpu.get_barrier_semaphore()
    for t_peer in (t_x, t_y, t_d):
        pl.semaphore_signal(barrier, inc=1, device_id=(t_peer, dp, dq), device_id_type=MESH)

    def greet(i):
        pl.semaphore_signal(
            barrier, inc=1, device_id=group_dev(lax.rem(me + i + 1, groups)), device_id_type=MESH
        )

    each(groups - 1, greet)

    def t_rows(t):
        return at(t, heads_w)

    locals_ = [(k.x_in.at[at(tp, tokens)], k.xb)]
    heads_in = (k.wq_in, k.wk_in, k.wv_in)
    locals_ += [(heads_in[c], k.wqkv.at[c, t_rows(tp)]) for c in range(3)]
    locals_ += [(k.wo_in, k.wo.at[t_rows(tp)]), (k.wu_in, k.wu.at[tp]), (k.wd_in, k.wd.at[tp])]
    locals_ += [(k.queue_in.at[pl.ds(j * tokens, tokens)], k.du.at[j]) for j in range(tp_n)]
    local = [pltpu.make_async_copy(src, dst, k.loc.at[i]) for i, (src, dst) in enumerate(locals_)]
    for copy in local:
        copy.start()
    k.bb[tp] = jnp.zeros((8, width), F32)
    k.bb[tp, 0:1, :] = k.b_up[...][None, :]
    k.bb[tp, 1:2, 0:heads_w] = k.b_q[...][None, :]
    k.bb[tp, 2:3, 0:heads_w] = k.b_v[...][None, :]
    k.es[...] = jnp.zeros_like(k.es)
    k.pulled[...] = jnp.zeros_like(k.pulled)
    k.xs[...] = jnp.zeros_like(k.xs)
    k.vec[...] = jnp.zeros_like(k.vec)
    pl.semaphore_wait(barrier, 3 + groups - 1)

    def part(c, t, h):
        if c < 3:
            return k.wqkv.at[c, pl.ds(pl.multiple_of(t * heads_w + h * head_half, 32), head_half)]
        if c == 3:
            return k.wo.at[pl.ds(pl.multiple_of(t * heads_w + h * head_half, 32), head_half)]
        if c == 4:
            return k.wu.at[t, at(h, half)]
        return k.wd.at[t, pl.ds(pl.multiple_of(h * half + dp * quarter, 16), quarter)]

    def source(c):
        if c < 3:
            return heads_in[c].at[at(core, head_half)]
        if c == 3:
            return k.wo_in.at[at(core, head_half)]
        if c == 4:
            return k.wu_in.at[at(core, half)]
        return k.wd_in.at[pl.ds(pl.multiple_of(core * half + dp * quarter, 16), quarter)]

    def w_copy(c, i):
        if i < 2:
            return remote(
                source(c), part(c, tp, core), k.w_ss.at[c, i], k.w_rs.at[c, i], (dev_a, dev_b)[i]
            )
        there = part(c, t_a, core)
        return remote(there, there, k.w_ss.at[c, 2], k.w_rs.at[c, 2], dev_b)

    def w_arrived(c, i):
        there = part(c, others[i], core)
        remote(there, there, k.w_ss.at[c, i], k.w_rs.at[c, i], dev_a).wait_recv()

    def s_part(c, t, h):
        return k.wd.at[t, at(h, half)] if c == 5 else part(c, t, h)

    def s_copy(c, i):
        there = s_part(c, others[i], core)
        return remote(there, there, k.s_ss.at[c, i], k.s_rs.at[c, i], dev_s)

    def s_arrived(c, t, i):
        there = s_part(c, t, 1 - core)
        remote(there, there, k.s_ss.at[c, i], k.s_rs.at[c, i], dev_s).wait_recv()

    def from_a(c):
        s_arrived(c, t_a, 1)

    def from_b(c):
        s_arrived(c, t_b, 0)

    def from_d(c):
        s_arrived(c, t_d, 2)

    def zd_copy(i, j):
        there = part(5, others[i], core)
        return remote(
            there,
            there,
            k.zd_ss.at[i, j],
            k.zd_rs.at[i, dp],
            (tp, lax.rem(dp + 1 + j, dp_n), dq),
        )

    def zd_arrived(i, j):
        z = lax.rem(dp + 1 + j, dp_n)
        there = k.wd.at[others[i], pl.ds(pl.multiple_of(core * half + z * quarter, 16), quarter)]
        remote(there, there, k.zd_ss.at[i, j], k.zd_rs.at[i, z], dev_s).wait_recv()

    def send_own(c):
        w_copy(c, 0).start()
        w_copy(c, 1).start()

    def pass_on(c):
        w_arrived(c, 0)
        w_copy(c, 2).start()
        if c < 5:
            s_copy(c, 0).start()
        w_arrived(c, 1)
        if c < 5:
            s_copy(c, 1).start()

    def last_on(c):
        w_arrived(c, 2)
        s_copy(c, 2).start()

    def send_planes(i):
        for j in range(dp_n - 1):
            zd_copy(i, j).start()

    def bias_copy(i):
        mine = k.bb.at[tp]
        return remote(mine, mine, k.b_ss.at[i], k.b_rs.at[i], ((t_x, t_y, t_d)[i], dp, dq))

    def bias_arrived(i):
        there = k.bb.at[(t_x, t_y, t_d)[i]]
        remote(there, there, k.b_ss.at[i], k.b_rs.at[i], dev_s).wait_recv()

    first_head = lax.broadcasted_iota(jnp.int32, (seq, 2 * HD), 1) < HD

    def project(t):
        for c in range(3):
            out = dot_nt(k.xb[...], k.wqkv[c, t_rows(t), :])
            if c != 1:
                row = 1 if c == 0 else 2
                out = out + k.bb[t, row : row + 1, 0:heads_w]
            out = out.astype(BF)
            k.qkv[c, t] = out * BF(0.125) if c == 0 else out

    def head_views(block):
        views = []
        for h in range(heads_t):
            base = h // 2 * 2 * HD
            if h == heads_t - 1 and heads_t % 2:
                views.append((slice(base, base + HD), None))
            else:
                views.append((slice(base, base + 2 * HD), h % 2))
        return views

    views = head_views(heads_w)

    def masked(value, side):
        if side is None:
            return value
        keep = first_head if side == 0 else ~first_head
        return jnp.where(keep, value, jnp.zeros_like(value))

    def merged(outs, store):
        for h, (lanes, side) in enumerate(views):
            if side is None:
                store(lanes, outs[h])
            elif side == 1:
                store(lanes, jnp.where(first_head, outs[h - 1], outs[h]))

    def attend(t, crop):
        rows = slice(crop * seq, (crop + 1) * seq)
        ids = jnp.broadcast_to(k.ids[pl.ds(crops_dev * tp + crop, 1), :], (seq, seq))
        outs = []
        for h, (lanes, side) in enumerate(views):
            s = dot_nt(masked(k.qkv[0, t, rows, lanes], side), k.qkv[1, t, rows, lanes])
            s = jnp.where(ids != 0, s, MASKED)
            e = jnp.exp(s - jnp.max(s, axis=-1, keepdims=True))
            p = (e * (1.0 / jnp.sum(e, axis=-1, keepdims=True))).astype(BF)
            k.prob[(crop * tp_n + t) * heads_t + h] = p
            outs.append(dot_nn(p, k.qkv[2, t, rows, lanes]))

        def store(lanes, value):
            k.ctx[t, rows, lanes] = value.astype(BF)

        merged(outs, store)

    def attention(t):
        project(t)
        for crop in range(crops_dev):
            attend(t, crop)

    send_own(5)
    send_own(0)
    send_own(1)
    for i in range(3):
        bias_copy(i).start()
    for copy in local[0:4]:
        copy.wait()
    a_copies = [
        remote(k.xb.at[:, other_half], k.x_s, k.a_ss.at[0], k.a_rs.at[0], dev_s),
        remote(k.ctx, k.ctx_s, k.a_ss.at[1], k.a_rs.at[1], dev_s),
        remote(k.h1b, k.h1_s, k.a_ss.at[2], k.a_rs.at[2], dev_s),
    ]
    a_copies[0].start()
    project(tp)
    pass_on(5)
    send_planes(0)
    send_planes(1)
    send_own(2)
    send_own(3)
    attend(tp, 0)
    pass_on(0)
    for crop in range(1, crops_dev):
        attend(tp, crop)
    pass_on(1)
    w_arrived(5, 2)
    send_planes(2)
    pass_on(2)
    pass_on(3)
    send_own(4)
    for i in range(3):
        bias_arrived(i)
    for c in range(3):
        from_a(c)
    attention(t_a)
    last_on(0)
    for c in range(3):
        from_b(c)
    attention(t_b)
    last_on(1)
    last_on(2)
    last_on(3)
    for c in range(3):
        from_d(c)
    attention(t_d)
    a_copies[1].start()

    local[4].wait()
    from_a(3)
    from_b(3)
    from_d(3)

    def attn_out(i):
        rows = at(i, 256)
        total = k.xb[rows, :].astype(F32) + k.b_out[...][None, :]
        for t in range(tp_n):
            total = total + dot_nn(k.ctx[t, rows, :], k.wo[t * heads_w : (t + 1) * heads_w, :])
        k.r2[rows, :] = total

    loop(tokens // 256, attn_out)

    def norm(v):
        centered = v - jnp.mean(v, axis=-1, keepdims=True)
        rstd = lax.rsqrt(jnp.mean(centered * centered, axis=-1, keepdims=True) + LN_EPS)
        return centered * rstd, rstd

    gain_one = k.gain1[...][None, :]
    shift_one = k.shift1[...][None, :]
    b_down = k.b_down[...][None, :]

    def norm_one(i):
        rows = at(i, 64)
        xh, rstd = norm(k.r2[rows, :])
        k.xh1[rows, :] = xh
        k.rstd1[rows, :] = rstd
        h1 = xh * gain_one + shift_one
        k.h1b[rows, :] = h1.astype(BF)
        k.r2[rows, :] = h1 + b_down

    loop(tokens // 64, norm_one)
    a_copies[2].start()

    def act_copy(i):
        t = (tp, t_a, t_b, t_d)[i]
        return remote(
            k.act.at[t, :, other_half], k.act_s.at[t], k.a_ss.at[3 + i], k.a_rs.at[3 + t], dev_s
        )

    def up(t):
        def tile(i):
            cols = at(i, 256)
            u = dot_nn(k.h1b[...], k.wu[t, :, cols]) + k.bb[t, 0:1, cols]
            cdf = 0.5 * lax.erf(u * 0.7071067811865476) + 0.5
            k.act[t, :, cols] = (u * cdf).astype(BF)
            k.gp[t, :, cols] = (cdf + u * (jnp.exp(u * u * -0.5) * 0.3989422804014327)).astype(BF)

        loop(lane_blocks, tile)

    def down(t):
        def tile(i):
            cols = at(i, 256)
            k.r2[:, cols] += dot_nn(k.act[t], k.wd[t, :, cols])

        loop(lane_blocks, tile)

    local[5].wait()
    local[6].wait()
    pass_on(4)
    up(tp)
    act_copy(0).start()
    from_a(4)
    up(t_a)
    act_copy(1).start()
    from_b(4)
    up(t_b)
    act_copy(2).start()
    down(tp)
    for i in range(3):
        for j in range(dp_n - 1):
            zd_arrived(i, j)
        s_copy(5, i).start()
    last_on(4)
    from_a(5)
    down(t_a)
    from_b(5)
    down(t_b)
    from_d(4)
    up(t_d)
    act_copy(3).start()
    from_d(5)
    down(t_d)

    sub64 = lax.broadcasted_iota(jnp.int32, (64, 1), 0).astype(F32)
    zero_row = jnp.zeros((1, width), F32)

    def crop_ids(c):
        return k.ids[pl.ds(crops_dev * tp + c, 1), :]

    lens = [
        jnp.sum(jnp.where(crop_ids(c) != 0, 1.0, 0.0), axis=-1, keepdims=True)
        for c in range(crops_dev)
    ]
    for c in range(crops_dev):

        def norm_two(i, total, c=c):
            rows = pl.ds(pl.multiple_of(c * seq + i * 64, 64), 64)
            xh, rstd = norm(k.r2[rows, :])
            k.r2[rows, :] = xh
            k.rstd2[rows, :] = rstd
            live = sub64 + (i * 64).astype(F32) < lens[c]
            return total + jnp.sum(jnp.where(live, xh, 0.0), axis=0, keepdims=True)

        k.xs[c : c + 1, :] = lax.fori_loop(0, seq // 64, norm_two, zero_row)

    row8 = lax.broadcasted_iota(jnp.int32, (8, 1), 0)

    def per_crop(values, other=0.0):
        out = jnp.full((8, 1), other, F32)
        for c in range(crops_dev):
            out = jnp.where(row8 == c, values[c], out)
        return out

    crop_len = per_crop(lens, 1.0)
    gain_two, shift_two = k.gain2[...][None, :], k.shift2[...][None, :]
    xs = k.xs[...]
    is_crop = row8 < crops_dev
    pooled = jnp.where(is_crop, xs / crop_len * gain_two + shift_two, 0.0)
    inv_norm = lax.rsqrt(jnp.sum(pooled * pooled, axis=-1, keepdims=True) + 1e-06)
    e_own = (pooled * inv_norm).astype(BF).astype(F32)
    live_n = k.cnt[0]
    crops_group = crops_dev * tp_n
    dom_total = [jnp.float32(0.0), jnp.float32(0.0)]
    for c in range(crops_group):
        is_live = jnp.where(c < live_n, 1.0, 0.0)
        is_one = k.dom[c].astype(F32)
        dom_total[0] = dom_total[0] + is_live * (1.0 - is_one)
        dom_total[1] = dom_total[1] + is_live * is_one
    lane_row = lax.broadcasted_iota(jnp.int32, (1, 256), 1)
    meta_row = crops_dev * lane_blocks

    def crop_block(c, j):
        return slice(c * lane_blocks + j, c * lane_blocks + j + 1)

    def lanes_of(j):
        return slice(j * 256, (j + 1) * 256)

    for c in range(crops_dev):
        for j in range(lane_blocks):
            k.emsg[me, crop_block(c, j), :] = e_own[c : c + 1, lanes_of(j)]
    k.emsg[me, meta_row : meta_row + 1, :] = jnp.where(
        lane_row == 0, dom_total[0], jnp.where(lane_row == 1, dom_total[1], 0.0)
    )

    def e_copy(i):
        mine = k.emsg.at[me]
        return remote(
            mine, mine, k.e_ss.at[i], k.e_rs.at[me], group_dev(lax.rem(me + 1 + i, groups))
        )

    def e_wait(i):
        g = lax.rem(me + 1 + i, groups)
        remote(k.emsg.at[g], k.emsg.at[g], k.e_ss.at[i], k.e_rs.at[g], dev_s).wait_recv()

    each(groups - 1, lambda i: e_copy(i).start())
    k.posf[...] = k.pos_in[...].astype(F32)
    positives = jnp.concatenate(
        [k.posf[pl.ds(crops_dev * tp + c, 1), :] for c in range(crops_dev)]
        + [jnp.zeros((8 - crops_dev, width), F32)],
        axis=0,
    )
    pos = jnp.sum(e_own * positives, axis=-1, keepdims=True) * INV_TEMP
    for copy in local[7:]:
        copy.wait()
    each(groups - 1, e_wait)
    for c in range(crops_dev):
        for j in range(lane_blocks):
            k.es[:, c : c + 1, lanes_of(j)] = k.emsg[:, crop_block(c, j), :]

    n_block = 8
    lane_msg = lax.broadcasted_iota(jnp.int32, (n_block, 1, 256), 2)

    def queue_block(b):
        span = pl.ds(b * n_block, n_block)
        es = k.es[span].reshape(8 * n_block, width).astype(BF)
        for j in range(tp_n):
            k.neg[:, j * tokens : (j + 1) * tokens] = dot_nt(es, k.du[j]) * INV_TEMP
        neg = k.neg[...]
        top = jnp.max(neg, axis=-1, keepdims=True)
        share = jnp.exp(neg - top)
        total = jnp.sum(share, axis=-1, keepdims=True)
        high = share.astype(BF)
        k.shares[0 : 8 * n_block, :] = high
        k.shares[8 * n_block :, :] = (share - high.astype(F32)).astype(BF)
        for j in range(lane_blocks):
            both = dot_nn(k.shares[:, 0:tokens], k.du[0, :, lanes_of(j)])
            for i in range(1, tp_n):
                both = both + dot_nn(
                    k.shares[:, i * tokens : (i + 1) * tokens], k.du[i, :, lanes_of(j)]
                )
            pull = (both[0 : 8 * n_block] + both[8 * n_block :]).reshape(n_block, 8, 256)
            for c in range(crops_dev):
                k.pm_out[span, crop_block(c, j), :] = pull[:, c : c + 1, :]
        top = top.reshape(n_block, 8, 1)
        total = total.reshape(n_block, 8, 1)
        stats = jnp.zeros((n_block, 1, 256), F32)
        for c in range(crops_dev):
            stats = jnp.where(lane_msg == 2 * c, top[:, c : c + 1, :], stats)
            stats = jnp.where(lane_msg == 2 * c + 1, total[:, c : c + 1, :], stats)
        k.pm_out[span, meta_row : meta_row + 1, :] = stats

    loop(groups // n_block, queue_block)

    def p_copy(i):
        g = lax.rem(me + 1 + i, groups)
        return remote(k.pm_out.at[g], k.pm_in.at[me], k.p_ss.at[i], k.p_rs.at[me], group_dev(g))

    def p_wait(i):
        g = lax.rem(me + 1 + i, groups)
        remote(k.pm_in.at[g], k.pm_in.at[g], k.p_ss.at[i], k.p_rs.at[g], dev_s).wait_recv()

    each(groups - 1, lambda i: p_copy(i).start())
    k.pm_in[me] = k.pm_out[me]
    dom_lanes = jnp.sum(k.emsg[:, meta_row : meta_row + 1, :], axis=0)
    weights = []
    for c in range(crops_dev):
        at_c = crops_dev * tp + c
        is_one = k.dom[at_c].astype(F32)
        own_total = dom_lanes[:, 0:1] * (1.0 - is_one) + dom_lanes[:, 1:2] * is_one
        is_live = jnp.where(at_c < live_n, 1.0, 0.0)
        weights.append(
            is_live * (LOSS_SCALE * crops_group * groups) / (2.0 * jnp.maximum(own_total, 1.0))
        )
    crop_weight = per_crop(weights)
    each(groups - 1, p_wait)

    tops_all, totals_all = [], []
    for c in range(crops_dev):
        tops = k.pm_in[:, meta_row : meta_row + 1, 2 * c : 2 * c + 1]
        totals = k.pm_in[:, meta_row : meta_row + 1, 2 * c + 1 : 2 * c + 2]
        top_c = jnp.max(tops, axis=0, keepdims=True)
        scale = jnp.exp(tops - top_c)
        tops_all.append(top_c[0])
        totals_all.append(jnp.sum(scale * totals, axis=0))
        for j in range(lane_blocks):
            k.pulled[c : c + 1, lanes_of(j)] = jnp.sum(
                scale * k.pm_in[:, crop_block(c, j), :], axis=0
            )
    total_all = per_crop(totals_all, 1.0)
    lse_q = per_crop(tops_all) + jnp.log(total_all)
    top_both = jnp.maximum(pos, lse_q)
    lse = top_both + jnp.log(jnp.exp(pos - top_both) + jnp.exp(lse_q - top_both))
    de = crop_weight * (
        (jnp.exp(lse_q - lse) / total_all * INV_TEMP) * k.pulled[...]
        + ((jnp.exp(pos - lse) - 1.0) * INV_TEMP) * positives
    )
    dpool = inv_norm * (
        de - pooled * (jnp.sum(pooled * de, axis=-1, keepdims=True) * inv_norm * inv_norm)
    )
    dpool = jnp.where(is_crop, dpool / crop_len, 0.0)
    k.vec[6:7, :] = jnp.sum(dpool * xs, axis=0, keepdims=True)
    k.vec[7:8, :] = jnp.sum(dpool * crop_len, axis=0, keepdims=True)

    dgain = dpool * gain_two
    dgain_mean = jnp.mean(dgain, axis=-1, keepdims=True)
    b_down_sum = zero_row
    for c in range(crops_dev):
        dg, dg_mean = dgain[c : c + 1, :], dgain_mean[c : c + 1, :]

        def norm_two_back(i, total, c=c, dg=dg, dg_mean=dg_mean):
            rows = pl.ds(pl.multiple_of(c * seq + i * 64, 64), 64)
            xh = k.r2[rows, :]
            live = sub64 + (i * 64).astype(F32) < lens[c]
            scale = jnp.where(live, k.rstd2[rows, :], 0.0)
            dr = scale * (dg - dg_mean - xh * jnp.mean(dg * xh, axis=-1, keepdims=True))
            k.r2[rows, :] = dr
            k.df[rows, :] = dr.astype(BF)
            return total + jnp.sum(dr, axis=0, keepdims=True)

        b_down_sum = lax.fori_loop(0, seq // 64, norm_two_back, b_down_sum)
    k.vec[3:4, :] = b_down_sum
    df_copy = remote(k.df, k.df_s, k.a_ss.at[7], k.a_rs.at[7], dev_s)
    df_copy.start()

    for c in range(6):
        for i in range(3):
            w_copy(c, i).wait_send()
            s_copy(c, i).wait_send()
    for i in range(3):
        for j in range(dp_n - 1):
            zd_copy(i, j).wait_send()
        bias_copy(i).wait_send()
    for i in range(4):
        act_copy(i).wait_send()
    for copy in a_copies:
        copy.wait_send()
    each(groups - 1, lambda i: e_copy(i).wait_send())
    each(groups - 1, lambda i: p_copy(i).wait_send())

    units = 6
    unit = half // 2
    store_in = (k.g0, k.act, k.gp)

    def g_ref(n, t):
        return store_in[n // 2].at[t, pl.ds(n % 2 * unit, unit)]

    def g1_copy(n, i):
        t_from = (t_a, t_d)[i]
        return remote(
            g_ref(n, t_from), k.r_one.at[n, i], k.g1_ss.at[n, i], k.g1_rs.at[n, i], dev_a
        )

    def g2_copy(n):
        return remote(g_ref(n, t_b), k.r_two.at[n], k.g2_ss.at[n], k.g2_rs.at[n], dev_b)

    def z_side(bit):
        return lax.rem(dp // (1 << bit), 2)

    def z_span(bits):
        start, size = 0, unit
        for bit in range(bits):
            size //= 2
            start = start + z_side(bit) * size
        return start, size

    def z_dev(bit):
        return (tp, flip(dp, 1 << bit), dq)

    whole = [z_dev(bit) for bit in range(halvings, dp_bits)]
    whole += [(tp, dp, flip(dq, 2 << bit)) for bit in range(hi_bits)]

    def z_rows(start, size):
        return pl.ds(pl.multiple_of(start, 16), size)

    def gz_copy(n, bit):
        start, size = z_span(bit)
        size //= 2
        away = start + (1 - z_side(bit)) * size
        return remote(
            g_ref(n, tp).at[z_rows(away, size)],
            k.z_one.at[n, pl.ds(unit - 2 * size, size)],
            k.gz_ss.at[n, bit],
            k.gz_rs.at[n, bit],
            z_dev(bit),
        )

    def gh_copy(n, i):
        rows = z_rows(*z_span(halvings))
        return remote(
            g_ref(n, tp).at[rows], k.z_hi.at[n, i], k.gh_ss.at[n, i], k.gh_rs.at[n, i], whole[i]
        )

    def ga_copy(n, bit):
        rows = k.res.at[n, z_rows(*z_span(bit + 1))]
        return remote(rows, rows, k.ga_ss.at[n, bit], k.ga_rs.at[n, bit], z_dev(bit))

    def ga_wait(n, bit):
        start, size = z_span(bit)
        away = start + (1 - z_side(bit)) * (size // 2)
        rows = k.res.at[n, z_rows(away, size // 2)]
        remote(rows, rows, k.ga_ss.at[n, bit], k.ga_rs.at[n, bit], dev_s).wait_recv()

    def final_parts(n, of_core):
        kind, s = n // 2, n % 2
        parts = []
        for h in range(2):
            src = k.res.at[n, :, h * half : (h + 1) * half]
            if kind == 0:
                rows = pl.ds(pl.multiple_of(of_core * half + h * unit, unit), unit)
                dst = k.gd_out.at[rows, s * half : (s + 1) * half]
            elif kind == 1:
                first = s * half + h * unit
                dst = k.gu_out.at[first : first + unit, at(of_core, half)]
            else:
                dst = k.gh_out.at[2 * s + h, :, at(of_core, half)]
            parts.append((src, dst))
        return parts

    def final_copies(n):
        away, here = [], []
        for h, (src, dst) in enumerate(final_parts(n, core)):
            away.append(remote(src, dst, k.gf_ss.at[n, h], k.gf_rs.at[n, h], dev_s))
            here.append(pltpu.make_async_copy(src, dst, k.out_sem.at[2 * n + h]))
        return away, here

    def final_arrived(n):
        for h, (_, dst) in enumerate(final_parts(n, 1 - core)):
            remote(dst, dst, k.gf_ss.at[n, h], k.gf_rs.at[n, h], dev_s).wait_recv()

    def add_rows(dst, srcs):
        def step(i):
            rows = at(i, 64)
            total = dst[rows, :].astype(F32)
            for src in srcs:
                total = total + src[rows, :].astype(F32)
            dst[rows, :] = total.astype(BF)

        loop(unit // 64, step)

    def plane_first(n):
        g1_copy(n, 1).wait_recv()
        add_rows(g_ref(n, t_b), [k.r_one.at[n, 1]])
        g2_copy(n).start()

    def plane_second(n):
        g1_copy(n, 0).wait_recv()
        g2_copy(n).wait_recv()
        add_rows(g_ref(n, tp), [k.r_one.at[n, 0], k.r_two.at[n]])
        gz_copy(n, 0).start()

    def z_add(n, bit):
        gz_copy(n, bit).wait()
        start, size = z_span(bit + 1)
        mine = g_ref(n, tp).at[z_rows(start, size)]
        total = mine[...].astype(F32) + k.z_one[n, pl.ds(unit - 2 * size, size)].astype(F32)
        if bit + 1 < halvings:
            mine[...] = total.astype(BF)
            gz_copy(n, bit + 1).start()
            return
        for i in range(len(whole)):
            mine[...] = total.astype(BF)
            gh_copy(n, i).start()
            gh_copy(n, i).wait()
            total = mine[...].astype(F32) + k.z_hi[n, i].astype(F32)
        k.res[n, z_rows(start, size)] = total.astype(BF)
        ga_copy(n, halvings - 1).start()

    def z_back(n, bit):
        ga_wait(n, bit)
        if bit > 0:
            ga_copy(n, bit - 1).start()
            return
        for copies in final_copies(n):
            for copy in copies:
                copy.start()

    shard = {"a": t_a, "b": t_b, "d": t_d, "p": tp}
    place = "dabp"

    def du_copy(name):
        t = shard[name]
        i = 8 + place.index(name)
        return remote(k.du.at[t, :, other_half], k.du_s.at[t], k.a_ss.at[i], k.a_rs.at[8 + t], dev_s)

    def hidden_back(name):
        t = shard[name]

        def tile(j):
            cols = at(j, 256)
            da = dot_nt(k.df[...], k.wd[t, cols, :])
            d = (da * k.gp[t, :, cols].astype(F32)).astype(BF)
            k.du[t, :, cols] = d
            k.vec[pl.ds(8 + t, 1), cols] = jnp.sum(d.astype(F32), axis=0, keepdims=True)

        loop(lane_blocks, tile)
        du_copy(name).start()

    seen = set()

    def once(tag, wait):
        if tag not in seen:
            seen.add(tag)
            wait()

    def arrived(ref, index):
        remote(ref, ref, k.a_ss.at[0], k.a_rs.at[index], dev_s).wait_recv()

    def put(n, t, g):
        ref = g_ref(n, t)
        ref[:, 0:half] = g[0:unit].astype(BF)
        ref[:, half:width] = g[unit:half].astype(BF)

    def send_piece(n, name):
        if name in "ad":
            g1_copy(n, "ad".index(name)).start()

    def down_piece(name, s):
        t = shard[name]
        once("df", df_copy.wait_recv)
        once("act" + name, lambda: arrived(k.act_s.at[t], 3 + t))
        cols = slice(s * half, (s + 1) * half)
        put(
            s,
            t,
            dot_tn(k.act[t, :, own_half], k.df[:, cols]) + dot_tn(k.act_s[t], k.df_s[:, cols]),
        )
        send_piece(s, name)

    def up_piece(name, s):
        t = shard[name]
        once("h1", a_copies[2].wait_recv)
        once("du" + name, lambda: arrived(k.du_s.at[t], 8 + t))
        rows = slice(s * half, (s + 1) * half)
        put(
            2 + s,
            t,
            dot_tn(k.h1b[:, rows], k.du[t, :, own_half]) + dot_tn(k.h1_s[:, rows], k.du_s[t]),
        )
        send_piece(2 + s, name)

    def hidden_grad():
        def tile(i):
            cols = at(i, 256)
            total = k.r2[:, cols]
            for t in range(tp_n):
                total = total + dot_nt(k.du[t], k.wu[t, cols, :])
            k.r2[:, cols] = total

        loop(lane_blocks, tile)

    do_copy = remote(k.do.at[:, other_half], k.do_s, k.a_ss.at[12], k.a_rs.at[12], dev_s)

    def norm_one_back():
        def rows_back(i, sums):
            rows = at(i, 64)
            dh, xh = k.r2[rows, :], k.xh1[rows, :]
            dxh = dh * gain_one
            dr = k.rstd1[rows, :] * (
                dxh
                - jnp.mean(dxh, axis=-1, keepdims=True)
                - xh * jnp.mean(dxh * xh, axis=-1, keepdims=True)
            )
            k.r2[rows, :] = dr
            k.do[rows, :] = dr.astype(BF)
            return (
                sums[0] + jnp.sum(dr, axis=0, keepdims=True),
                sums[1] + jnp.sum(dh * xh, axis=0, keepdims=True),
                sums[2] + jnp.sum(dh, axis=0, keepdims=True),
            )

        out_sum, gain_sum, shift_sum = lax.fori_loop(
            0, tokens // 64, rows_back, (zero_row, zero_row, zero_row)
        )
        k.vec[2:3, :] = out_sum
        k.vec[4:5, :] = gain_sum
        k.vec[5:6, :] = shift_sum
        do_copy.start()

    def grad_lanes(c, lanes):
        return slice(c * slot + lanes.start, c * slot + lanes.stop)

    def dqkv_copy(name):
        t = shard[name]
        i = 13 + place.index(name)
        return remote(k.wd.at[t, 0:tokens], k.dqkv_s.at[t], k.a_ss.at[i], k.a_rs.at[13 + t], dev_s)

    def attend_back(name, crop):
        t = shard[name]
        rows = slice(crop * seq, (crop + 1) * seq)
        dctx_all = dot_nt(k.do[rows, :], k.wo[t_rows(t), :]).astype(BF)
        dqs, dks, dvs = [], [], []
        for h, (lanes, side) in enumerate(views):
            q, key, val = (k.qkv[c, t, rows, lanes] for c in range(3))
            dctx = dctx_all[:, lanes]
            p = k.prob[(crop * tp_n + t) * heads_t + h]
            pf = p.astype(F32)
            dprob = dot_nt(masked(dctx, side), val)
            ds = (pf * (dprob - jnp.sum(dprob * pf, axis=-1, keepdims=True))).astype(BF)
            dvs.append(dot_tn(p, dctx))
            dqs.append(dot_nn(ds, key) * 0.125)
            dks.append(dot_tn(ds, q))
        for c, outs in enumerate((dqs, dks, dvs)):

            def store(lanes, value, c=c):
                k.wd[t, rows, grad_lanes(c, lanes)] = value.astype(BF)

            merged(outs, store)
        if crop == crops_dev - 1:
            dqkv_copy(name).start()

    heads_lanes = slice(0, heads_w)

    def head_grad(t, c):
        cols = grad_lanes(c, heads_lanes)
        g = dot_tn(k.wd[t, 0:tokens, cols], k.xb[:, own_half])
        return (g + dot_tn(k.dqkv_s[t, :, cols], k.x_s[...])).astype(BF)

    def out_piece(name):
        t = shard[name]
        once("do", do_copy.wait_recv)
        once("ctx", a_copies[1].wait_recv)
        g = dot_tn(k.ctx[t], k.do[:, own_half]) + dot_tn(k.ctx_s[t], k.do_s[...])
        g_ref(5, t)[:, half:width] = g.astype(BF)

    def query_key_piece(name):
        t = shard[name]
        once("x", a_copies[0].wait_recv)
        once("dqkv" + name, lambda: arrived(k.dqkv_s.at[t], 13 + t))
        g_ref(4, t)[:, 0:half] = head_grad(t, 0)
        g_ref(4, t)[:, half:width] = head_grad(t, 1)
        send_piece(4, name)

    def value_piece(name):
        t = shard[name]
        once("x", a_copies[0].wait_recv)
        once("dqkv" + name, lambda: arrived(k.dqkv_s.at[t], 13 + t))
        g_ref(5, t)[:, 0:half] = head_grad(t, 2)
        send_piece(5, name)

    def input_grad():
        do_copy.wait_send()

        def tile(i):
            cols = at(i, 256)
            total = k.r2[:, cols]
            for t in range(tp_n):
                for c in range(3):
                    total = total + dot_nn(
                        k.wd[t, 0:tokens, grad_lanes(c, heads_lanes)],
                        k.wqkv[c, t * heads_w : (t + 1) * heads_w, cols],
                    )
            k.do[:, cols] = total.astype(BF)

        loop(lane_blocks, tile)

    def dx_rows(t):
        return k.dx_out.at[at(t, tokens)]

    dx_local = pltpu.make_async_copy(k.do, dx_rows(tp), k.out_sem.at[2 * units])

    def dx_copy(i):
        if i < 2:
            return remote(k.do, dx_rows(tp), k.x_ss.at[i], k.x_rs.at[i], (dev_a, dev_b)[i])
        return remote(dx_rows(t_a), dx_rows(t_a), k.x_ss.at[2], k.x_rs.at[2], dev_b)

    def dx_arrived(i):
        there = dx_rows(others[i])
        remote(there, there, k.x_ss.at[i], k.x_rs.at[i], dev_a).wait_recv()

    def dx_send():
        dx_copy(0).start()
        dx_copy(1).start()
        dx_local.start()

    def dx_pass():
        dx_arrived(0)
        dx_copy(2).start()

    def dx_last():
        dx_arrived(1)
        dx_arrived(2)

    def v_sibling():
        return remote(k.vec, k.v_hi.at[0], k.v_ss.at[0], k.v_rs.at[0], dev_s)

    def v_plane(i):
        mine = k.v_plane.at[tp]
        return remote(
            mine, mine, k.v_ss.at[1 + i], k.v_rs.at[1 + i], ((t_x, t_y, t_d)[i], dp, dq)
        )

    def v_plane_arrived(i):
        there = k.v_plane.at[(t_x, t_y, t_d)[i]]
        remote(there, there, k.v_ss.at[1 + i], k.v_rs.at[1 + i], dev_s).wait_recv()

    def v_planes(j):
        mine = k.v_z.at[dp]
        return remote(
            mine, mine, k.v_ss.at[4 + j], k.v_rs.at[4 + dp], (tp, lax.rem(dp + 1 + j, dp_n), dq)
        )

    def v_planes_arrived(j):
        z = lax.rem(dp + 1 + j, dp_n)
        there = k.v_z.at[z]
        remote(there, there, k.v_ss.at[4 + j], k.v_rs.at[4 + z], dev_s).wait_recv()

    def v_group(bit):
        i = 4 + dp_n + bit
        return remote(
            k.v_hi.at[1 + 2 * bit],
            k.v_hi.at[2 + 2 * bit],
            k.v_ss.at[i],
            k.v_rs.at[i],
            (tp, dp, flip(dq, 2 << bit)),
        )

    def vector_send():
        for t in range(tp_n):
            for c, lanes in ((0, slice(0, heads_w)), (2, slice(slot, slot + heads_w))):
                grads = k.wd[t, 0:tokens, grad_lanes(c, heads_lanes)].astype(F32)
                k.vec[12 + t : 13 + t, lanes] = jnp.sum(grads, axis=0, keepdims=True)
        v_sibling().start()

    def vector_plane():
        v_sibling().wait()
        k.v_plane[tp] = k.vec[...] + k.v_hi[0]
        for i in range(3):
            v_plane(i).start()

    def vector_planes():
        for i in range(3):
            v_plane_arrived(i)
        total = k.v_plane[0]
        for t in range(1, tp_n):
            total = total + k.v_plane[t]
        k.v_z[dp] = total
        for j in range(dp_n - 1):
            v_planes(j).start()

    def vector_last():
        for j in range(dp_n - 1):
            v_planes_arrived(j)
        total = k.v_z[0]
        for z in range(1, dp_n):
            total = total + k.v_z[z]
        for bit in range(hi_bits):
            k.v_hi[1 + 2 * bit] = total
            v_group(bit).start()
            v_group(bit).wait_recv()
            total = total + k.v_hi[2 + 2 * bit]
        k.vec_out[...] = total

    steps = {
        "HG": hidden_grad,
        "L1B": norm_one_back,
        "IG": input_grad,
        "DX": dx_send,
        "DXF": dx_pass,
        "DXL": dx_last,
        "VS": vector_send,
        "V1": vector_plane,
        "V2": vector_planes,
        "V3": vector_last,
    }
    for name in place:
        steps["HB" + name] = functools.partial(hidden_back, name)
        steps["OP" + name] = functools.partial(out_piece, name)
        steps["HQ" + name] = functools.partial(query_key_piece, name)
        steps["HV" + name] = functools.partial(value_piece, name)
        for s in range(2):
            steps["DP" + name + str(s)] = functools.partial(down_piece, name, s)
            steps["UP" + name + str(s)] = functools.partial(up_piece, name, s)
        for crop in range(crops_dev):
            steps["AB" + name + str(crop)] = functools.partial(attend_back, name, crop)
    for n in range(units):
        tag = "_" + "DUH"[n // 2] + str(n % 2)
        steps["P1" + tag] = functools.partial(plane_first, n)
        steps["P2" + tag] = functools.partial(plane_second, n)
        for bit in range(halvings):
            steps["Z" + str(bit) + tag] = functools.partial(z_add, n, bit)
            steps["A" + str(halvings - 1 - bit) + tag] = functools.partial(z_back, n, halvings - 1 - bit)
        steps["F" + tag] = functools.partial(final_arrived, n)
    for step in BACKWARD_ORDER:
        steps.pop(step)()
    for step in steps.values():
        step()

    df_copy.wait_send()
    dx_local.wait()
    for i in range(3):
        dx_copy(i).wait_send()
        v_plane(i).wait_send()
    for j in range(dp_n - 1):
        v_planes(j).wait_send()
    for bit in range(hi_bits):
        v_group(bit).wait_send()
    for name in place:
        du_copy(name).wait_send()
        dqkv_copy(name).wait_send()
    for n in range(units):
        away, here = final_copies(n)
        for copy in away:
            copy.wait_send()
        for copy in here:
            copy.wait()
        for i in range(2):
            g1_copy(n, i).wait_send()
        g2_copy(n).wait_send()
        for bit in range(halvings):
            ga_copy(n, bit).wait_send()


def run_layer(mesh_sizes, args):
    tp_n, dp_n, dq_n = mesh_sizes
    ids, x_in = args[0], args[13]
    width = x_in.shape[1]
    crops_dev = ids.shape[0] // tp_n
    tokens = x_in.shape[0] // tp_n
    seq = tokens // crops_dev
    groups = dp_n * dq_n
    half = width // 2
    heads_w = width // tp_n
    dp_bits = dp_n.bit_length() - 1
    hi_bits = (dq_n // 2).bit_length() - 1
    heads = width // HD
    unit = half // 2
    halvings = halvings_of(width, dp_n)
    n_whole = max(dp_bits - halvings + hi_bits, 1)
    smem = pl.BlockSpec(memory_space=pltpu.SMEM)
    vmem = pl.BlockSpec(memory_space=pltpu.VMEM)
    hbm = pl.BlockSpec(memory_space=pl.ANY)
    dma = pltpu.SemaphoreType.DMA

    def b16(*shape):
        return pltpu.VMEM(shape, BF)

    def f32(*shape):
        return pltpu.VMEM(shape, F32)

    scratch = [
        b16(3, width, width),
        b16(width, width),
        b16(tp_n, width, width),
        b16(tp_n, width, width),
        b16(tokens, width),
        b16(3, tp_n, tokens, heads_w),
        b16(crops_dev * heads, seq, seq),
        b16(tp_n, tokens, heads_w),
        f32(tokens, width),
        f32(tokens, 1),
        b16(tokens, width),
        b16(tp_n, tokens, width),
        b16(tp_n, tokens, width),
        f32(tokens, width),
        f32(tokens, 1),
        b16(tokens, half),
        b16(tp_n, tokens, heads_w),
        b16(tokens, width),
        b16(tp_n, tokens, half),
        b16(tokens, width),
        b16(tp_n, tokens, half),
        b16(tokens, half),
        b16(tp_n, tokens, width),
        b16(tokens, width),
        b16(tp_n, tokens, width),
        b16(tokens, width),
        b16(tp_n, half, width),
        b16(6, 2, unit, width),
        b16(6, unit, width),
        b16(6, unit - (unit >> halvings), width),
        b16(6, n_whole, unit >> halvings, width),
        b16(6, unit, width),
        f32(tp_n, 8, width),
        f32(groups, 8, 256),
        f32(groups, 8, width),
        f32(64, tp_n * tokens),
        b16(128, tp_n * tokens),
        f32(groups, 8, 256),
        f32(groups, 8, 256),
        f32(8, width),
        f32(ids.shape[0], width),
        f32(8, width),
        f32(16, width),
        f32(tp_n, 16, width),
        f32(dp_n, 16, width),
        f32(1 + 2 * hi_bits, 16, width),
        dma((7 + tp_n,)),
        dma((6, 3)),
        dma((6, 3)),
        dma((6, 3)),
        dma((6, 3)),
        dma((3, dp_n)),
        dma((3, dp_n)),
        dma((3,)),
        dma((3,)),
        dma((17,)),
        dma((17,)),
        dma((groups,)),
        dma((groups,)),
        dma((groups,)),
        dma((groups,)),
        dma((6, 2)),
        dma((6, 2)),
        dma((6,)),
        dma((6,)),
        dma((6, halvings)),
        dma((6, halvings)),
        dma((6, halvings)),
        dma((6, halvings)),
        dma((6, n_whole)),
        dma((6, n_whole)),
        dma((6, 2)),
        dma((6, 2)),
        dma((3,)),
        dma((3,)),
        dma((4 + dp_n + hi_bits,)),
        dma((4 + dp_n + hi_bits,)),
        dma((13,)),
    ]
    return pl.pallas_call(
        functools.partial(layer_kernel, (tp_n, dp_n, dq_n, crops_dev, seq, width)),
        out_shape=(
            jax.ShapeDtypeStruct((width, width), BF),
            jax.ShapeDtypeStruct((width, width), BF),
            jax.ShapeDtypeStruct((4, heads_w, width), BF),
            jax.ShapeDtypeStruct((tp_n * tokens, width), BF),
            jax.ShapeDtypeStruct((16, width), F32),
        ),
        in_specs=[vmem, smem, smem] + [vmem] * 10 + [hbm] * 8,
        out_specs=(hbm, hbm, hbm, hbm, vmem),
        scratch_shapes=scratch,
        compiler_params=pltpu.CompilerParams(
            collective_id=0, has_side_effects=True, vmem_limit_bytes=63 * 2**20
        ),
    )(*args)


def widen_kernel(gd, gu, gh, dx, gd_o, gu_o, gq_o, gk_o, gv_o, go_o, dx_o):
    gd_o[...] = gd[...].astype(F32)
    gu_o[...] = gu[...].astype(F32)
    dx_o[...] = dx[...].astype(F32)
    for c, out in enumerate((gq_o, gk_o, gv_o, go_o)):
        out[...] = gh[c].astype(F32)


def widen(gd, gu, gh, dx):
    width, tokens, heads_w = gd.shape[0], dx.shape[0], gh.shape[1]
    steps = 8
    row_steps = heads_w // 48
    rows = pl.BlockSpec((width // steps, width), lambda i: (i, 0))
    out = pl.BlockSpec((48, width), lambda i: (jnp.minimum(i, row_steps - 1), 0))
    tokens_spec = pl.BlockSpec((tokens // steps, width), lambda i: (i, 0))
    return pl.pallas_call(
        widen_kernel,
        grid=(steps,),
        out_shape=(
            jax.ShapeDtypeStruct((width, width), F32),
            jax.ShapeDtypeStruct((width, width), F32),
            jax.ShapeDtypeStruct((heads_w, width), F32),
            jax.ShapeDtypeStruct((heads_w, width), F32),
            jax.ShapeDtypeStruct((heads_w, width), F32),
            jax.ShapeDtypeStruct((heads_w, width), F32),
            jax.ShapeDtypeStruct((tokens, width), F32),
        ),
        in_specs=[
            rows,
            rows,
            pl.BlockSpec((4, 48, width), lambda i: (0, jnp.minimum(i, row_steps - 1), 0)),
            tokens_spec,
        ],
        out_specs=(rows, rows, out, out, out, out, tokens_spec),
    )(gd, gu, gh, dx)


def body(
    mesh_sizes,
    inputs,
    token_ids,
    crop_counts,
    domain_ids,
    positives,
    distractor_buffer,
    w_query,
    b_query,
    w_key,
    w_value,
    b_value,
    w_out,
    b_out,
    gain_one,
    shift_one,
    w_up,
    b_up,
    w_down,
    b_down,
    gain_two,
    shift_two,
):
    tp = lax.axis_index("tp")
    heads_w = w_query.shape[1]
    slot = (heads_w + 127) // 128 * 128
    gd, gu, gh, dx, vec = run_layer(
        mesh_sizes,
        (
            token_ids,
            domain_ids,
            crop_counts,
            positives,
            b_query,
            b_value,
            b_up,
            b_out,
            gain_one,
            shift_one,
            b_down,
            gain_two,
            shift_two,
            inputs,
            w_query.T,
            w_key.T,
            w_value.T,
            w_out,
            w_up,
            w_down,
            distractor_buffer,
        ),
    )
    grad_w_down, grad_w_up, grad_w_query, grad_w_key, grad_w_value, grad_w_out, grad_inputs = widen(
        gd, gu, gh, dx
    )
    own_up = lax.dynamic_slice_in_dim(vec, 8 + tp, 1)[0]
    own_heads = lax.dynamic_slice_in_dim(vec, 12 + tp, 1)[0]
    return (
        grad_inputs,
        grad_w_query.T,
        own_heads[0:heads_w],
        grad_w_key.T,
        grad_w_value.T,
        own_heads[slot : slot + heads_w],
        grad_w_out,
        vec[2],
        vec[4],
        vec[5],
        grad_w_up,
        own_up,
        grad_w_down,
        vec[3],
        vec[6],
        vec[7],
    )


def solution(mesh):
    mesh_sizes = (mesh.shape["tp"], mesh.shape["dp"], mesh.shape["dq"])
    rows = P(("dp", "dq"), None)
    groups = P(("dp", "dq"))
    return jax.shard_map(
        functools.partial(body, mesh_sizes),
        mesh=mesh,
        in_specs=(
            rows,
            rows,
            groups,
            groups,
            rows,
            rows,
            P(None, "tp"),
            P("tp"),
            P(None, "tp"),
            P(None, "tp"),
            P("tp"),
            P("tp", None),
            P(),
            P(),
            P(),
            P(None, "tp"),
            P("tp"),
            P("tp", None),
            P(),
            P(),
            P(),
        ),
        out_specs=(
            rows,
            P(None, "tp"),
            P("tp"),
            P(None, "tp"),
            P(None, "tp"),
            P("tp"),
            P("tp", None),
            P(),
            P(),
            P(),
            P(None, "tp"),
            P("tp"),
            P("tp", None),
            P(),
            P(),
            P(),
        ),
        check_vma=False,
    )
```

```python
import functools

import jax
import jax.numpy as jnp
from jax import lax
from jax.experimental import pallas as pl
from jax.experimental.pallas import tpu as pltpu
from jax.sharding import PartitionSpec as P

HD = 64
LN_EPS = 1e-12
INV_TEMP = 1.0 / 0.05
LOSS_SCALE = 128.0
MASKED = -1000000000.0
BF = jnp.bfloat16
F32 = jnp.float32
MESH = pl.DeviceIdType.MESH


BACKWARD_ORDER = (
    "HBb", "DPd0", "DPd1", "HBp", "HBa", "DPb1", "DPa0", "DPb0", "P1_D0", "HBd", "HG", "P1_D1",
    "UPd1", "DPa1", "L1B", "DPp0", "P2_D0", "DPp1", "UPa1", "UPb0", "Z0_D0",
    "UPb1", "ABd", "P1_U1", "P2_D1", "UPd0", "Z1_D0", "ABp", "UPp1", "UPa0", "P2_U1",
    "Z0_D1", "HQd", "P1_U0", "A1_D0", "OPd", "ABa", "Z0_U1", "OPp", "UPp0", "HVd",
    "Z1_D1", "ABb", "P2_U0", "HQp", "OPb", "HQa", "OPa", "A0_D0", "Z1_U1", "HQb", "A1_D1",
    "P1_H0", "HVb", "P1_H1", "IG", "Z0_U0", "HVp", "VS", "P2_H0", "HVa", "F_D0", "Z1_U0",
    "P2_H1", "DX", "Z0_H0", "A1_U0", "Z0_H1", "Z1_H0", "A1_U1", "Z1_H1", "V1", "A1_H0", "A0_U1",
    "DXF", "A1_H1", "A0_U0", "F_U1", "V2", "A0_D1", "A0_H0", "F_U0", "A0_H1", "DXL", "F_H0",
    "F_D1", "F_H1", "V3",
)


def dot_nn(left, right):
    return lax.dot_general(left, right, (((1,), (0,)), ((), ())), preferred_element_type=F32)


def dot_nt(left, right):
    return lax.dot_general(left, right, (((1,), (1,)), ((), ())), preferred_element_type=F32)


def dot_tn(left, right):
    return lax.dot_general(left, right, (((0,), (0,)), ((), ())), preferred_element_type=F32)


def loop(count, step):
    def run(i, carry):
        step(i)
        return carry

    lax.fori_loop(0, count, run, 0)


def each(count, step):
    def run(i, carry):
        step(i)
        return carry

    lax.fori_loop(0, count, run, 0)


def at(index, size):
    return pl.ds(pl.multiple_of(index * size, size), size)


def remote(src, dst, send_sem, recv_sem, device):
    return pltpu.make_async_remote_copy(
        src_ref=src,
        dst_ref=dst,
        send_sem=send_sem,
        recv_sem=recv_sem,
        device_id=device,
        device_id_type=MESH,
    )


def flip(index, bit):
    return index + bit - 2 * bit * lax.rem(index // bit, 2)


def halvings_of(width, dp_n):
    count, rows = 0, width // 4
    while 2 << count <= dp_n and rows // 2 % 16 == 0:
        count, rows = count + 1, rows // 2
    return count


def layer_kernel(sizes, *refs):
    tp_n, dp_n, dq_n, crops_dev, seq, width = sizes
    names = (
        "ids", "dom", "cnt", "pos_in", "b_q", "b_v", "b_up", "b_out", "gain1", "shift1", "b_down",
        "gain2", "shift2", "x_in", "wq_in", "wk_in", "wv_in", "wo_in", "wu_in", "wd_in", "queue_in",
        "gd_out", "gu_out", "gh_out", "dx_out", "vec_out",
        "wqkv", "wo", "wu", "wd", "xb", "qkv", "prob", "ctx", "xh1", "rstd1", "h1b", "act", "gp",
        "r2", "rstd2",
        "x_s", "ctx_s", "h1_s", "act_s", "df_s", "du_s", "do_s", "dqkv_s",
        "df", "du", "do", "g0", "r_one", "r_two", "z_one", "z_hi", "res",
        "bb", "emsg", "es", "neg", "shares", "pm_out", "pm_in", "xs", "posf", "pulled",
        "vec", "v_plane", "v_z", "v_hi",
        "loc", "w_ss", "w_rs", "s_ss", "s_rs", "zd_ss", "zd_rs", "b_ss", "b_rs",
        "a_ss", "a_rs", "e_ss", "e_rs", "p_ss", "p_rs",
        "g1_ss", "g1_rs", "g2_ss", "g2_rs", "gz_ss", "gz_rs", "ga_ss", "ga_rs", "gh_ss", "gh_rs",
        "gf_ss", "gf_rs", "x_ss", "x_rs", "v_ss", "v_rs", "out_sem",
    )

    class Refs:
        pass

    k = Refs()
    for name, ref in zip(names, refs, strict=True):
        setattr(k, name, ref)

    tokens = crops_dev * seq
    groups = dp_n * dq_n
    dp_bits = dp_n.bit_length() - 1
    hi_bits = (dq_n // 2).bit_length() - 1
    heads_w = width // tp_n
    heads_t = heads_w // HD
    slot = (heads_w + 127) // 128 * 128
    half = width // 2
    head_half = heads_w // 2
    quarter = half // dp_n
    lane_blocks = width // 256
    halvings = halvings_of(width, dp_n)

    tp, dp, dq = lax.axis_index("tp"), lax.axis_index("dp"), lax.axis_index("dq")
    core = lax.rem(dq, 2)
    t_x = tp + 1 - 2 * lax.rem(tp, 2)
    t_y = lax.rem(tp + 2, 4)
    t_d = 3 - tp
    t_a = t_x + core * (t_y - t_x)
    t_b = t_x + t_y - t_a
    me = dp * dq_n + dq
    dev_a = (t_a, dp, dq)
    dev_b = (t_b, dp, dq)
    dev_s = (tp, dp, dq + 1 - 2 * core)
    others = (t_a, t_b, t_d)

    def group_dev(g):
        return (tp, g // dq_n, lax.rem(g, dq_n))

    own_half = at(core, half)
    other_half = at(1 - core, half)

    barrier = pltpu.get_barrier_semaphore()
    for t_peer in (t_x, t_y, t_d):
        pl.semaphore_signal(barrier, inc=1, device_id=(t_peer, dp, dq), device_id_type=MESH)

    def greet(i):
        pl.semaphore_signal(
            barrier, inc=1, device_id=group_dev(lax.rem(me + i + 1, groups)), device_id_type=MESH
        )

    each(groups - 1, greet)

    def t_rows(t):
        return at(t, heads_w)

    locals_ = [(k.x_in.at[at(tp, tokens)], k.xb)]
    heads_in = (k.wq_in, k.wk_in, k.wv_in)
    locals_ += [(heads_in[c], k.wqkv.at[c, t_rows(tp)]) for c in range(3)]
    locals_ += [(k.wo_in, k.wo.at[t_rows(tp)]), (k.wu_in, k.wu.at[tp]), (k.wd_in, k.wd.at[tp])]
    locals_ += [(k.queue_in.at[pl.ds(j * tokens, tokens)], k.du.at[j]) for j in range(tp_n)]
    local = [pltpu.make_async_copy(src, dst, k.loc.at[i]) for i, (src, dst) in enumerate(locals_)]
    for copy in local:
        copy.start()
    k.bb[tp] = jnp.zeros((8, width), F32)
    k.bb[tp, 0:1, :] = k.b_up[...][None, :]
    k.bb[tp, 1:2, 0:heads_w] = k.b_q[...][None, :]
    k.bb[tp, 2:3, 0:heads_w] = k.b_v[...][None, :]
    k.es[...] = jnp.zeros_like(k.es)
    k.pulled[...] = jnp.zeros_like(k.pulled)
    k.xs[...] = jnp.zeros_like(k.xs)
    k.vec[...] = jnp.zeros_like(k.vec)
    pl.semaphore_wait(barrier, 3 + groups - 1)

    def part(c, t, h):
        if c < 3:
            return k.wqkv.at[c, pl.ds(pl.multiple_of(t * heads_w + h * head_half, 32), head_half)]
        if c == 3:
            return k.wo.at[pl.ds(pl.multiple_of(t * heads_w + h * head_half, 32), head_half)]
        if c == 4:
            return k.wu.at[t, at(h, half)]
        return k.wd.at[t, pl.ds(pl.multiple_of(h * half + dp * quarter, 16), quarter)]

    def source(c):
        if c < 3:
            return heads_in[c].at[at(core, head_half)]
        if c == 3:
            return k.wo_in.at[at(core, head_half)]
        if c == 4:
            return k.wu_in.at[at(core, half)]
        return k.wd_in.at[pl.ds(pl.multiple_of(core * half + dp * quarter, 16), quarter)]

    def w_copy(c, i):
        if i < 2:
            return remote(
                source(c), part(c, tp, core), k.w_ss.at[c, i], k.w_rs.at[c, i], (dev_a, dev_b)[i]
            )
        there = part(c, t_a, core)
        return remote(there, there, k.w_ss.at[c, 2], k.w_rs.at[c, 2], dev_b)

    def w_arrived(c, i):
        there = part(c, others[i], core)
        remote(there, there, k.w_ss.at[c, i], k.w_rs.at[c, i], dev_a).wait_recv()

    def s_part(c, t, h):
        return k.wd.at[t, at(h, half)] if c == 5 else part(c, t, h)

    def s_copy(c, i):
        there = s_part(c, others[i], core)
        return remote(there, there, k.s_ss.at[c, i], k.s_rs.at[c, i], dev_s)

    def s_arrived(c, t, i):
        there = s_part(c, t, 1 - core)
        remote(there, there, k.s_ss.at[c, i], k.s_rs.at[c, i], dev_s).wait_recv()

    def from_a(c):
        s_arrived(c, t_a, 1)

    def from_b(c):
        s_arrived(c, t_b, 0)

    def from_d(c):
        s_arrived(c, t_d, 2)

    def zd_copy(i, j):
        there = part(5, others[i], core)
        return remote(
            there,
            there,
            k.zd_ss.at[i, j],
            k.zd_rs.at[i, dp],
            (tp, lax.rem(dp + 1 + j, dp_n), dq),
        )

    def zd_arrived(i, j):
        z = lax.rem(dp + 1 + j, dp_n)
        there = k.wd.at[others[i], pl.ds(pl.multiple_of(core * half + z * quarter, 16), quarter)]
        remote(there, there, k.zd_ss.at[i, j], k.zd_rs.at[i, z], dev_s).wait_recv()

    def send_own(c):
        w_copy(c, 0).start()
        w_copy(c, 1).start()

    def pass_on(c):
        w_arrived(c, 0)
        w_copy(c, 2).start()
        if c < 5:
            s_copy(c, 0).start()
        w_arrived(c, 1)
        if c < 5:
            s_copy(c, 1).start()

    def last_on(c):
        w_arrived(c, 2)
        s_copy(c, 2).start()

    def send_planes(i):
        for j in range(dp_n - 1):
            zd_copy(i, j).start()

    def bias_copy(i):
        mine = k.bb.at[tp]
        return remote(mine, mine, k.b_ss.at[i], k.b_rs.at[i], ((t_x, t_y, t_d)[i], dp, dq))

    def bias_arrived(i):
        there = k.bb.at[(t_x, t_y, t_d)[i]]
        remote(there, there, k.b_ss.at[i], k.b_rs.at[i], dev_s).wait_recv()

    first_head = lax.broadcasted_iota(jnp.int32, (seq, 2 * HD), 1) < HD

    def project(t):
        for c in range(3):
            out = dot_nt(k.xb[...], k.wqkv[c, t_rows(t), :])
            if c != 1:
                row = 1 if c == 0 else 2
                out = out + k.bb[t, row : row + 1, 0:heads_w]
            out = out.astype(BF)
            k.qkv[c, t] = out * BF(0.125) if c == 0 else out

    def head_views(block):
        views = []
        for h in range(heads_t):
            base = h // 2 * 2 * HD
            if h == heads_t - 1 and heads_t % 2:
                views.append((slice(base, base + HD), None))
            else:
                views.append((slice(base, base + 2 * HD), h % 2))
        return views

    views = head_views(heads_w)

    def masked(value, side):
        if side is None:
            return value
        keep = first_head if side == 0 else ~first_head
        return jnp.where(keep, value, jnp.zeros_like(value))

    def merged(outs, store):
        for h, (lanes, side) in enumerate(views):
            if side is None:
                store(lanes, outs[h])
            elif side == 1:
                store(lanes, jnp.where(first_head, outs[h - 1], outs[h]))

    def attend(t, crop):
        rows = at(crop, seq)
        ids = jnp.broadcast_to(k.ids[pl.ds(crops_dev * tp + crop, 1), :], (seq, seq))
        outs = []
        for h, (lanes, side) in enumerate(views):
            s = dot_nt(masked(k.qkv[0, t, rows, lanes], side), k.qkv[1, t, rows, lanes])
            s = jnp.where(ids != 0, s, MASKED)
            e = jnp.exp(s - jnp.max(s, axis=-1, keepdims=True))
            p = (e * (1.0 / jnp.sum(e, axis=-1, keepdims=True))).astype(BF)
            k.prob[(crop * tp_n + t) * heads_t + h] = p
            outs.append(dot_nn(p, k.qkv[2, t, rows, lanes]))

        def store(lanes, value):
            k.ctx[t, rows, lanes] = value.astype(BF)

        merged(outs, store)

    def attention(t):
        project(t)
        each(crops_dev, lambda crop: attend(t, crop))

    send_own(5)
    send_own(0)
    send_own(1)
    for i in range(3):
        bias_copy(i).start()
    for copy in local[0:4]:
        copy.wait()
    a_copies = [
        remote(k.xb.at[:, other_half], k.x_s, k.a_ss.at[0], k.a_rs.at[0], dev_s),
        remote(k.ctx, k.ctx_s, k.a_ss.at[1], k.a_rs.at[1], dev_s),
        remote(k.h1b, k.h1_s, k.a_ss.at[2], k.a_rs.at[2], dev_s),
    ]
    a_copies[0].start()
    project(tp)
    pass_on(5)
    send_planes(0)
    send_planes(1)
    send_own(2)
    send_own(3)
    attend(tp, 0)
    pass_on(0)
    for crop in range(1, crops_dev):
        attend(tp, crop)
    pass_on(1)
    w_arrived(5, 2)
    send_planes(2)
    pass_on(2)
    pass_on(3)
    send_own(4)
    for i in range(3):
        bias_arrived(i)
    for c in range(3):
        from_a(c)
    attention(t_a)
    last_on(0)
    for c in range(3):
        from_b(c)
    attention(t_b)
    last_on(1)
    last_on(2)
    last_on(3)
    for c in range(3):
        from_d(c)
    attention(t_d)
    a_copies[1].start()

    local[4].wait()
    from_a(3)
    from_b(3)
    from_d(3)

    def attn_out(i):
        rows = at(i, 256)
        total = k.xb[rows, :].astype(F32) + k.b_out[...][None, :]
        for t in range(tp_n):
            total = total + dot_nn(k.ctx[t, rows, :], k.wo[t * heads_w : (t + 1) * heads_w, :])
        k.r2[rows, :] = total

    loop(tokens // 256, attn_out)

    def norm(v):
        centered = v - jnp.mean(v, axis=-1, keepdims=True)
        rstd = lax.rsqrt(jnp.mean(centered * centered, axis=-1, keepdims=True) + LN_EPS)
        return centered * rstd, rstd

    gain_one = k.gain1[...][None, :]
    shift_one = k.shift1[...][None, :]
    b_down = k.b_down[...][None, :]

    def norm_one(i):
        rows = at(i, 64)
        xh, rstd = norm(k.r2[rows, :])
        k.xh1[rows, :] = xh
        k.rstd1[rows, :] = rstd
        h1 = xh * gain_one + shift_one
        k.h1b[rows, :] = h1.astype(BF)
        k.r2[rows, :] = h1 + b_down

    loop(tokens // 64, norm_one)
    a_copies[2].start()

    def act_copy(i):
        t = (tp, t_a, t_b, t_d)[i]
        return remote(
            k.act.at[t, :, other_half], k.act_s.at[t], k.a_ss.at[3 + i], k.a_rs.at[3 + t], dev_s
        )

    def up(t):
        def tile(i):
            cols = at(i, 256)
            u = dot_nn(k.h1b[...], k.wu[t, :, cols]) + k.bb[t, 0:1, cols]
            cdf = 0.5 * lax.erf(u * 0.7071067811865476) + 0.5
            k.act[t, :, cols] = (u * cdf).astype(BF)
            k.gp[t, :, cols] = (cdf + u * (jnp.exp(u * u * -0.5) * 0.3989422804014327)).astype(BF)

        loop(lane_blocks, tile)

    def down(t):
        def tile(i):
            cols = at(i, 256)
            k.r2[:, cols] += dot_nn(k.act[t], k.wd[t, :, cols])

        loop(lane_blocks, tile)

    local[5].wait()
    local[6].wait()
    pass_on(4)
    up(tp)
    act_copy(0).start()
    from_a(4)
    up(t_a)
    act_copy(1).start()
    from_b(4)
    up(t_b)
    act_copy(2).start()
    down(tp)
    for i in range(3):
        for j in range(dp_n - 1):
            zd_arrived(i, j)
        s_copy(5, i).start()
    last_on(4)
    from_a(5)
    down(t_a)
    from_b(5)
    down(t_b)
    from_d(4)
    up(t_d)
    act_copy(3).start()
    from_d(5)
    down(t_d)

    sub64 = lax.broadcasted_iota(jnp.int32, (64, 1), 0).astype(F32)
    zero_row = jnp.zeros((1, width), F32)

    def crop_ids(c):
        return k.ids[pl.ds(crops_dev * tp + c, 1), :]

    lens = [
        jnp.sum(jnp.where(crop_ids(c) != 0, 1.0, 0.0), axis=-1, keepdims=True)
        for c in range(crops_dev)
    ]
    for c in range(crops_dev):

        def norm_two(i, total, c=c):
            rows = pl.ds(pl.multiple_of(c * seq + i * 64, 64), 64)
            xh, rstd = norm(k.r2[rows, :])
            k.r2[rows, :] = xh
            k.rstd2[rows, :] = rstd
            live = sub64 + (i * 64).astype(F32) < lens[c]
            return total + jnp.sum(jnp.where(live, xh, 0.0), axis=0, keepdims=True)

        k.xs[c : c + 1, :] = lax.fori_loop(0, seq // 64, norm_two, zero_row)

    row8 = lax.broadcasted_iota(jnp.int32, (8, 1), 0)

    def per_crop(values, other=0.0):
        out = jnp.full((8, 1), other, F32)
        for c in range(crops_dev):
            out = jnp.where(row8 == c, values[c], out)
        return out

    crop_len = per_crop(lens, 1.0)
    gain_two, shift_two = k.gain2[...][None, :], k.shift2[...][None, :]
    xs = k.xs[...]
    is_crop = row8 < crops_dev
    pooled = jnp.where(is_crop, xs / crop_len * gain_two + shift_two, 0.0)
    inv_norm = lax.rsqrt(jnp.sum(pooled * pooled, axis=-1, keepdims=True) + 1e-06)
    e_own = (pooled * inv_norm).astype(BF).astype(F32)
    live_n = k.cnt[0]
    crops_group = crops_dev * tp_n
    dom_total = [jnp.float32(0.0), jnp.float32(0.0)]
    for c in range(crops_group):
        is_live = jnp.where(c < live_n, 1.0, 0.0)
        is_one = k.dom[c].astype(F32)
        dom_total[0] = dom_total[0] + is_live * (1.0 - is_one)
        dom_total[1] = dom_total[1] + is_live * is_one
    lane_row = lax.broadcasted_iota(jnp.int32, (1, 256), 1)
    meta_row = crops_dev * lane_blocks

    def crop_block(c, j):
        return slice(c * lane_blocks + j, c * lane_blocks + j + 1)

    def lanes_of(j):
        return slice(j * 256, (j + 1) * 256)

    for c in range(crops_dev):
        for j in range(lane_blocks):
            k.emsg[me, crop_block(c, j), :] = e_own[c : c + 1, lanes_of(j)]
    k.emsg[me, meta_row : meta_row + 1, :] = jnp.where(
        lane_row == 0, dom_total[0], jnp.where(lane_row == 1, dom_total[1], 0.0)
    )

    def e_copy(i):
        mine = k.emsg.at[me]
        return remote(
            mine, mine, k.e_ss.at[i], k.e_rs.at[me], group_dev(lax.rem(me + 1 + i, groups))
        )

    def e_wait(i):
        g = lax.rem(me + 1 + i, groups)
        remote(k.emsg.at[g], k.emsg.at[g], k.e_ss.at[i], k.e_rs.at[g], dev_s).wait_recv()

    each(groups - 1, lambda i: e_copy(i).start())
    k.posf[...] = k.pos_in[...].astype(F32)
    positives = jnp.concatenate(
        [k.posf[pl.ds(crops_dev * tp + c, 1), :] for c in range(crops_dev)]
        + [jnp.zeros((8 - crops_dev, width), F32)],
        axis=0,
    )
    pos = jnp.sum(e_own * positives, axis=-1, keepdims=True) * INV_TEMP
    for copy in local[7:]:
        copy.wait()
    each(groups - 1, e_wait)
    for c in range(crops_dev):
        for j in range(lane_blocks):
            k.es[:, c : c + 1, lanes_of(j)] = k.emsg[:, crop_block(c, j), :]

    n_block = 8
    lane_msg = lax.broadcasted_iota(jnp.int32, (n_block, 1, 256), 2)

    def queue_block(b):
        span = pl.ds(b * n_block, n_block)
        es = k.es[span].reshape(8 * n_block, width).astype(BF)
        for j in range(tp_n):
            k.neg[:, j * tokens : (j + 1) * tokens] = dot_nt(es, k.du[j]) * INV_TEMP
        neg = k.neg[...]
        top = jnp.max(neg, axis=-1, keepdims=True)
        share = jnp.exp(neg - top)
        total = jnp.sum(share, axis=-1, keepdims=True)
        high = share.astype(BF)
        k.shares[0 : 8 * n_block, :] = high
        k.shares[8 * n_block :, :] = (share - high.astype(F32)).astype(BF)
        for j in range(lane_blocks):
            both = dot_nn(k.shares[:, 0:tokens], k.du[0, :, lanes_of(j)])
            for i in range(1, tp_n):
                both = both + dot_nn(
                    k.shares[:, i * tokens : (i + 1) * tokens], k.du[i, :, lanes_of(j)]
                )
            pull = (both[0 : 8 * n_block] + both[8 * n_block :]).reshape(n_block, 8, 256)
            for c in range(crops_dev):
                k.pm_out[span, crop_block(c, j), :] = pull[:, c : c + 1, :]
        top = top.reshape(n_block, 8, 1)
        total = total.reshape(n_block, 8, 1)
        stats = jnp.zeros((n_block, 1, 256), F32)
        for c in range(crops_dev):
            stats = jnp.where(lane_msg == 2 * c, top[:, c : c + 1, :], stats)
            stats = jnp.where(lane_msg == 2 * c + 1, total[:, c : c + 1, :], stats)
        k.pm_out[span, meta_row : meta_row + 1, :] = stats

    loop(groups // n_block, queue_block)

    def p_copy(i):
        g = lax.rem(me + 1 + i, groups)
        return remote(k.pm_out.at[g], k.pm_in.at[me], k.p_ss.at[i], k.p_rs.at[me], group_dev(g))

    def p_wait(i):
        g = lax.rem(me + 1 + i, groups)
        remote(k.pm_in.at[g], k.pm_in.at[g], k.p_ss.at[i], k.p_rs.at[g], dev_s).wait_recv()

    each(groups - 1, lambda i: p_copy(i).start())
    k.pm_in[me] = k.pm_out[me]
    dom_lanes = jnp.sum(k.emsg[:, meta_row : meta_row + 1, :], axis=0)
    weights = []
    for c in range(crops_dev):
        at_c = crops_dev * tp + c
        is_one = k.dom[at_c].astype(F32)
        own_total = dom_lanes[:, 0:1] * (1.0 - is_one) + dom_lanes[:, 1:2] * is_one
        is_live = jnp.where(at_c < live_n, 1.0, 0.0)
        weights.append(
            is_live * (LOSS_SCALE * crops_group * groups) / (2.0 * jnp.maximum(own_total, 1.0))
        )
    crop_weight = per_crop(weights)
    each(groups - 1, p_wait)

    tops_all, totals_all = [], []
    for c in range(crops_dev):
        tops = k.pm_in[:, meta_row : meta_row + 1, 2 * c : 2 * c + 1]
        totals = k.pm_in[:, meta_row : meta_row + 1, 2 * c + 1 : 2 * c + 2]
        top_c = jnp.max(tops, axis=0, keepdims=True)
        scale = jnp.exp(tops - top_c)
        tops_all.append(top_c[0])
        totals_all.append(jnp.sum(scale * totals, axis=0))
        for j in range(lane_blocks):
            k.pulled[c : c + 1, lanes_of(j)] = jnp.sum(
                scale * k.pm_in[:, crop_block(c, j), :], axis=0
            )
    total_all = per_crop(totals_all, 1.0)
    lse_q = per_crop(tops_all) + jnp.log(total_all)
    top_both = jnp.maximum(pos, lse_q)
    lse = top_both + jnp.log(jnp.exp(pos - top_both) + jnp.exp(lse_q - top_both))
    de = crop_weight * (
        (jnp.exp(lse_q - lse) / total_all * INV_TEMP) * k.pulled[...]
        + ((jnp.exp(pos - lse) - 1.0) * INV_TEMP) * positives
    )
    dpool = inv_norm * (
        de - pooled * (jnp.sum(pooled * de, axis=-1, keepdims=True) * inv_norm * inv_norm)
    )
    dpool = jnp.where(is_crop, dpool / crop_len, 0.0)
    k.vec[6:7, :] = jnp.sum(dpool * xs, axis=0, keepdims=True)
    k.vec[7:8, :] = jnp.sum(dpool * crop_len, axis=0, keepdims=True)

    dgain = dpool * gain_two
    dgain_mean = jnp.mean(dgain, axis=-1, keepdims=True)
    b_down_sum = zero_row
    for c in range(crops_dev):
        dg, dg_mean = dgain[c : c + 1, :], dgain_mean[c : c + 1, :]

        def norm_two_back(i, total, c=c, dg=dg, dg_mean=dg_mean):
            rows = pl.ds(pl.multiple_of(c * seq + i * 64, 64), 64)
            xh = k.r2[rows, :]
            live = sub64 + (i * 64).astype(F32) < lens[c]
            scale = jnp.where(live, k.rstd2[rows, :], 0.0)
            dr = scale * (dg - dg_mean - xh * jnp.mean(dg * xh, axis=-1, keepdims=True))
            k.r2[rows, :] = dr
            k.df[rows, :] = dr.astype(BF)
            return total + jnp.sum(dr, axis=0, keepdims=True)

        b_down_sum = lax.fori_loop(0, seq // 64, norm_two_back, b_down_sum)
    k.vec[3:4, :] = b_down_sum
    df_copy = remote(k.df, k.df_s, k.a_ss.at[7], k.a_rs.at[7], dev_s)
    df_copy.start()

    for c in range(6):
        for i in range(3):
            w_copy(c, i).wait_send()
            s_copy(c, i).wait_send()
    for i in range(3):
        for j in range(dp_n - 1):
            zd_copy(i, j).wait_send()
        bias_copy(i).wait_send()
    for i in range(4):
        act_copy(i).wait_send()
    for copy in a_copies:
        copy.wait_send()
    each(groups - 1, lambda i: e_copy(i).wait_send())
    each(groups - 1, lambda i: p_copy(i).wait_send())

    units = 6
    unit = half // 2
    store_in = (k.g0, k.act, k.gp)

    def g_ref(n, t):
        return store_in[n // 2].at[t, pl.ds(n % 2 * unit, unit)]

    def g1_copy(n, i):
        t_from = (t_a, t_d)[i]
        return remote(
            g_ref(n, t_from), k.r_one.at[n, i], k.g1_ss.at[n, i], k.g1_rs.at[n, i], dev_a
        )

    def g2_copy(n):
        return remote(g_ref(n, t_b), k.r_two.at[n], k.g2_ss.at[n], k.g2_rs.at[n], dev_b)

    def z_side(bit):
        return lax.rem(dp // (1 << bit), 2)

    def z_span(bits):
        start, size = 0, unit
        for bit in range(bits):
            size //= 2
            start = start + z_side(bit) * size
        return start, size

    def z_dev(bit):
        return (tp, flip(dp, 1 << bit), dq)

    whole = [z_dev(bit) for bit in range(halvings, dp_bits)]
    whole += [(tp, dp, flip(dq, 2 << bit)) for bit in range(hi_bits)]

    def z_rows(start, size):
        return pl.ds(pl.multiple_of(start, 16), size)

    def gz_copy(n, bit):
        start, size = z_span(bit)
        size //= 2
        away = start + (1 - z_side(bit)) * size
        return remote(
            g_ref(n, tp).at[z_rows(away, size)],
            k.z_one.at[n, pl.ds(unit - 2 * size, size)],
            k.gz_ss.at[n, bit],
            k.gz_rs.at[n, bit],
            z_dev(bit),
        )

    def gh_copy(n, i):
        rows = z_rows(*z_span(halvings))
        return remote(
            g_ref(n, tp).at[rows], k.z_hi.at[n, i], k.gh_ss.at[n, i], k.gh_rs.at[n, i], whole[i]
        )

    def ga_copy(n, bit):
        rows = k.res.at[n, z_rows(*z_span(bit + 1))]
        return remote(rows, rows, k.ga_ss.at[n, bit], k.ga_rs.at[n, bit], z_dev(bit))

    def ga_wait(n, bit):
        start, size = z_span(bit)
        away = start + (1 - z_side(bit)) * (size // 2)
        rows = k.res.at[n, z_rows(away, size // 2)]
        remote(rows, rows, k.ga_ss.at[n, bit], k.ga_rs.at[n, bit], dev_s).wait_recv()

    def final_parts(n, of_core):
        kind, s = n // 2, n % 2
        parts = []
        for h in range(2):
            src = k.res.at[n, :, h * half : (h + 1) * half]
            if kind == 0:
                rows = pl.ds(pl.multiple_of(of_core * half + h * unit, unit), unit)
                dst = k.gd_out.at[rows, s * half : (s + 1) * half]
            elif kind == 1:
                first = s * half + h * unit
                dst = k.gu_out.at[first : first + unit, at(of_core, half)]
            else:
                dst = k.gh_out.at[2 * s + h, :, at(of_core, half)]
            parts.append((src, dst))
        return parts

    def final_copies(n):
        away, here = [], []
        for h, (src, dst) in enumerate(final_parts(n, core)):
            away.append(remote(src, dst, k.gf_ss.at[n, h], k.gf_rs.at[n, h], dev_s))
            here.append(pltpu.make_async_copy(src, dst, k.out_sem.at[2 * n + h]))
        return away, here

    def final_arrived(n):
        for h, (_, dst) in enumerate(final_parts(n, 1 - core)):
            remote(dst, dst, k.gf_ss.at[n, h], k.gf_rs.at[n, h], dev_s).wait_recv()

    def add_rows(dst, srcs):
        def step(i):
            rows = at(i, 64)
            total = dst[rows, :].astype(F32)
            for src in srcs:
                total = total + src[rows, :].astype(F32)
            dst[rows, :] = total.astype(BF)

        loop(unit // 64, step)

    def plane_first(n):
        g1_copy(n, 1).wait_recv()
        add_rows(g_ref(n, t_b), [k.r_one.at[n, 1]])
        g2_copy(n).start()

    def plane_second(n):
        g1_copy(n, 0).wait_recv()
        g2_copy(n).wait_recv()
        add_rows(g_ref(n, tp), [k.r_one.at[n, 0], k.r_two.at[n]])
        gz_copy(n, 0).start()

    def z_add(n, bit):
        gz_copy(n, bit).wait()
        start, size = z_span(bit + 1)
        mine = g_ref(n, tp).at[z_rows(start, size)]
        total = mine[...].astype(F32) + k.z_one[n, pl.ds(unit - 2 * size, size)].astype(F32)
        if bit + 1 < halvings:
            mine[...] = total.astype(BF)
            gz_copy(n, bit + 1).start()
            return
        for i in range(len(whole)):
            mine[...] = total.astype(BF)
            gh_copy(n, i).start()
            gh_copy(n, i).wait()
            total = mine[...].astype(F32) + k.z_hi[n, i].astype(F32)
        k.res[n, z_rows(start, size)] = total.astype(BF)
        ga_copy(n, halvings - 1).start()

    def z_back(n, bit):
        ga_wait(n, bit)
        if bit > 0:
            ga_copy(n, bit - 1).start()
            return
        for copies in final_copies(n):
            for copy in copies:
                copy.start()

    shard = {"a": t_a, "b": t_b, "d": t_d, "p": tp}
    place = "dabp"

    def du_copy(name):
        t = shard[name]
        i = 8 + place.index(name)
        return remote(k.du.at[t, :, other_half], k.du_s.at[t], k.a_ss.at[i], k.a_rs.at[8 + t], dev_s)

    def hidden_back(name):
        t = shard[name]

        def tile(j):
            cols = at(j, 256)
            da = dot_nt(k.df[...], k.wd[t, cols, :])
            d = (da * k.gp[t, :, cols].astype(F32)).astype(BF)
            k.du[t, :, cols] = d
            k.vec[pl.ds(8 + t, 1), cols] = jnp.sum(d.astype(F32), axis=0, keepdims=True)

        loop(lane_blocks, tile)
        du_copy(name).start()

    seen = set()

    def once(tag, wait):
        if tag not in seen:
            seen.add(tag)
            wait()

    def arrived(ref, index):
        remote(ref, ref, k.a_ss.at[0], k.a_rs.at[index], dev_s).wait_recv()

    def put(n, t, g):
        ref = g_ref(n, t)
        ref[:, 0:half] = g[0:unit].astype(BF)
        ref[:, half:width] = g[unit:half].astype(BF)

    def send_piece(n, name):
        if name in "ad":
            g1_copy(n, "ad".index(name)).start()

    def down_piece(name, s):
        t = shard[name]
        once("df", df_copy.wait_recv)
        once("act" + name, lambda: arrived(k.act_s.at[t], 3 + t))
        cols = slice(s * half, (s + 1) * half)
        put(
            s,
            t,
            dot_tn(k.act[t, :, own_half], k.df[:, cols]) + dot_tn(k.act_s[t], k.df_s[:, cols]),
        )
        send_piece(s, name)

    def up_piece(name, s):
        t = shard[name]
        once("h1", a_copies[2].wait_recv)
        once("du" + name, lambda: arrived(k.du_s.at[t], 8 + t))
        rows = slice(s * half, (s + 1) * half)
        put(
            2 + s,
            t,
            dot_tn(k.h1b[:, rows], k.du[t, :, own_half]) + dot_tn(k.h1_s[:, rows], k.du_s[t]),
        )
        send_piece(2 + s, name)

    def hidden_grad():
        def tile(i):
            cols = at(i, 256)
            total = k.r2[:, cols]
            for t in range(tp_n):
                total = total + dot_nt(k.du[t], k.wu[t, cols, :])
            k.r2[:, cols] = total

        loop(lane_blocks, tile)

    do_copy = remote(k.do.at[:, other_half], k.do_s, k.a_ss.at[12], k.a_rs.at[12], dev_s)

    def norm_one_back():
        def rows_back(i, sums):
            rows = at(i, 64)
            dh, xh = k.r2[rows, :], k.xh1[rows, :]
            dxh = dh * gain_one
            dr = k.rstd1[rows, :] * (
                dxh
                - jnp.mean(dxh, axis=-1, keepdims=True)
                - xh * jnp.mean(dxh * xh, axis=-1, keepdims=True)
            )
            k.r2[rows, :] = dr
            k.do[rows, :] = dr.astype(BF)
            return (
                sums[0] + jnp.sum(dr, axis=0, keepdims=True),
                sums[1] + jnp.sum(dh * xh, axis=0, keepdims=True),
                sums[2] + jnp.sum(dh, axis=0, keepdims=True),
            )

        out_sum, gain_sum, shift_sum = lax.fori_loop(
            0, tokens // 64, rows_back, (zero_row, zero_row, zero_row)
        )
        k.vec[2:3, :] = out_sum
        k.vec[4:5, :] = gain_sum
        k.vec[5:6, :] = shift_sum
        do_copy.start()

    def grad_lanes(c, lanes):
        return slice(c * slot + lanes.start, c * slot + lanes.stop)

    def dqkv_copy(name):
        t = shard[name]
        i = 13 + place.index(name)
        return remote(k.wd.at[t, 0:tokens], k.dqkv_s.at[t], k.a_ss.at[i], k.a_rs.at[13 + t], dev_s)

    def attention_back(name):
        t = shard[name]
        each(crops_dev, lambda crop: attend_back(t, crop))
        dqkv_copy(name).start()

    def attend_back(t, crop):
        rows = at(crop, seq)
        dctx_all = dot_nt(k.do[rows, :], k.wo[t_rows(t), :]).astype(BF)
        dqs, dks, dvs = [], [], []
        for h, (lanes, side) in enumerate(views):
            q, key, val = (k.qkv[c, t, rows, lanes] for c in range(3))
            dctx = dctx_all[:, lanes]
            p = k.prob[(crop * tp_n + t) * heads_t + h]
            pf = p.astype(F32)
            dprob = dot_nt(masked(dctx, side), val)
            ds = (pf * (dprob - jnp.sum(dprob * pf, axis=-1, keepdims=True))).astype(BF)
            dvs.append(dot_tn(p, dctx))
            dqs.append(dot_nn(ds, key) * 0.125)
            dks.append(dot_tn(ds, q))
        for c, outs in enumerate((dqs, dks, dvs)):

            def store(lanes, value, c=c):
                k.wd[t, rows, grad_lanes(c, lanes)] = value.astype(BF)

            merged(outs, store)

    heads_lanes = slice(0, heads_w)

    def head_grad(t, c):
        cols = grad_lanes(c, heads_lanes)
        g = dot_tn(k.wd[t, 0:tokens, cols], k.xb[:, own_half])
        return (g + dot_tn(k.dqkv_s[t, :, cols], k.x_s[...])).astype(BF)

    def out_piece(name):
        t = shard[name]
        once("do", do_copy.wait_recv)
        once("ctx", a_copies[1].wait_recv)
        g = dot_tn(k.ctx[t], k.do[:, own_half]) + dot_tn(k.ctx_s[t], k.do_s[...])
        g_ref(5, t)[:, half:width] = g.astype(BF)

    def query_key_piece(name):
        t = shard[name]
        once("x", a_copies[0].wait_recv)
        once("dqkv" + name, lambda: arrived(k.dqkv_s.at[t], 13 + t))
        g_ref(4, t)[:, 0:half] = head_grad(t, 0)
        g_ref(4, t)[:, half:width] = head_grad(t, 1)
        send_piece(4, name)

    def value_piece(name):
        t = shard[name]
        once("x", a_copies[0].wait_recv)
        once("dqkv" + name, lambda: arrived(k.dqkv_s.at[t], 13 + t))
        g_ref(5, t)[:, 0:half] = head_grad(t, 2)
        send_piece(5, name)

    def input_grad():
        do_copy.wait_send()

        def tile(i):
            cols = at(i, 256)
            total = k.r2[:, cols]
            for t in range(tp_n):
                for c in range(3):
                    total = total + dot_nn(
                        k.wd[t, 0:tokens, grad_lanes(c, heads_lanes)],
                        k.wqkv[c, t * heads_w : (t + 1) * heads_w, cols],
                    )
            k.do[:, cols] = total.astype(BF)

        loop(lane_blocks, tile)

    def dx_rows(t):
        return k.dx_out.at[at(t, tokens)]

    dx_local = pltpu.make_async_copy(k.do, dx_rows(tp), k.out_sem.at[2 * units])

    def dx_copy(i):
        if i < 2:
            return remote(k.do, dx_rows(tp), k.x_ss.at[i], k.x_rs.at[i], (dev_a, dev_b)[i])
        return remote(dx_rows(t_a), dx_rows(t_a), k.x_ss.at[2], k.x_rs.at[2], dev_b)

    def dx_arrived(i):
        there = dx_rows(others[i])
        remote(there, there, k.x_ss.at[i], k.x_rs.at[i], dev_a).wait_recv()

    def dx_send():
        dx_copy(0).start()
        dx_copy(1).start()
        dx_local.start()

    def dx_pass():
        dx_arrived(0)
        dx_copy(2).start()

    def dx_last():
        dx_arrived(1)
        dx_arrived(2)

    def v_sibling():
        return remote(k.vec, k.v_hi.at[0], k.v_ss.at[0], k.v_rs.at[0], dev_s)

    def v_plane(i):
        mine = k.v_plane.at[tp]
        return remote(
            mine, mine, k.v_ss.at[1 + i], k.v_rs.at[1 + i], ((t_x, t_y, t_d)[i], dp, dq)
        )

    def v_plane_arrived(i):
        there = k.v_plane.at[(t_x, t_y, t_d)[i]]
        remote(there, there, k.v_ss.at[1 + i], k.v_rs.at[1 + i], dev_s).wait_recv()

    def v_planes(j):
        mine = k.v_z.at[dp]
        return remote(
            mine, mine, k.v_ss.at[4 + j], k.v_rs.at[4 + dp], (tp, lax.rem(dp + 1 + j, dp_n), dq)
        )

    def v_planes_arrived(j):
        z = lax.rem(dp + 1 + j, dp_n)
        there = k.v_z.at[z]
        remote(there, there, k.v_ss.at[4 + j], k.v_rs.at[4 + z], dev_s).wait_recv()

    def v_group(bit):
        i = 4 + dp_n + bit
        return remote(
            k.v_hi.at[1 + 2 * bit],
            k.v_hi.at[2 + 2 * bit],
            k.v_ss.at[i],
            k.v_rs.at[i],
            (tp, dp, flip(dq, 2 << bit)),
        )

    def vector_send():
        for t in range(tp_n):
            for c, lanes in ((0, slice(0, heads_w)), (2, slice(slot, slot + heads_w))):
                grads = k.wd[t, 0:tokens, grad_lanes(c, heads_lanes)].astype(F32)
                k.vec[12 + t : 13 + t, lanes] = jnp.sum(grads, axis=0, keepdims=True)
        v_sibling().start()

    def vector_plane():
        v_sibling().wait()
        k.v_plane[tp] = k.vec[...] + k.v_hi[0]
        for i in range(3):
            v_plane(i).start()

    def vector_planes():
        for i in range(3):
            v_plane_arrived(i)
        total = k.v_plane[0]
        for t in range(1, tp_n):
            total = total + k.v_plane[t]
        k.v_z[dp] = total
        for j in range(dp_n - 1):
            v_planes(j).start()

    def vector_last():
        for j in range(dp_n - 1):
            v_planes_arrived(j)
        total = k.v_z[0]
        for z in range(1, dp_n):
            total = total + k.v_z[z]
        for bit in range(hi_bits):
            k.v_hi[1 + 2 * bit] = total
            v_group(bit).start()
            v_group(bit).wait_recv()
            total = total + k.v_hi[2 + 2 * bit]
        k.vec_out[...] = total

    steps = {
        "HG": hidden_grad,
        "L1B": norm_one_back,
        "IG": input_grad,
        "DX": dx_send,
        "DXF": dx_pass,
        "DXL": dx_last,
        "VS": vector_send,
        "V1": vector_plane,
        "V2": vector_planes,
        "V3": vector_last,
    }
    for name in place:
        steps["HB" + name] = functools.partial(hidden_back, name)
        steps["OP" + name] = functools.partial(out_piece, name)
        steps["HQ" + name] = functools.partial(query_key_piece, name)
        steps["HV" + name] = functools.partial(value_piece, name)
        for s in range(2):
            steps["DP" + name + str(s)] = functools.partial(down_piece, name, s)
            steps["UP" + name + str(s)] = functools.partial(up_piece, name, s)
        steps["AB" + name] = functools.partial(attention_back, name)
    for n in range(units):
        tag = "_" + "DUH"[n // 2] + str(n % 2)
        steps["P1" + tag] = functools.partial(plane_first, n)
        steps["P2" + tag] = functools.partial(plane_second, n)
        for bit in range(halvings):
            steps["Z" + str(bit) + tag] = functools.partial(z_add, n, bit)
            steps["A" + str(halvings - 1 - bit) + tag] = functools.partial(z_back, n, halvings - 1 - bit)
        steps["F" + tag] = functools.partial(final_arrived, n)
    for step in BACKWARD_ORDER:
        steps.pop(step)()
    for step in steps.values():
        step()

    df_copy.wait_send()
    dx_local.wait()
    for i in range(3):
        dx_copy(i).wait_send()
        v_plane(i).wait_send()
    for j in range(dp_n - 1):
        v_planes(j).wait_send()
    for bit in range(hi_bits):
        v_group(bit).wait_send()
    for name in place:
        du_copy(name).wait_send()
        dqkv_copy(name).wait_send()
    for n in range(units):
        away, here = final_copies(n)
        for copy in away:
            copy.wait_send()
        for copy in here:
            copy.wait()
        for i in range(2):
            g1_copy(n, i).wait_send()
        g2_copy(n).wait_send()
        for bit in range(halvings):
            ga_copy(n, bit).wait_send()


def run_layer(mesh_sizes, args):
    tp_n, dp_n, dq_n = mesh_sizes
    ids, x_in = args[0], args[13]
    width = x_in.shape[1]
    crops_dev = ids.shape[0] // tp_n
    tokens = x_in.shape[0] // tp_n
    seq = tokens // crops_dev
    groups = dp_n * dq_n
    half = width // 2
    heads_w = width // tp_n
    dp_bits = dp_n.bit_length() - 1
    hi_bits = (dq_n // 2).bit_length() - 1
    heads = width // HD
    unit = half // 2
    halvings = halvings_of(width, dp_n)
    n_whole = max(dp_bits - halvings + hi_bits, 1)
    smem = pl.BlockSpec(memory_space=pltpu.SMEM)
    vmem = pl.BlockSpec(memory_space=pltpu.VMEM)
    hbm = pl.BlockSpec(memory_space=pl.ANY)
    dma = pltpu.SemaphoreType.DMA

    def b16(*shape):
        return pltpu.VMEM(shape, BF)

    def f32(*shape):
        return pltpu.VMEM(shape, F32)

    scratch = [
        b16(3, width, width),
        b16(width, width),
        b16(tp_n, width, width),
        b16(tp_n, width, width),
        b16(tokens, width),
        b16(3, tp_n, tokens, heads_w),
        b16(crops_dev * heads, seq, seq),
        b16(tp_n, tokens, heads_w),
        f32(tokens, width),
        f32(tokens, 1),
        b16(tokens, width),
        b16(tp_n, tokens, width),
        b16(tp_n, tokens, width),
        f32(tokens, width),
        f32(tokens, 1),
        b16(tokens, half),
        b16(tp_n, tokens, heads_w),
        b16(tokens, width),
        b16(tp_n, tokens, half),
        b16(tokens, width),
        b16(tp_n, tokens, half),
        b16(tokens, half),
        b16(tp_n, tokens, width),
        b16(tokens, width),
        b16(tp_n, tokens, width),
        b16(tokens, width),
        b16(tp_n, half, width),
        b16(6, 2, unit, width),
        b16(6, unit, width),
        b16(6, unit - (unit >> halvings), width),
        b16(6, n_whole, unit >> halvings, width),
        b16(6, unit, width),
        f32(tp_n, 8, width),
        f32(groups, 8, 256),
        f32(groups, 8, width),
        f32(64, tp_n * tokens),
        b16(128, tp_n * tokens),
        f32(groups, 8, 256),
        f32(groups, 8, 256),
        f32(8, width),
        f32(ids.shape[0], width),
        f32(8, width),
        f32(16, width),
        f32(tp_n, 16, width),
        f32(dp_n, 16, width),
        f32(1 + 2 * hi_bits, 16, width),
        dma((7 + tp_n,)),
        dma((6, 3)),
        dma((6, 3)),
        dma((6, 3)),
        dma((6, 3)),
        dma((3, dp_n)),
        dma((3, dp_n)),
        dma((3,)),
        dma((3,)),
        dma((17,)),
        dma((17,)),
        dma((groups,)),
        dma((groups,)),
        dma((groups,)),
        dma((groups,)),
        dma((6, 2)),
        dma((6, 2)),
        dma((6,)),
        dma((6,)),
        dma((6, halvings)),
        dma((6, halvings)),
        dma((6, halvings)),
        dma((6, halvings)),
        dma((6, n_whole)),
        dma((6, n_whole)),
        dma((6, 2)),
        dma((6, 2)),
        dma((3,)),
        dma((3,)),
        dma((4 + dp_n + hi_bits,)),
        dma((4 + dp_n + hi_bits,)),
        dma((13,)),
    ]
    return pl.pallas_call(
        functools.partial(layer_kernel, (tp_n, dp_n, dq_n, crops_dev, seq, width)),
        out_shape=(
            jax.ShapeDtypeStruct((width, width), BF),
            jax.ShapeDtypeStruct((width, width), BF),
            jax.ShapeDtypeStruct((4, heads_w, width), BF),
            jax.ShapeDtypeStruct((tp_n * tokens, width), BF),
            jax.ShapeDtypeStruct((16, width), F32),
        ),
        in_specs=[vmem, smem, smem] + [vmem] * 10 + [hbm] * 8,
        out_specs=(hbm, hbm, hbm, hbm, vmem),
        scratch_shapes=scratch,
        compiler_params=pltpu.CompilerParams(
            collective_id=0, has_side_effects=True, vmem_limit_bytes=63 * 2**20
        ),
    )(*args)


def widen_kernel(
    gd, gu, gh, dx, vec, gd_o, gu_o, gq_o, gk_o, gv_o, go_o, dx_o, b_q, b_v, b_up, *rows
):
    gd_o[...] = gd[...].astype(F32)
    gu_o[...] = gu[...].astype(F32)
    dx_o[...] = dx[...].astype(F32)
    for c, out in enumerate((gq_o, gk_o, gv_o, go_o)):
        out[...] = gh[c].astype(F32)

    @pl.when(pl.program_id(0) == 0)
    def vectors():
        tp = lax.axis_index("tp")
        heads_w = b_q.shape[0]
        slot = (heads_w + 127) // 128 * 128
        b_up[...] = vec[pl.ds(8 + tp, 1), :][0]
        b_q[...] = vec[pl.ds(12 + tp, 1), 0:heads_w][0]
        b_v[...] = vec[pl.ds(12 + tp, 1), slot : slot + heads_w][0]
        for i, out in enumerate(rows):
            out[...] = vec[2 + i : 3 + i, :][0]


def widen(gd, gu, gh, dx, vec):
    width, tokens, heads_w = gd.shape[0], dx.shape[0], gh.shape[1]
    steps = 8
    row_steps = heads_w // 48
    rows = pl.BlockSpec((width // steps, width), lambda i: (i, 0))
    out = pl.BlockSpec((48, width), lambda i: (jnp.minimum(i, row_steps - 1), 0))
    tokens_spec = pl.BlockSpec((tokens // steps, width), lambda i: (i, 0))
    return pl.pallas_call(
        widen_kernel,
        grid=(steps,),
        out_shape=(
            jax.ShapeDtypeStruct((width, width), F32),
            jax.ShapeDtypeStruct((width, width), F32),
            jax.ShapeDtypeStruct((heads_w, width), F32),
            jax.ShapeDtypeStruct((heads_w, width), F32),
            jax.ShapeDtypeStruct((heads_w, width), F32),
            jax.ShapeDtypeStruct((heads_w, width), F32),
            jax.ShapeDtypeStruct((tokens, width), F32),
            jax.ShapeDtypeStruct((heads_w,), F32),
            jax.ShapeDtypeStruct((heads_w,), F32),
        )
        + (jax.ShapeDtypeStruct((width,), F32),) * 7,
        in_specs=[
            rows,
            rows,
            pl.BlockSpec((4, 48, width), lambda i: (0, jnp.minimum(i, row_steps - 1), 0)),
            tokens_spec,
            pl.BlockSpec((16, width), lambda i: (0, 0)),
        ],
        out_specs=(rows, rows, out, out, out, out, tokens_spec)
        + (pl.BlockSpec((heads_w,), lambda i: (0,)),) * 2
        + (pl.BlockSpec((width,), lambda i: (0,)),) * 7,
    )(gd, gu, gh, dx, vec)


def body(
    mesh_sizes,
    inputs,
    token_ids,
    crop_counts,
    domain_ids,
    positives,
    distractor_buffer,
    w_query,
    b_query,
    w_key,
    w_value,
    b_value,
    w_out,
    b_out,
    gain_one,
    shift_one,
    w_up,
    b_up,
    w_down,
    b_down,
    gain_two,
    shift_two,
):
    gd, gu, gh, dx, vec = run_layer(
        mesh_sizes,
        (
            token_ids,
            domain_ids,
            crop_counts,
            positives,
            b_query,
            b_value,
            b_up,
            b_out,
            gain_one,
            shift_one,
            b_down,
            gain_two,
            shift_two,
            inputs,
            w_query.T,
            w_key.T,
            w_value.T,
            w_out,
            w_up,
            w_down,
            distractor_buffer,
        ),
    )
    (
        grad_w_down,
        grad_w_up,
        grad_w_query,
        grad_w_key,
        grad_w_value,
        grad_w_out,
        grad_inputs,
        grad_b_query,
        grad_b_value,
        grad_b_up,
        grad_b_out,
        grad_b_down,
        grad_gain_one,
        grad_shift_one,
        grad_gain_two,
        grad_shift_two,
    ) = widen(gd, gu, gh, dx, vec)
    return (
        grad_inputs,
        grad_w_query.T,
        grad_b_query,
        grad_w_key.T,
        grad_w_value.T,
        grad_b_value,
        grad_w_out,
        grad_b_out,
        grad_gain_one,
        grad_shift_one,
        grad_w_up,
        grad_b_up,
        grad_w_down,
        grad_b_down,
        grad_gain_two,
        grad_shift_two,
    )


def solution(mesh):
    mesh_sizes = (mesh.shape["tp"], mesh.shape["dp"], mesh.shape["dq"])
    rows = P(("dp", "dq"), None)
    groups = P(("dp", "dq"))
    return jax.shard_map(
        functools.partial(body, mesh_sizes),
        mesh=mesh,
        in_specs=(
            rows,
            rows,
            groups,
            groups,
            rows,
            rows,
            P(None, "tp"),
            P("tp"),
            P(None, "tp"),
            P(None, "tp"),
            P("tp"),
            P("tp", None),
            P(),
            P(),
            P(),
            P(None, "tp"),
            P("tp"),
            P("tp", None),
            P(),
            P(),
            P(),
        ),
        out_specs=(
            rows,
            P(None, "tp"),
            P("tp"),
            P(None, "tp"),
            P(None, "tp"),
            P("tp"),
            P("tp", None),
            P(),
            P(),
            P(),
            P(None, "tp"),
            P("tp"),
            P("tp", None),
            P(),
            P(),
            P(),
        ),
        check_vma=False,
    )
```

```python
import functools
from typing import NamedTuple

import jax
import jax.numpy as jnp
from jax import lax
from jax.experimental import pallas as pl
from jax.experimental.pallas import tpu as pltpu
from jax.sharding import PartitionSpec as P

HD = 64
LN_EPS = 1e-12
INV_TEMP = 1.0 / 0.05
LOSS_SCALE = 128.0
MASKED = -1000000000.0
BF = jnp.bfloat16
F32 = jnp.float32
MESH = pl.DeviceIdType.MESH


FORWARD_ORDER = (
    "SOd", "SOk", "PTp", "FAd", "SOv", "SOq", "Zb", "FAk", "FAv", "FAq", "SOo", "ATp", "FBk",
    "FBq", "Za", "FBv", "PTb", "FAo", "Lk", "PTa", "Lv", "SOu", "ATb", "Lq", "ATa", "FBo",
    "PTd", "Lo", "ATd", "Zd", "OUT", "FAu", "Up", "FBu", "ZSb", "ZSa", "Ub", "Ua", "Dp", "Lu",
    "Db", "Da", "ZSd", "Ud", "Dd",
)
BACKWARD_ORDER = (
    "HBb", "DPd0", "DPd1", "HBp", "HBa", "DPb1", "DPa0", "DPb0", "P1_D0", "HBd", "HG", "P1_D1",
    "UPd1", "DPa1", "L1B", "DPp0", "P2_D0", "DPp1", "UPa1", "UPb0", "Z0_D0",
    "UPb1", "ABd", "P1_U1", "P2_D1", "UPd0", "Z1_D0", "ABp", "UPp1", "UPa0", "P2_U1",
    "Z0_D1", "HQd", "P1_U0", "A1_D0", "OPd", "ABa", "Z0_U1", "OPp", "UPp0", "HVd",
    "Z1_D1", "ABb", "P2_U0", "HQp", "OPb", "HQa", "OPa", "A0_D0", "Z1_U1", "HQb", "A1_D1",
    "P1_H0", "HVb", "P1_H1", "IG", "Z0_U0", "HVp", "VS", "P2_H0", "HVa", "F_D0", "Z1_U0",
    "P2_H1", "DX", "Z0_H0", "A1_U0", "Z0_H1", "Z1_H0", "A1_U1", "Z1_H1", "V1", "A1_H0", "A0_U1",
    "DXF", "A1_H1", "A0_U0", "F_U1", "V2", "A0_D1", "A0_H0", "F_U0", "A0_H1", "DXL", "F_H0",
    "F_D1", "F_H1", "V3",
)


def dot_nn(left, right):
    return lax.dot_general(left, right, (((1,), (0,)), ((), ())), preferred_element_type=F32)


def dot_nt(left, right):
    return lax.dot_general(left, right, (((1,), (1,)), ((), ())), preferred_element_type=F32)


def dot_tn(left, right):
    return lax.dot_general(left, right, (((0,), (0,)), ((), ())), preferred_element_type=F32)


def loop(count, step):
    def run(i, carry):
        step(i)
        return carry

    lax.fori_loop(0, count, run, 0)


def each(count, step):
    def run(i, carry):
        step(i)
        return carry

    lax.fori_loop(0, count, run, 0)


def at(index, size):
    return pl.ds(pl.multiple_of(index * size, size), size)


def remote(src, dst, send_sem, recv_sem, device):
    return pltpu.make_async_remote_copy(
        src_ref=src,
        dst_ref=dst,
        send_sem=send_sem,
        recv_sem=recv_sem,
        device_id=device,
        device_id_type=MESH,
    )


def flip(index, bit):
    return index + bit - 2 * bit * lax.rem(index // bit, 2)


def halvings_of(width, dp_n):
    count, rows = 0, width // 4
    while 2 << count <= dp_n and rows // 2 % 16 == 0:
        count, rows = count + 1, rows // 2
    return count


class Refs(NamedTuple):
    ids: object
    dom: object
    cnt: object
    pos_in: object
    b_q: object
    b_v: object
    b_up: object
    b_out: object
    gain1: object
    shift1: object
    b_down: object
    gain2: object
    shift2: object
    x_in: object
    wq_in: object
    wk_in: object
    wv_in: object
    wo_in: object
    wu_in: object
    wd_in: object
    queue_in: object
    gd_out: object
    gu_out: object
    gh_out: object
    dx_out: object
    vec_out: object
    wqkv: object
    wo: object
    wu: object
    wd: object
    xb: object
    qkv: object
    prob: object
    ctx: object
    xh1: object
    rstd1: object
    h1b: object
    act: object
    gp: object
    r2: object
    rstd2: object
    x_s: object
    ctx_s: object
    h1_s: object
    act_s: object
    df_s: object
    du_s: object
    do_s: object
    dqkv_s: object
    df: object
    du: object
    do: object
    g0: object
    r_one: object
    r_two: object
    z_one: object
    z_hi: object
    res: object
    bb: object
    emsg: object
    es: object
    neg: object
    shares: object
    pm_out: object
    pm_in: object
    xs: object
    posf: object
    pulled: object
    vec: object
    v_plane: object
    v_z: object
    v_hi: object
    loc: object
    w_ss: object
    w_rs: object
    s_ss: object
    s_rs: object
    zd_ss: object
    zd_rs: object
    b_ss: object
    b_rs: object
    a_ss: object
    a_rs: object
    e_ss: object
    e_rs: object
    p_ss: object
    p_rs: object
    g1_ss: object
    g1_rs: object
    g2_ss: object
    g2_rs: object
    gz_ss: object
    gz_rs: object
    ga_ss: object
    ga_rs: object
    gh_ss: object
    gh_rs: object
    gf_ss: object
    gf_rs: object
    x_ss: object
    x_rs: object
    v_ss: object
    v_rs: object
    out_sem: object


def layer_kernel(sizes, *refs):
    tp_n, dp_n, dq_n, crops_dev, seq, width = sizes
    k = Refs(*refs)
    tokens = crops_dev * seq
    groups = dp_n * dq_n
    dp_bits = dp_n.bit_length() - 1
    hi_bits = (dq_n // 2).bit_length() - 1
    heads_w = width // tp_n
    heads_t = heads_w // HD
    slot = (heads_w + 127) // 128 * 128
    half = width // 2
    head_half = heads_w // 2
    quarter = half // dp_n
    lane_blocks = width // 256
    halvings = halvings_of(width, dp_n)

    tp, dp, dq = lax.axis_index("tp"), lax.axis_index("dp"), lax.axis_index("dq")
    core = lax.rem(dq, 2)
    t_x = tp + 1 - 2 * lax.rem(tp, 2)
    t_y = lax.rem(tp + 2, 4)
    t_d = 3 - tp
    t_a = t_x + core * (t_y - t_x)
    t_b = t_x + t_y - t_a
    me = dp * dq_n + dq
    dev_a = (t_a, dp, dq)
    dev_b = (t_b, dp, dq)
    dev_s = (tp, dp, dq + 1 - 2 * core)
    others = (t_a, t_b, t_d)

    def group_dev(g):
        return (tp, g // dq_n, lax.rem(g, dq_n))

    own_half = at(core, half)
    other_half = at(1 - core, half)

    barrier = pltpu.get_barrier_semaphore()
    for t_peer in (t_x, t_y, t_d):
        pl.semaphore_signal(barrier, inc=1, device_id=(t_peer, dp, dq), device_id_type=MESH)

    def greet(i):
        pl.semaphore_signal(
            barrier, inc=1, device_id=group_dev(lax.rem(me + i + 1, groups)), device_id_type=MESH
        )

    each(groups - 1, greet)

    def t_rows(t):
        return at(t, heads_w)

    locals_ = [(k.x_in.at[at(tp, tokens)], k.xb)]
    heads_in = (k.wq_in, k.wk_in, k.wv_in)
    locals_ += [(heads_in[c], k.wqkv.at[c, t_rows(tp)]) for c in range(3)]
    locals_ += [(k.wo_in, k.wo.at[t_rows(tp)]), (k.wu_in, k.wu.at[tp]), (k.wd_in, k.wd.at[tp])]
    locals_ += [(k.queue_in.at[pl.ds(j * tokens, tokens)], k.du.at[j]) for j in range(tp_n)]
    local = [pltpu.make_async_copy(src, dst, k.loc.at[i]) for i, (src, dst) in enumerate(locals_)]
    for copy in local:
        copy.start()
    k.bb[tp] = jnp.zeros((8, width), F32)
    k.bb[tp, 0:1, :] = k.b_up[...][None, :]
    k.bb[tp, 1:2, 0:heads_w] = k.b_q[...][None, :]
    k.bb[tp, 2:3, 0:heads_w] = k.b_v[...][None, :]
    k.es[...] = jnp.zeros_like(k.es)
    k.pulled[...] = jnp.zeros_like(k.pulled)
    k.xs[...] = jnp.zeros_like(k.xs)
    k.vec[...] = jnp.zeros_like(k.vec)
    pl.semaphore_wait(barrier, 3 + groups - 1)

    shard = {"a": t_a, "b": t_b, "d": t_d, "p": tp}

    def part(c, t, h):
        if c < 3:
            return k.wqkv.at[c, pl.ds(pl.multiple_of(t * heads_w + h * head_half, 32), head_half)]
        if c == 3:
            return k.wo.at[pl.ds(pl.multiple_of(t * heads_w + h * head_half, 32), head_half)]
        if c == 4:
            return k.wu.at[t, at(h, half)]
        return k.wd.at[t, pl.ds(pl.multiple_of(h * half + dp * quarter, 16), quarter)]

    def source(c):
        if c < 3:
            return heads_in[c].at[at(core, head_half)]
        if c == 3:
            return k.wo_in.at[at(core, head_half)]
        if c == 4:
            return k.wu_in.at[at(core, half)]
        return k.wd_in.at[pl.ds(pl.multiple_of(core * half + dp * quarter, 16), quarter)]

    def w_copy(c, i):
        if i < 2:
            return remote(
                source(c), part(c, tp, core), k.w_ss.at[c, i], k.w_rs.at[c, i], (dev_a, dev_b)[i]
            )
        there = part(c, t_a, core)
        return remote(there, there, k.w_ss.at[c, 2], k.w_rs.at[c, 2], dev_b)

    def w_arrived(c, i):
        there = part(c, others[i], core)
        remote(there, there, k.w_ss.at[c, i], k.w_rs.at[c, i], dev_a).wait_recv()

    def s_part(c, t, h):
        return k.wd.at[t, at(h, half)] if c == 5 else part(c, t, h)

    def s_copy(c, i):
        there = s_part(c, others[i], core)
        return remote(there, there, k.s_ss.at[c, i], k.s_rs.at[c, i], dev_s)

    def s_arrived(c, t, i):
        there = s_part(c, t, 1 - core)
        remote(there, there, k.s_ss.at[c, i], k.s_rs.at[c, i], dev_s).wait_recv()

    def handed_on(c, name):
        if name != "p":
            i = "bad".index(name)
            s_arrived(c, shard[name], i)

    def zd_copy(i, j):
        there = part(5, others[i], core)
        return remote(
            there,
            there,
            k.zd_ss.at[i],
            k.zd_rs.at[i],
            (tp, lax.rem(dp + 1 + j, dp_n), dq),
        )

    def send_own(c):
        w_copy(c, 0).start()
        w_copy(c, 1).start()

    def last_on(c):
        w_arrived(c, 2)
        s_copy(c, 2).start()

    def first_on(c):
        w_arrived(c, 0)
        w_copy(c, 2).start()
        if c < 5:
            s_copy(c, 0).start()

    def second_on(c):
        w_arrived(c, 1)
        s_copy(c, 1).start()

    def send_planes(i):
        if i > 0:
            w_arrived(5, i)
        for j in range(dp_n - 1):
            zd_copy(i, j).start()

    def planes_on(i):
        there = k.wd.at[others[i], 0 : (dp_n - 1) * quarter]
        remote(there, there, k.zd_ss.at[i], k.zd_rs.at[i], dev_s).wait_recv()
        s_copy(5, i).start()

    def bias_copy(i):
        mine = k.bb.at[tp]
        return remote(mine, mine, k.b_ss.at[i], k.b_rs.at[i], ((t_x, t_y, t_d)[i], dp, dq))

    def bias_arrived(i):
        there = k.bb.at[(t_x, t_y, t_d)[i]]
        remote(there, there, k.b_ss.at[i], k.b_rs.at[i], dev_s).wait_recv()

    first_head = lax.broadcasted_iota(jnp.int32, (seq, 2 * HD), 1) < HD

    def project(t):
        for c in range(3):
            out = dot_nt(k.xb[...], k.wqkv[c, t_rows(t), :])
            if c != 1:
                row = 1 if c == 0 else 2
                out = out + k.bb[t, row : row + 1, 0:heads_w]
            out = out.astype(BF)
            k.qkv[c, t] = out * BF(0.125) if c == 0 else out

    def head_views(block):
        views = []
        for h in range(heads_t):
            base = h // 2 * 2 * HD
            if h == heads_t - 1 and heads_t % 2:
                views.append((slice(base, base + HD), None))
            else:
                views.append((slice(base, base + 2 * HD), h % 2))
        return views

    views = head_views(heads_w)

    def masked(value, side):
        if side is None:
            return value
        keep = first_head if side == 0 else ~first_head
        return jnp.where(keep, value, jnp.zeros_like(value))

    def merged(outs, store):
        for h, (lanes, side) in enumerate(views):
            if side is None:
                store(lanes, outs[h])
            elif side == 1:
                store(lanes, jnp.where(first_head, outs[h - 1], outs[h]))

    def attend(t, crop):
        rows = at(crop, seq)
        ids = jnp.broadcast_to(k.ids[pl.ds(crops_dev * tp + crop, 1), :], (seq, seq))
        outs = []
        for h, (lanes, side) in enumerate(views):
            s = dot_nt(masked(k.qkv[0, t, rows, lanes], side), k.qkv[1, t, rows, lanes])
            s = jnp.where(ids != 0, s, MASKED)
            e = jnp.exp(s - jnp.max(s, axis=-1, keepdims=True))
            p = (e * (1.0 / jnp.sum(e, axis=-1, keepdims=True))).astype(BF)
            k.prob[(crop * tp_n + t) * heads_t + h] = p
            outs.append(dot_nn(p, k.qkv[2, t, rows, lanes]))

        def store(lanes, value):
            k.ctx[t, rows, lanes] = value.astype(BF)

        merged(outs, store)

    seen = set()

    def once(tag, wait):
        if tag not in seen:
            seen.add(tag)
            wait()

    def biases():
        for i in range(3):
            bias_arrived(i)

    def project_step(name):
        if name != "p":
            once("bias", biases)
        else:
            for i in range(3):
                bias_copy(i).start()
            for copy in local[0:4]:
                copy.wait()
            a_copies[0].start()
        for c in range(3):
            handed_on(c, name)
        project(shard[name])

    def attend_step(name):
        each(crops_dev, lambda crop: attend(shard[name], crop))

    def attn_out(i):
        rows = at(i, 256)
        total = k.xb[rows, :].astype(F32) + k.b_out[...][None, :]
        for t in range(tp_n):
            total = total + dot_nn(k.ctx[t, rows, :], k.wo[t * heads_w : (t + 1) * heads_w, :])
        k.r2[rows, :] = total

    def norm(v):
        centered = v - jnp.mean(v, axis=-1, keepdims=True)
        rstd = lax.rsqrt(jnp.mean(centered * centered, axis=-1, keepdims=True) + LN_EPS)
        return centered * rstd, rstd

    gain_one = k.gain1[...][None, :]
    shift_one = k.shift1[...][None, :]
    b_down = k.b_down[...][None, :]

    def norm_one(i):
        rows = at(i, 256)
        xh, rstd = norm(k.r2[rows, :])
        k.xh1[rows, :] = xh
        k.rstd1[rows, :] = rstd
        h1 = xh * gain_one + shift_one
        k.h1b[rows, :] = h1.astype(BF)
        k.r2[rows, :] = h1 + b_down

    def out_step():
        a_copies[1].start()
        local[4].wait()
        for name in "abd":
            handed_on(3, name)
        for i in range(tokens // 256):
            attn_out(i)
            norm_one(i)
        a_copies[2].start()

    def act_copy(i):
        t = (tp, t_a, t_b, t_d)[i]
        return remote(
            k.act.at[t, :, other_half], k.act_s.at[t], k.a_ss.at[3 + i], k.a_rs.at[3 + t], dev_s
        )

    def up(t):
        def tile(i):
            cols = at(i, 256)
            u = dot_nn(k.h1b[...], k.wu[t, :, cols]) + k.bb[t, 0:1, cols]
            cdf = 0.5 * lax.erf(u * 0.7071067811865476) + 0.5
            k.act[t, :, cols] = (u * cdf).astype(BF)
            k.gp[t, :, cols] = (cdf + u * (jnp.exp(u * u * -0.5) * 0.3989422804014327)).astype(BF)

        for i in range(lane_blocks):
            tile(i)

    def down(t):
        k.r2[...] += dot_nn(k.act[t], k.wd[t])

    def up_step(name):
        if name == "p":
            local[5].wait()
        handed_on(4, name)
        up(shard[name])
        act_copy("pabd".index(name)).start()

    def down_step(name):
        if name == "p":
            local[6].wait()
        handed_on(5, name)
        down(shard[name])

    a_copies = [
        remote(k.xb.at[:, other_half], k.x_s, k.a_ss.at[0], k.a_rs.at[0], dev_s),
        remote(k.ctx, k.ctx_s, k.a_ss.at[1], k.a_rs.at[1], dev_s),
        remote(k.h1b, k.h1_s, k.a_ss.at[2], k.a_rs.at[2], dev_s),
    ]
    chunk = "qkvoud"
    forward = {"OUT": out_step}
    for name in "pabd":
        forward["PT" + name] = functools.partial(project_step, name)
        forward["AT" + name] = functools.partial(attend_step, name)
        forward["U" + name] = functools.partial(up_step, name)
        forward["D" + name] = functools.partial(down_step, name)
    for i, name in enumerate("abd"):
        forward["Z" + name] = functools.partial(send_planes, i)
        forward["ZS" + name] = functools.partial(planes_on, i)
    for c, name in enumerate(chunk):
        forward["SO" + name] = functools.partial(send_own, c)
        forward["FA" + name] = functools.partial(first_on, c)
        forward["FB" + name] = functools.partial(second_on, c)
        forward["L" + name] = functools.partial(last_on, c)
    for step in FORWARD_ORDER:
        forward[step]()

    sub256 = lax.broadcasted_iota(jnp.int32, (256, 1), 0).astype(F32)
    zero_row = jnp.zeros((1, width), F32)

    def crop_ids(c):
        return k.ids[pl.ds(crops_dev * tp + c, 1), :]

    lens = [
        jnp.sum(jnp.where(crop_ids(c) != 0, 1.0, 0.0), axis=-1, keepdims=True)
        for c in range(crops_dev)
    ]
    for c in range(crops_dev):

        def norm_two(i, total, c=c):
            rows = pl.ds(pl.multiple_of(c * seq + i * 256, 256), 256)
            xh, rstd = norm(k.r2[rows, :])
            k.r2[rows, :] = xh
            k.rstd2[rows, :] = rstd
            live = sub256 + (i * 256).astype(F32) < lens[c]
            return total + jnp.sum(jnp.where(live, xh, 0.0), axis=0, keepdims=True)

        k.xs[c : c + 1, :] = lax.fori_loop(0, seq // 256, norm_two, zero_row)

    row8 = lax.broadcasted_iota(jnp.int32, (8, 1), 0)

    def per_crop(values, other=0.0):
        out = jnp.full((8, 1), other, F32)
        for c in range(crops_dev):
            out = jnp.where(row8 == c, values[c], out)
        return out

    crop_len = per_crop(lens, 1.0)
    gain_two, shift_two = k.gain2[...][None, :], k.shift2[...][None, :]
    xs = k.xs[...]
    is_crop = row8 < crops_dev
    pooled = jnp.where(is_crop, xs / crop_len * gain_two + shift_two, 0.0)
    inv_norm = lax.rsqrt(jnp.sum(pooled * pooled, axis=-1, keepdims=True) + 1e-06)
    e_own = (pooled * inv_norm).astype(BF).astype(F32)
    live_n = k.cnt[0]
    crops_group = crops_dev * tp_n
    dom_total = [jnp.float32(0.0), jnp.float32(0.0)]
    for c in range(crops_group):
        is_live = jnp.where(c < live_n, 1.0, 0.0)
        is_one = k.dom[c].astype(F32)
        dom_total[0] = dom_total[0] + is_live * (1.0 - is_one)
        dom_total[1] = dom_total[1] + is_live * is_one
    lane_row = lax.broadcasted_iota(jnp.int32, (1, 256), 1)
    meta_row = crops_dev * lane_blocks

    def crop_block(c, j):
        return slice(c * lane_blocks + j, c * lane_blocks + j + 1)

    def lanes_of(j):
        return slice(j * 256, (j + 1) * 256)

    for c in range(crops_dev):
        for j in range(lane_blocks):
            k.emsg[me, crop_block(c, j), :] = e_own[c : c + 1, lanes_of(j)]
    k.emsg[me, meta_row : meta_row + 1, :] = jnp.where(
        lane_row == 0, dom_total[0], jnp.where(lane_row == 1, dom_total[1], 0.0)
    )

    def e_copy(i):
        mine = k.emsg.at[me]
        return remote(
            mine, mine, k.e_ss.at[0], k.e_rs.at[0], group_dev(lax.rem(me + 1 + i, groups))
        )

    e_all = remote(
        k.emsg.at[0 : groups - 1], k.emsg.at[0 : groups - 1], k.e_ss.at[0], k.e_rs.at[0], dev_s
    )

    each(groups - 1, lambda i: e_copy(i).start())
    k.posf[...] = k.pos_in[...].astype(F32)
    positives = jnp.concatenate(
        [k.posf[pl.ds(crops_dev * tp + c, 1), :] for c in range(crops_dev)]
        + [jnp.zeros((8 - crops_dev, width), F32)],
        axis=0,
    )
    pos = jnp.sum(e_own * positives, axis=-1, keepdims=True) * INV_TEMP
    for copy in local[7:]:
        copy.wait()
    e_all.wait_recv()

    n_block = 8
    lane_msg = lax.broadcasted_iota(jnp.int32, (n_block, 1, 256), 2)

    def queue_block(b):
        span = pl.ds(b * n_block, n_block)
        for c in range(crops_dev):
            for j in range(lane_blocks):
                k.es[:, c : c + 1, lanes_of(j)] = k.emsg[span, crop_block(c, j), :]
        es = k.es[...].reshape(8 * n_block, width).astype(BF)
        for j in range(tp_n):
            k.neg[:, j * tokens : (j + 1) * tokens] = dot_nt(es, k.du[j]) * INV_TEMP
        neg = k.neg[...]
        top = jnp.max(neg, axis=-1, keepdims=True)
        share = jnp.exp(neg - top)
        total = jnp.sum(share, axis=-1, keepdims=True)
        high = share.astype(BF)
        k.shares[0 : 8 * n_block, :] = high
        k.shares[8 * n_block :, :] = (share - high.astype(F32)).astype(BF)
        for j in range(lane_blocks):
            both = dot_nn(k.shares[:, 0:tokens], k.du[0, :, lanes_of(j)])
            for i in range(1, tp_n):
                both = both + dot_nn(
                    k.shares[:, i * tokens : (i + 1) * tokens], k.du[i, :, lanes_of(j)]
                )
            pull = (both[0 : 8 * n_block] + both[8 * n_block :]).reshape(n_block, 8, 256)
            for c in range(crops_dev):
                k.pm_out[span, crop_block(c, j), :] = pull[:, c : c + 1, :]
        top = top.reshape(n_block, 8, 1)
        total = total.reshape(n_block, 8, 1)
        stats = jnp.zeros((n_block, 1, 256), F32)
        for c in range(crops_dev):
            stats = jnp.where(lane_msg == 2 * c, top[:, c : c + 1, :], stats)
            stats = jnp.where(lane_msg == 2 * c + 1, total[:, c : c + 1, :], stats)
        k.pm_out[span, meta_row : meta_row + 1, :] = stats

    loop(groups // n_block, queue_block)

    def p_copy(i):
        g = lax.rem(me + 1 + i, groups)
        return remote(k.pm_out.at[g], k.pm_in.at[me], k.p_ss.at[0], k.p_rs.at[0], group_dev(g))

    p_all = remote(
        k.pm_out.at[0 : groups - 1], k.pm_in.at[0 : groups - 1], k.p_ss.at[0], k.p_rs.at[0], dev_s
    )

    each(groups - 1, lambda i: p_copy(i).start())
    k.pm_in[me] = k.pm_out[me]
    dom_lanes = jnp.sum(k.emsg[:, meta_row : meta_row + 1, :], axis=0)
    weights = []
    for c in range(crops_dev):
        at_c = crops_dev * tp + c
        is_one = k.dom[at_c].astype(F32)
        own_total = dom_lanes[:, 0:1] * (1.0 - is_one) + dom_lanes[:, 1:2] * is_one
        is_live = jnp.where(at_c < live_n, 1.0, 0.0)
        weights.append(
            is_live * (LOSS_SCALE * crops_group * groups) / (2.0 * jnp.maximum(own_total, 1.0))
        )
    crop_weight = per_crop(weights)
    p_all.wait_recv()

    tops_all, totals_all = [], []
    for c in range(crops_dev):
        tops = k.pm_in[:, meta_row : meta_row + 1, 2 * c : 2 * c + 1]
        totals = k.pm_in[:, meta_row : meta_row + 1, 2 * c + 1 : 2 * c + 2]
        top_c = jnp.max(tops, axis=0, keepdims=True)
        scale = jnp.exp(tops - top_c)
        tops_all.append(top_c[0])
        totals_all.append(jnp.sum(scale * totals, axis=0))
        for j in range(lane_blocks):
            k.pulled[c : c + 1, lanes_of(j)] = jnp.sum(
                scale * k.pm_in[:, crop_block(c, j), :], axis=0
            )
    total_all = per_crop(totals_all, 1.0)
    lse_q = per_crop(tops_all) + jnp.log(total_all)
    top_both = jnp.maximum(pos, lse_q)
    lse = top_both + jnp.log(jnp.exp(pos - top_both) + jnp.exp(lse_q - top_both))
    de = crop_weight * (
        (jnp.exp(lse_q - lse) / total_all * INV_TEMP) * k.pulled[...]
        + ((jnp.exp(pos - lse) - 1.0) * INV_TEMP) * positives
    )
    dpool = inv_norm * (
        de - pooled * (jnp.sum(pooled * de, axis=-1, keepdims=True) * inv_norm * inv_norm)
    )
    dpool = jnp.where(is_crop, dpool / crop_len, 0.0)
    k.vec[6:7, :] = jnp.sum(dpool * xs, axis=0, keepdims=True)
    k.vec[7:8, :] = jnp.sum(dpool * crop_len, axis=0, keepdims=True)

    dgain = dpool * gain_two
    dgain_mean = jnp.mean(dgain, axis=-1, keepdims=True)
    b_down_sum = zero_row
    for c in range(crops_dev):
        dg, dg_mean = dgain[c : c + 1, :], dgain_mean[c : c + 1, :]

        def norm_two_back(i, total, c=c, dg=dg, dg_mean=dg_mean):
            rows = pl.ds(pl.multiple_of(c * seq + i * 256, 256), 256)
            xh = k.r2[rows, :]
            live = sub256 + (i * 256).astype(F32) < lens[c]
            scale = jnp.where(live, k.rstd2[rows, :], 0.0)
            dr = scale * (dg - dg_mean - xh * jnp.mean(dg * xh, axis=-1, keepdims=True))
            k.r2[rows, :] = dr
            k.df[rows, :] = dr.astype(BF)
            return total + jnp.sum(dr, axis=0, keepdims=True)

        b_down_sum = lax.fori_loop(0, seq // 256, norm_two_back, b_down_sum)
    k.vec[3:4, :] = b_down_sum
    df_copy = remote(k.df, k.df_s, k.a_ss.at[7], k.a_rs.at[7], dev_s)
    df_copy.start()

    for c in range(6):
        for i in range(3):
            w_copy(c, i).wait_send()
            s_copy(c, i).wait_send()
    for i in range(3):
        there = k.wd.at[others[i], 0 : (dp_n - 1) * quarter]
        remote(there, there, k.zd_ss.at[i], k.zd_rs.at[i], dev_s).wait_send()
        bias_copy(i).wait_send()
    for i in range(4):
        act_copy(i).wait_send()
    for copy in a_copies:
        copy.wait_send()
    e_all.wait_send()
    p_all.wait_send()

    units = 6
    unit = half // 2
    store_in = (k.g0, k.act, k.gp)

    def g_ref(n, t):
        return store_in[n // 2].at[t, pl.ds(n % 2 * unit, unit)]

    def g1_copy(n, i):
        t_from = (t_a, t_d)[i]
        return remote(
            g_ref(n, t_from), k.r_one.at[n, i], k.g1_ss.at[n, i], k.g1_rs.at[n, i], dev_a
        )

    def g2_copy(n):
        return remote(g_ref(n, t_b), k.r_two.at[n], k.g2_ss.at[n], k.g2_rs.at[n], dev_b)

    def z_side(bit):
        return lax.rem(dp // (1 << bit), 2)

    def z_span(bits):
        start, size = 0, unit
        for bit in range(bits):
            size //= 2
            start = start + z_side(bit) * size
        return start, size

    def z_dev(bit):
        return (tp, flip(dp, 1 << bit), dq)

    whole = [z_dev(bit) for bit in range(halvings, dp_bits)]
    whole += [(tp, dp, flip(dq, 2 << bit)) for bit in range(hi_bits)]

    def z_rows(start, size):
        return pl.ds(pl.multiple_of(start, 16), size)

    def gz_copy(n, bit):
        start, size = z_span(bit)
        size //= 2
        away = start + (1 - z_side(bit)) * size
        return remote(
            g_ref(n, tp).at[z_rows(away, size)],
            k.z_one.at[n, pl.ds(unit - 2 * size, size)],
            k.gz_ss.at[n, bit],
            k.gz_rs.at[n, bit],
            z_dev(bit),
        )

    def gh_copy(n, i):
        rows = z_rows(*z_span(halvings))
        return remote(
            g_ref(n, tp).at[rows], k.z_hi.at[n, i], k.gh_ss.at[n, i], k.gh_rs.at[n, i], whole[i]
        )

    def ga_copy(n, bit):
        rows = k.res.at[n, z_rows(*z_span(bit + 1))]
        return remote(rows, rows, k.ga_ss.at[n, bit], k.ga_rs.at[n, bit], z_dev(bit))

    def ga_wait(n, bit):
        start, size = z_span(bit)
        away = start + (1 - z_side(bit)) * (size // 2)
        rows = k.res.at[n, z_rows(away, size // 2)]
        remote(rows, rows, k.ga_ss.at[n, bit], k.ga_rs.at[n, bit], dev_s).wait_recv()

    def final_parts(n, of_core):
        kind, s = n // 2, n % 2
        parts = []
        for h in range(2):
            src = k.res.at[n, :, h * half : (h + 1) * half]
            if kind == 0:
                rows = pl.ds(pl.multiple_of(of_core * half + h * unit, unit), unit)
                dst = k.gd_out.at[rows, s * half : (s + 1) * half]
            elif kind == 1:
                first = s * half + h * unit
                dst = k.gu_out.at[first : first + unit, at(of_core, half)]
            else:
                dst = k.gh_out.at[2 * s + h, :, at(of_core, half)]
            parts.append((src, dst))
        return parts

    def final_copies(n):
        away, here = [], []
        for src, dst in final_parts(n, core):
            away.append(remote(src, dst, k.gf_ss.at[n], k.gf_rs.at[n], dev_s))
            here.append(pltpu.make_async_copy(src, dst, k.out_sem.at[n]))
        return away, here

    def final_both(n):
        return remote(k.res.at[n], k.res.at[n], k.gf_ss.at[n], k.gf_rs.at[n], dev_s)

    def final_arrived(n):
        final_both(n).wait_recv()

    def add_rows(dst, srcs):
        def step(i):
            rows = at(i, 192)
            total = dst[rows, :].astype(F32)
            for src in srcs:
                total = total + src[rows, :].astype(F32)
            dst[rows, :] = total.astype(BF)

        loop(unit // 192, step)

    def plane_first(n):
        g1_copy(n, 1).wait_recv()
        add_rows(g_ref(n, t_b), [k.r_one.at[n, 1]])
        g2_copy(n).start()

    def plane_second(n):
        g1_copy(n, 0).wait_recv()
        g2_copy(n).wait_recv()
        add_rows(g_ref(n, tp), [k.r_one.at[n, 0], k.r_two.at[n]])
        gz_copy(n, 0).start()

    def z_add(n, bit):
        gz_copy(n, bit).wait()
        start, size = z_span(bit + 1)
        mine = g_ref(n, tp).at[z_rows(start, size)]
        total = mine[...].astype(F32) + k.z_one[n, pl.ds(unit - 2 * size, size)].astype(F32)
        if bit + 1 < halvings:
            mine[...] = total.astype(BF)
            gz_copy(n, bit + 1).start()
            return
        for i in range(len(whole)):
            mine[...] = total.astype(BF)
            gh_copy(n, i).start()
            gh_copy(n, i).wait()
            total = mine[...].astype(F32) + k.z_hi[n, i].astype(F32)
        k.res[n, z_rows(start, size)] = total.astype(BF)
        ga_copy(n, halvings - 1).start()

    def z_back(n, bit):
        ga_wait(n, bit)
        if bit > 0:
            ga_copy(n, bit - 1).start()
            return
        for copies in final_copies(n):
            for copy in copies:
                copy.start()

    place = "dabp"

    def du_copy(name):
        t = shard[name]
        i = 8 + place.index(name)
        return remote(k.du.at[t, :, other_half], k.du_s.at[t], k.a_ss.at[i], k.a_rs.at[8 + t], dev_s)

    def hidden_back(name):
        t = shard[name]

        def tile(j):
            cols = at(j, 256)
            da = dot_nt(k.df[...], k.wd[t, cols, :])
            d = (da * k.gp[t, :, cols].astype(F32)).astype(BF)
            k.du[t, :, cols] = d
            k.vec[pl.ds(8 + t, 1), cols] = jnp.sum(d.astype(F32), axis=0, keepdims=True)

        for i in range(lane_blocks):
            tile(i)
        du_copy(name).start()

    def arrived(ref, index):
        remote(ref, ref, k.a_ss.at[0], k.a_rs.at[index], dev_s).wait_recv()

    def put(n, t, g):
        ref = g_ref(n, t)
        ref[:, 0:half] = g[0:unit].astype(BF)
        ref[:, half:width] = g[unit:half].astype(BF)

    def send_piece(n, name):
        if name in "ad":
            g1_copy(n, "ad".index(name)).start()

    def down_piece(name, s):
        t = shard[name]
        once("df", df_copy.wait_recv)
        once("act" + name, lambda: arrived(k.act_s.at[t], 3 + t))
        cols = slice(s * half, (s + 1) * half)
        put(
            s,
            t,
            dot_tn(k.act[t, :, own_half], k.df[:, cols]) + dot_tn(k.act_s[t], k.df_s[:, cols]),
        )
        send_piece(s, name)

    def up_piece(name, s):
        t = shard[name]
        once("h1", a_copies[2].wait_recv)
        once("du" + name, lambda: arrived(k.du_s.at[t], 8 + t))
        rows = slice(s * half, (s + 1) * half)
        put(
            2 + s,
            t,
            dot_tn(k.h1b[:, rows], k.du[t, :, own_half]) + dot_tn(k.h1_s[:, rows], k.du_s[t]),
        )
        send_piece(2 + s, name)

    def hidden_grad():
        def tile(i):
            cols = at(i, 256)
            total = k.r2[:, cols]
            for t in range(tp_n):
                total = total + dot_nt(k.du[t], k.wu[t, cols, :])
            k.r2[:, cols] = total

        for i in range(lane_blocks):
            tile(i)

    do_copy = remote(k.do.at[:, other_half], k.do_s, k.a_ss.at[12], k.a_rs.at[12], dev_s)

    def norm_one_back():
        def rows_back(i, sums):
            rows = at(i, 256)
            dh, xh = k.r2[rows, :], k.xh1[rows, :]
            dxh = dh * gain_one
            dr = k.rstd1[rows, :] * (
                dxh
                - jnp.mean(dxh, axis=-1, keepdims=True)
                - xh * jnp.mean(dxh * xh, axis=-1, keepdims=True)
            )
            k.r2[rows, :] = dr
            k.do[rows, :] = dr.astype(BF)
            return (
                sums[0] + jnp.sum(dr, axis=0, keepdims=True),
                sums[1] + jnp.sum(dh * xh, axis=0, keepdims=True),
                sums[2] + jnp.sum(dh, axis=0, keepdims=True),
            )

        out_sum, gain_sum, shift_sum = lax.fori_loop(
            0, tokens // 256, rows_back, (zero_row, zero_row, zero_row)
        )
        k.vec[2:3, :] = out_sum
        k.vec[4:5, :] = gain_sum
        k.vec[5:6, :] = shift_sum
        do_copy.start()

    def grad_lanes(c, lanes):
        return slice(c * slot + lanes.start, c * slot + lanes.stop)

    def dqkv_copy(name):
        t = shard[name]
        i = 13 + place.index(name)
        return remote(k.wd.at[t, 0:tokens], k.dqkv_s.at[t], k.a_ss.at[i], k.a_rs.at[13 + t], dev_s)

    def attention_back(name):
        t = shard[name]
        each(crops_dev, lambda crop: attend_back(t, crop))
        dqkv_copy(name).start()

    def attend_back(t, crop):
        rows = at(crop, seq)
        dctx_all = dot_nt(k.do[rows, :], k.wo[t_rows(t), :]).astype(BF)
        dqs, dks, dvs = [], [], []
        for h, (lanes, side) in enumerate(views):
            q, key, val = (k.qkv[c, t, rows, lanes] for c in range(3))
            dctx = dctx_all[:, lanes]
            p = k.prob[(crop * tp_n + t) * heads_t + h]
            pf = p.astype(F32)
            dprob = dot_nt(masked(dctx, side), val)
            ds = (pf * (dprob - jnp.sum(dprob * pf, axis=-1, keepdims=True))).astype(BF)
            dvs.append(dot_tn(p, dctx))
            dqs.append(dot_nn(ds, key) * 0.125)
            dks.append(dot_tn(ds, q))
        for c, outs in enumerate((dqs, dks, dvs)):

            def store(lanes, value, c=c):
                k.wd[t, rows, grad_lanes(c, lanes)] = value.astype(BF)

            merged(outs, store)

    heads_lanes = slice(0, heads_w)

    def head_grad(t, c):
        cols = grad_lanes(c, heads_lanes)
        g = dot_tn(k.wd[t, 0:tokens, cols], k.xb[:, own_half])
        return (g + dot_tn(k.dqkv_s[t, :, cols], k.x_s[...])).astype(BF)

    def out_piece(name):
        t = shard[name]
        once("do", do_copy.wait_recv)
        once("ctx", a_copies[1].wait_recv)
        g = dot_tn(k.ctx[t], k.do[:, own_half]) + dot_tn(k.ctx_s[t], k.do_s[...])
        g_ref(5, t)[:, half:width] = g.astype(BF)

    def query_key_piece(name):
        t = shard[name]
        once("x", a_copies[0].wait_recv)
        once("dqkv" + name, lambda: arrived(k.dqkv_s.at[t], 13 + t))
        g_ref(4, t)[:, 0:half] = head_grad(t, 0)
        g_ref(4, t)[:, half:width] = head_grad(t, 1)
        send_piece(4, name)

    def value_piece(name):
        t = shard[name]
        once("x", a_copies[0].wait_recv)
        once("dqkv" + name, lambda: arrived(k.dqkv_s.at[t], 13 + t))
        g_ref(5, t)[:, 0:half] = head_grad(t, 2)
        send_piece(5, name)

    def input_grad():
        do_copy.wait_send()

        def tile(i):
            cols = at(i, 256)
            total = k.r2[:, cols]
            for t in range(tp_n):
                for c in range(3):
                    total = total + dot_nn(
                        k.wd[t, 0:tokens, grad_lanes(c, heads_lanes)],
                        k.wqkv[c, t * heads_w : (t + 1) * heads_w, cols],
                    )
            k.do[:, cols] = total.astype(BF)

        for i in range(lane_blocks):
            tile(i)

    def dx_rows(t):
        return k.dx_out.at[at(t, tokens)]

    dx_local = pltpu.make_async_copy(k.do, dx_rows(tp), k.out_sem.at[units])

    def dx_copy(i):
        if i < 2:
            return remote(k.do, dx_rows(tp), k.x_ss.at[i], k.x_rs.at[i], (dev_a, dev_b)[i])
        return remote(dx_rows(t_a), dx_rows(t_a), k.x_ss.at[2], k.x_rs.at[2], dev_b)

    def dx_arrived(i):
        there = dx_rows(others[i])
        remote(there, there, k.x_ss.at[i], k.x_rs.at[i], dev_a).wait_recv()

    def dx_send():
        dx_copy(0).start()
        dx_copy(1).start()
        dx_local.start()

    def dx_pass():
        dx_arrived(0)
        dx_copy(2).start()

    def dx_last():
        dx_arrived(1)
        dx_arrived(2)

    def v_sibling():
        return remote(k.vec, k.v_hi.at[0], k.v_ss.at[0], k.v_rs.at[0], dev_s)

    def v_plane(i):
        mine = k.v_plane.at[tp]
        return remote(
            mine, mine, k.v_ss.at[1 + i], k.v_rs.at[1 + i], ((t_x, t_y, t_d)[i], dp, dq)
        )

    def v_plane_arrived(i):
        there = k.v_plane.at[(t_x, t_y, t_d)[i]]
        remote(there, there, k.v_ss.at[1 + i], k.v_rs.at[1 + i], dev_s).wait_recv()

    def v_planes(j):
        mine = k.v_z.at[dp]
        return remote(
            mine, mine, k.v_ss.at[4 + j], k.v_rs.at[4 + dp], (tp, lax.rem(dp + 1 + j, dp_n), dq)
        )

    def v_planes_arrived(j):
        z = lax.rem(dp + 1 + j, dp_n)
        there = k.v_z.at[z]
        remote(there, there, k.v_ss.at[4 + j], k.v_rs.at[4 + z], dev_s).wait_recv()

    def v_group(bit):
        i = 4 + dp_n + bit
        return remote(
            k.v_hi.at[1 + 2 * bit],
            k.v_hi.at[2 + 2 * bit],
            k.v_ss.at[i],
            k.v_rs.at[i],
            (tp, dp, flip(dq, 2 << bit)),
        )

    def vector_send():
        for t in range(tp_n):
            for c, lanes in ((0, slice(0, heads_w)), (2, slice(slot, slot + heads_w))):
                grads = k.wd[t, 0:tokens, grad_lanes(c, heads_lanes)].astype(F32)
                k.vec[12 + t : 13 + t, lanes] = jnp.sum(grads, axis=0, keepdims=True)
        v_sibling().start()

    def vector_plane():
        v_sibling().wait()
        k.v_plane[tp] = k.vec[...] + k.v_hi[0]
        for i in range(3):
            v_plane(i).start()

    def vector_planes():
        for i in range(3):
            v_plane_arrived(i)
        total = k.v_plane[0]
        for t in range(1, tp_n):
            total = total + k.v_plane[t]
        k.v_z[dp] = total
        for j in range(dp_n - 1):
            v_planes(j).start()

    def vector_last():
        for j in range(dp_n - 1):
            v_planes_arrived(j)
        total = k.v_z[0]
        for z in range(1, dp_n):
            total = total + k.v_z[z]
        for bit in range(hi_bits):
            k.v_hi[1 + 2 * bit] = total
            v_group(bit).start()
            v_group(bit).wait_recv()
            total = total + k.v_hi[2 + 2 * bit]
        k.vec_out[...] = total

    steps = {
        "HG": hidden_grad,
        "L1B": norm_one_back,
        "IG": input_grad,
        "DX": dx_send,
        "DXF": dx_pass,
        "DXL": dx_last,
        "VS": vector_send,
        "V1": vector_plane,
        "V2": vector_planes,
        "V3": vector_last,
    }
    for name in place:
        steps["HB" + name] = functools.partial(hidden_back, name)
        steps["OP" + name] = functools.partial(out_piece, name)
        steps["HQ" + name] = functools.partial(query_key_piece, name)
        steps["HV" + name] = functools.partial(value_piece, name)
        for s in range(2):
            steps["DP" + name + str(s)] = functools.partial(down_piece, name, s)
            steps["UP" + name + str(s)] = functools.partial(up_piece, name, s)
        steps["AB" + name] = functools.partial(attention_back, name)
    for n in range(units):
        tag = "_" + "DUH"[n // 2] + str(n % 2)
        steps["P1" + tag] = functools.partial(plane_first, n)
        steps["P2" + tag] = functools.partial(plane_second, n)
        for bit in range(halvings):
            steps["Z" + str(bit) + tag] = functools.partial(z_add, n, bit)
            steps["A" + str(halvings - 1 - bit) + tag] = functools.partial(z_back, n, halvings - 1 - bit)
        steps["F" + tag] = functools.partial(final_arrived, n)
    for step in BACKWARD_ORDER:
        steps.pop(step)()
    for step in steps.values():
        step()

    df_copy.wait_send()
    dx_local.wait()
    for i in range(3):
        dx_copy(i).wait_send()
        v_plane(i).wait_send()
    for j in range(dp_n - 1):
        v_planes(j).wait_send()
    for bit in range(hi_bits):
        v_group(bit).wait_send()
    for name in place:
        du_copy(name).wait_send()
        dqkv_copy(name).wait_send()
    for n in range(units):
        final_both(n).wait_send()
        pltpu.make_async_copy(k.res.at[n], k.res.at[n], k.out_sem.at[n]).wait()
        for i in range(2):
            g1_copy(n, i).wait_send()
        g2_copy(n).wait_send()
        for bit in range(halvings):
            ga_copy(n, bit).wait_send()


def run_layer(mesh_sizes, args):
    tp_n, dp_n, dq_n = mesh_sizes
    ids, x_in = args[0], args[13]
    width = x_in.shape[1]
    crops_dev = ids.shape[0] // tp_n
    tokens = x_in.shape[0] // tp_n
    seq = tokens // crops_dev
    groups = dp_n * dq_n
    half = width // 2
    heads_w = width // tp_n
    dp_bits = dp_n.bit_length() - 1
    hi_bits = (dq_n // 2).bit_length() - 1
    heads = width // HD
    unit = half // 2
    halvings = halvings_of(width, dp_n)
    any_whole = dp_bits - halvings + hi_bits > 0
    n_whole = max(dp_bits - halvings + hi_bits, 1)
    smem = pl.BlockSpec(memory_space=pltpu.SMEM)
    vmem = pl.BlockSpec(memory_space=pltpu.VMEM)
    hbm = pl.BlockSpec(memory_space=pl.ANY)
    dma = pltpu.SemaphoreType.DMA

    def b16(*shape):
        return pltpu.VMEM(shape, BF)

    def f32(*shape):
        return pltpu.VMEM(shape, F32)

    scratch = [
        b16(3, width, width),
        b16(width, width),
        b16(tp_n, width, width),
        b16(tp_n, width, width),
        b16(tokens, width),
        b16(3, tp_n, tokens, heads_w),
        b16(crops_dev * heads, seq, seq),
        b16(tp_n, tokens, heads_w),
        f32(tokens, width),
        f32(tokens, 1),
        b16(tokens, width),
        b16(tp_n, tokens, width),
        b16(tp_n, tokens, width),
        f32(tokens, width),
        f32(tokens, 1),
        b16(tokens, half),
        b16(tp_n, tokens, heads_w),
        b16(tokens, width),
        b16(tp_n, tokens, half),
        b16(tokens, width),
        b16(tp_n, tokens, half),
        b16(tokens, half),
        b16(tp_n, tokens, width),
        b16(tokens, width),
        b16(tp_n, tokens, width),
        b16(tokens, width),
        b16(tp_n, half, width),
        b16(6, 2, unit, width),
        b16(6, unit, width),
        b16(6, unit - (unit >> halvings), width),
        b16(6 if any_whole else 1, n_whole, unit >> halvings, width),
        b16(6, unit, width),
        f32(tp_n, 8, width),
        f32(groups, 8, 256),
        f32(8, 8, width),
        f32(64, tp_n * tokens),
        b16(128, tp_n * tokens),
        f32(groups, 8, 256),
        f32(groups, 8, 256),
        f32(8, width),
        f32(ids.shape[0], width),
        f32(8, width),
        f32(16, width),
        f32(tp_n, 16, width),
        f32(dp_n, 16, width),
        f32(1 + 2 * hi_bits, 16, width),
        dma((7 + tp_n,)),
        dma((6, 3)),
        dma((6, 3)),
        dma((6, 3)),
        dma((6, 3)),
        dma((3,)),
        dma((3,)),
        dma((3,)),
        dma((3,)),
        dma((17,)),
        dma((17,)),
        dma((1,)),
        dma((1,)),
        dma((1,)),
        dma((1,)),
        dma((6, 2)),
        dma((6, 2)),
        dma((6,)),
        dma((6,)),
        dma((6, halvings)),
        dma((6, halvings)),
        dma((6, halvings)),
        dma((6, halvings)),
        dma((6 if any_whole else 1, n_whole)),
        dma((6 if any_whole else 1, n_whole)),
        dma((6,)),
        dma((6,)),
        dma((3,)),
        dma((3,)),
        dma((4 + dp_n + hi_bits,)),
        dma((4 + dp_n + hi_bits,)),
        dma((7,)),
    ]
    return pl.pallas_call(
        functools.partial(layer_kernel, (tp_n, dp_n, dq_n, crops_dev, seq, width)),
        out_shape=(
            jax.ShapeDtypeStruct((width, width), BF),
            jax.ShapeDtypeStruct((width, width), BF),
            jax.ShapeDtypeStruct((4, heads_w, width), BF),
            jax.ShapeDtypeStruct((tp_n * tokens, width), BF),
            jax.ShapeDtypeStruct((16, width), F32),
        ),
        in_specs=[vmem, smem, smem] + [vmem] * 10 + [hbm] * 8,
        out_specs=(hbm, hbm, hbm, hbm, vmem),
        scratch_shapes=scratch,
        compiler_params=pltpu.CompilerParams(
            collective_id=0, has_side_effects=True, vmem_limit_bytes=63 * 2**20
        ),
    )(*args)


def widen_kernel(parts, gd, gu, gh, dx, vec, *refs):
    outs, refs = refs[:7], refs[7:]
    b_q, b_v, b_up, *rows = refs[:9]
    narrow, wide, in_sem, out_sem = refs[9:]
    gd_o, gu_o, gq_o, gk_o, gv_o, go_o, dx_o = outs
    work = []
    first = 0
    for src, dst in ((dx, dx_o), (gd, gd_o), (gu, gu_o)):
        size = src.shape[0] // parts
        for p in range(parts):
            span = pl.ds(p * size, size)
            work.append((src.at[span], dst.at[span], first, size))
            first += size
    for c, dst in enumerate((gq_o, gk_o, gv_o, go_o)):
        size = gh.shape[1]
        work.append((gh.at[c], dst, first, size))
        first += size
    reads, writes = [], []
    for i, (src, dst, start, size) in enumerate(work):
        span = pl.ds(start, size)
        reads.append(pltpu.make_async_copy(src, narrow.at[span], in_sem.at[i]))
        writes.append(pltpu.make_async_copy(wide.at[span], dst, out_sem.at[i]))
    for read in reads:
        read.start()
    tp = lax.axis_index("tp")
    heads_w = b_q.shape[0]
    slot = (heads_w + 127) // 128 * 128
    b_up[...] = vec[pl.ds(8 + tp, 1), :][0]
    b_q[...] = vec[pl.ds(12 + tp, 1), 0:heads_w][0]
    b_v[...] = vec[pl.ds(12 + tp, 1), slot : slot + heads_w][0]
    for i, out in enumerate(rows):
        out[...] = vec[2 + i : 3 + i, :][0]
    for read, write, (_, _, start, size) in zip(reads, writes, work):
        read.wait()

        def step(i, start=start):
            span = pl.ds(pl.multiple_of(start + i * 64, 64), 64)
            wide[span, :] = narrow[span, :].astype(F32)

        loop(size // 64, step)
        write.start()
    for write in writes:
        write.wait()


def widen(gd, gu, gh, dx, vec):
    width, tokens, heads_w = gd.shape[0], dx.shape[0], gh.shape[1]
    parts = 4
    total = tokens + 2 * width + 4 * heads_w
    hbm = pl.BlockSpec(memory_space=pl.ANY)
    vmem = pl.BlockSpec(memory_space=pltpu.VMEM)
    copies = 3 * parts + 4
    return pl.pallas_call(
        functools.partial(widen_kernel, parts),
        out_shape=(
            (jax.ShapeDtypeStruct((width, width), F32),) * 2
            + (jax.ShapeDtypeStruct((heads_w, width), F32),) * 4
            + (jax.ShapeDtypeStruct((tokens, width), F32),)
            + (jax.ShapeDtypeStruct((heads_w,), F32),) * 2
            + (jax.ShapeDtypeStruct((width,), F32),) * 7
        ),
        in_specs=[hbm] * 4 + [vmem],
        out_specs=(hbm,) * 7 + (vmem,) * 9,
        scratch_shapes=[
            pltpu.VMEM((total, width), BF),
            pltpu.VMEM((total, width), F32),
            pltpu.SemaphoreType.DMA((copies,)),
            pltpu.SemaphoreType.DMA((copies,)),
        ],
        compiler_params=pltpu.CompilerParams(vmem_limit_bytes=63 * 2**20),
    )(gd, gu, gh, dx, vec)


def body(
    mesh_sizes,
    inputs,
    token_ids,
    crop_counts,
    domain_ids,
    positives,
    distractor_buffer,
    w_query,
    b_query,
    w_key,
    w_value,
    b_value,
    w_out,
    b_out,
    gain_one,
    shift_one,
    w_up,
    b_up,
    w_down,
    b_down,
    gain_two,
    shift_two,
):
    gd, gu, gh, dx, vec = run_layer(
        mesh_sizes,
        (
            token_ids,
            domain_ids,
            crop_counts,
            positives,
            b_query,
            b_value,
            b_up,
            b_out,
            gain_one,
            shift_one,
            b_down,
            gain_two,
            shift_two,
            inputs,
            w_query.T,
            w_key.T,
            w_value.T,
            w_out,
            w_up,
            w_down,
            distractor_buffer,
        ),
    )
    (
        grad_w_down,
        grad_w_up,
        grad_w_query,
        grad_w_key,
        grad_w_value,
        grad_w_out,
        grad_inputs,
        grad_b_query,
        grad_b_value,
        grad_b_up,
        grad_b_out,
        grad_b_down,
        grad_gain_one,
        grad_shift_one,
        grad_gain_two,
        grad_shift_two,
    ) = widen(gd, gu, gh, dx, vec)
    return (
        grad_inputs,
        grad_w_query.T,
        grad_b_query,
        grad_w_key.T,
        grad_w_value.T,
        grad_b_value,
        grad_w_out,
        grad_b_out,
        grad_gain_one,
        grad_shift_one,
        grad_w_up,
        grad_b_up,
        grad_w_down,
        grad_b_down,
        grad_gain_two,
        grad_shift_two,
    )


def solution(mesh):
    mesh_sizes = (mesh.shape["tp"], mesh.shape["dp"], mesh.shape["dq"])
    rows = P(("dp", "dq"), None)
    groups = P(("dp", "dq"))
    return jax.shard_map(
        functools.partial(body, mesh_sizes),
        mesh=mesh,
        in_specs=(
            rows,
            rows,
            groups,
            groups,
            rows,
            rows,
            P(None, "tp"),
            P("tp"),
            P(None, "tp"),
            P(None, "tp"),
            P("tp"),
            P("tp", None),
            P(),
            P(),
            P(),
            P(None, "tp"),
            P("tp"),
            P("tp", None),
            P(),
            P(),
            P(),
        ),
        out_specs=(
            rows,
            P(None, "tp"),
            P("tp"),
            P(None, "tp"),
            P(None, "tp"),
            P("tp"),
            P("tp", None),
            P(),
            P(),
            P(),
            P(None, "tp"),
            P("tp"),
            P("tp", None),
            P(),
            P(),
            P(),
        ),
        check_vma=False,
    )
```
